32 devices in a mesh: dp: 8 (over y, x, core), seq: 4 (over z).
Axes of the slice: x: 2, y: 2, z: 4, core: 2. Of those that a mesh axis runs over, the one named last changes fastest.
Arguments:
- tokens: bfloat16 [16, 640, 512], P('dp', 'seq'), may hold values from -6 to 6
- cotangent: bfloat16 [16, 640, 512], P('dp', 'seq'), may hold values from -6 to 6
- routes: int32 [2, 16, 640, 2], P(None, 'dp', 'seq'), may hold values from 0 to 3, all different within a row
- token_mask: int32 [16, 640], P('dp'), may hold values from 0 to 1, as said below
- ln1_gain: bfloat16 [2, 512], P(None, 'dp'), may hold values from 0.5 to 1.5
- ln1_bias: bfloat16 [2, 512], P(None, 'dp'), may hold values from -1.1953125 to 1.1953125
- qkv_weight: bfloat16 [2, 512, 1536], P(None, 'dp'), may hold values from -0.375 to 0.375
- out_weight: bfloat16 [2, 512, 512], P(None, 'dp'), may hold values from -1 to 1
- ln2_gain: bfloat16 [2, 512], P(None, 'dp'), may hold values from 0.5 to 1.5
- ln2_bias: bfloat16 [2, 512], P(None, 'dp'), may hold values from -1.1953125 to 1.1953125
- router_weight: bfloat16 [2, 512, 4], P(None, 'dp'), may hold values from -0.1875 to 0.1875
- expert_in: bfloat16 [2, 4, 512, 2048], P(None, None, 'dp'), may hold values from -0.25 to 0.25
- expert_out: bfloat16 [2, 4, 2048, 512], P(None, None, 'dp'), may hold values from -0.5 to 0.5
Outputs:
- output: bfloat16 [16, 640, 512], P('dp', 'seq')
- token_grad: float32 [16, 640, 512], P('dp', 'seq')
- ln1_gain_grad: float32 [2, 512], P(None, 'dp')
- ln1_bias_grad: float32 [2, 512], P(None, 'dp')
- qkv_weight_grad: float32 [2, 512, 1536], P(None, 'dp')
- out_weight_grad: float32 [2, 512, 512], P(None, 'dp')
- ln2_gain_grad: float32 [2, 512], P(None, 'dp')
- ln2_bias_grad: float32 [2, 512], P(None, 'dp')
- router_weight_grad: float32 [2, 512, 4], P(None, 'dp')
- expert_in_grad: float32 [2, 4, 512, 2048], P(None, None, 'dp')
- expert_out_grad: float32 [2, 4, 2048, 512], P(None, None, 'dp')
The draws below stay inside these ranges and needn't reach their ends.
Inputs may be any that keep to these rules, and one draw needn't show every extreme that they name: `token_mask`: in each image the valid tokens (1) come first and the pads (0) after them; each image has 481 to 640 valid tokens. `routes`: the two experts of a token differ.
All inputs are finite; a program needn't handle non-finite values.
Results may differ from the reference program's by a relative error of at most 0.028.
Values may be sent and summed in bfloat16 or wider, within the bound.
A program may use at most 320 MiB of HBM per device.

```python
import math
import jax
import jax.numpy as jnp
from jax import lax

D = 512
HEADS = 8
HEAD = 64
HID = 2048
EXPERTS = 4
LAYERS = 2
SEQ_LEN = 640
IMAGES = 16
MIN_VALID = 481


def draw_token_mask(key, part):
    lengths = jax.random.randint(key, (IMAGES, 1), MIN_VALID, SEQ_LEN + 1)
    places = jnp.arange(SEQ_LEN, dtype=jnp.int32)[None, :]
    return (places < lengths).astype(jnp.int32)


def raised(drawn, rng, source, target, shards_of, factor):
    def block_of(position):
        return (jnp.arange(drawn.shape[position]) // (drawn.shape[position] // shards_of)).reshape((-1,) + (1,) * (drawn.ndim - 1 - position))

    first = jax.random.permutation(rng, shards_of)[block_of(target)]
    second = (block_of(target) + shards_of // 2) % shards_of
    return jnp.where((block_of(source) == first) | (block_of(source) == second), factor * drawn, drawn)


def shard_levels(rng, extent, pieces, least, high):
    factor_of = 1.0
    for dim, shards_of in pieces:
        draws = jax.random.uniform(jax.random.fold_in(jax.random.fold_in(rng, 6), dim), (shards_of,), jnp.float32, least / len(pieces), high / len(pieces))
        factor_of = factor_of * jnp.repeat(jnp.exp(draws), extent[dim] // shards_of).reshape((-1,) + (1,) * (len(extent) - 1 - dim))
    return factor_of


def different_ones(own_key, rows, count, top, lift):
    sequence = jax.random.permutation(jax.random.fold_in(own_key, 1), count)
    pull = sequence
    for power in range(3):
        pull = pull * pull // count
    pull = pull * lift // count
    lots = jax.random.randint(jax.random.fold_in(own_key, 2), (rows, count), 0, 4096) + pull
    holders = jax.random.permutation(jax.random.fold_in(own_key, 3), rows)[jnp.arange(count) % rows]
    lots = jnp.where(jnp.arange(rows)[:, None] == holders[None, :], 1 << 14, lots)
    priority = lots * count + jnp.arange(count)
    return lax.top_k(priority.astype(jnp.int32), top)[1].astype(jnp.int32)


def centred(own_key, dims, width, reach, pieces=(), kind=jnp.bfloat16):
    factor_of = shard_levels(own_key, dims, pieces, -0.22, 0.18) if pieces else 1.0
    drawn = jax.random.normal(own_key, dims, jnp.float32) * width * factor_of
    return jnp.minimum(jnp.maximum(drawn, -reach), reach).astype(kind)


def gaussian_with(key, extent, scale, most, cuts, heavy, kind=jnp.bfloat16):
    array = scale * jax.random.normal(key, extent, jnp.float32)
    if cuts:
        array = array * shard_levels(key, extent, cuts, -0.22, 0.18)
    return jnp.clip(raised(array, jax.random.fold_in(key, 3), *heavy), -most, most).astype(kind)


def setup_inputs(seed: int = 0) -> dict:
    key_of = jax.random.split(jax.random.key(seed), 14)
    return {
        "tokens": gaussian_with(key_of[0], (IMAGES, SEQ_LEN, D), 1.0, 6.0, ((0, 8), (1, 4)), (0, 2, 8, 2.0)),
        "cotangent": centred(key_of[1], (IMAGES, SEQ_LEN, D), 1.0, 6.0, ((0, 8), (1, 4))),
        "routes": different_ones(key_of[2], LAYERS * IMAGES * SEQ_LEN, EXPERTS, 2, 4096).reshape((LAYERS, IMAGES, SEQ_LEN, 2)),
        "token_mask": draw_token_mask(jax.random.fold_in(key_of[13], 71), 0),
        "ln1_gain": jnp.clip(1.0 + 0.1 * jax.random.normal(key_of[4], (LAYERS, D), jnp.float32), 0.5, 1.5).astype(jnp.bfloat16),
        "ln1_bias": centred(key_of[5], (LAYERS, D), 0.2, 1.1953125, ((1, 8),)),
        "qkv_weight": centred(key_of[6], (LAYERS, D, 3 * D), (D // 2) ** -0.5, 0.375, ((1, 8),)),
        "out_weight": centred(key_of[7], (LAYERS, D, D), (D // 16) ** -0.5, 1.0, ((1, 8),)),
        "ln2_gain": jnp.clip(1.0 + 0.1 * jax.random.normal(key_of[8], (LAYERS, D), jnp.float32), 0.5, 1.5).astype(jnp.bfloat16),
        "ln2_bias": centred(key_of[9], (LAYERS, D), 0.2, 1.1953125, ((1, 8),)),
        "router_weight": centred(key_of[10], (LAYERS, D, EXPERTS), (2 * D) ** -0.5, 0.1875, ((1, 8),)),
        "expert_in": centred(key_of[11], (LAYERS, EXPERTS, D, HID), D ** -0.5, 0.25, ((2, 8),)),
        "expert_out": centred(key_of[12], (LAYERS, EXPERTS, HID, D), (HID // 16) ** -0.5, 0.5, ((2, 8),)),
    }


EPS = 1e-06
NEG = -1e+30
HIGH = lax.Precision.HIGHEST

@jax.custom_vjp
def low(v):
    return lax.optimization_barrier(v.astype(jnp.bfloat16)).astype(jnp.float32)

@jax.custom_vjp
def low_back(v):
    return v

def low_keep(v):
    return (low(v), None)

def low_pass(kept, grad):
    return (grad,)

def back_keep(v):
    return (v, None)

def back_low(kept, grad):
    return (low(grad),)
low.defvjp(low_keep, low_pass)
low_back.defvjp(back_keep, back_low)

def product(form, left, right):
    return jnp.einsum(form, left, right, precision=HIGH)

def normalize(values):
    center = values - lax.optimization_barrier(jnp.mean(values, -1, keepdims=True))
    spread = lax.optimization_barrier(jnp.mean(center * center, -1, keepdims=True))
    return center * lax.rsqrt(spread + EPS)

def softmax_last(values):
    shifted = values - lax.optimization_barrier(jnp.max(values, -1, keepdims=True))
    expo = jnp.exp(shifted)
    return expo / lax.optimization_barrier(jnp.sum(expo, -1, keepdims=True))

def two_layers(params, images, route_ids, valid):
    gain_one, bias_one, proj_packed, proj_out, gain_two, bias_two, router, up_all, down_all = params
    group = images.shape[0]
    state = images
    for level in range(LAYERS):
        normed = low(normalize(state) * gain_one[level] + bias_one[level])
        packed = low(low_back(product('gld,de->gle', normed, proj_packed[level])))
        queries = packed[..., :D].reshape(group, SEQ_LEN, HEADS, HEAD)
        keys_all = packed[..., D:2 * D].reshape(group, SEQ_LEN, HEADS, HEAD)
        values_all = packed[..., 2 * D:].reshape(group, SEQ_LEN, HEADS, HEAD)
        scores = low_back(product('gqhd,gkhd->ghqk', queries, keys_all) * HEAD ** (-0.5))
        scores = jnp.where(valid[:, None, None, :] > 0, scores, NEG)
        weights = low(softmax_last(scores))
        mixed = product('ghqk,gkhd->gqhd', weights, values_all).reshape(group, SEQ_LEN, D)
        mixed = low(low_back(mixed))
        middle = state + low_back(product('gld,de->gle', mixed, proj_out[level]))
        normed_two = low(normalize(middle) * gain_two[level] + bias_two[level])
        gates = softmax_last(product('gld,de->gle', normed_two, router[level]))
        matches = route_ids[level][..., None] == jnp.arange(EXPERTS, dtype=jnp.int32)
        chosen = lax.optimization_barrier(jnp.sum(matches.astype(jnp.float32), -2))
        combine = gates * chosen
        update = jnp.zeros_like(middle)
        for expert in range(EXPERTS):
            hidden_pre = low_back(product('gld,dh->glh', normed_two, up_all[level, expert]))
            hidden_act = low(jax.nn.gelu(hidden_pre, approximate=False))
            result = low_back(product('glh,hd->gld', hidden_act, down_all[level, expert]))
            update = update + combine[..., expert:expert + 1] * result
        state = middle + update
    return state

def reference(tokens, cotangent, routes, token_mask, ln1_gain, ln1_bias, qkv_weight, out_weight, ln2_gain, ln2_bias, router_weight, expert_in, expert_out):
    params = tuple((item.astype(jnp.float32) for item in (ln1_gain, ln1_bias, qkv_weight, out_weight, ln2_gain, ln2_bias, router_weight, expert_in, expert_out)))
    group = math.gcd(IMAGES, 4)
    count = IMAGES // group
    grouped_routes = jnp.transpose(routes.reshape(LAYERS, count, group, SEQ_LEN, 2), (1, 0, 2, 3, 4))
    grouped_mask = token_mask.reshape(count, group, SEQ_LEN)

    def forward(weights, inputs):
        grouped = inputs.reshape(count, group, SEQ_LEN, D)
        runner = jax.checkpoint(lambda item: two_layers(weights, item[0], item[1], item[2]))
        return lax.map(runner, (grouped, grouped_routes, grouped_mask)).reshape(IMAGES, SEQ_LEN, D)
    output, pullback = jax.vjp(forward, params, tokens.astype(jnp.float32))
    start_grad = cotangent.astype(jnp.float32) * token_mask[..., None].astype(jnp.float32)
    grads, token_grad = pullback(start_grad)
    return (output.astype(jnp.bfloat16), token_grad, grads[0], grads[1], grads[2], grads[3], grads[4], grads[5], grads[6], grads[7], grads[8])
```

```python
import jax
import jax.numpy as jnp
from jax import lax
from jax.sharding import PartitionSpec as P

HEAD = 64
EPS = 1e-06
NEG = -1e30
META = 16
F32 = jnp.float32
BF16 = jnp.bfloat16


def normalize(values):
    center = values - jnp.mean(values, -1, keepdims=True)
    inverse = lax.rsqrt(jnp.mean(center * center, -1, keepdims=True) + EPS)
    return center * inverse, inverse


def norm_back(grad_unit, unit, inverse):
    return inverse * (
        grad_unit
        - jnp.mean(grad_unit, -1, keepdims=True)
        - unit * jnp.mean(grad_unit * unit, -1, keepdims=True)
    )


def heads_of(values):
    return values.reshape(values.shape[0], values.shape[1] // HEAD, HEAD)


def mm(form, left, right):
    return jnp.einsum(form, left, right, preferred_element_type=F32)


def gelu_and_slope(values):
    cdf = 0.5 * (1.0 + lax.erf(values * 0.7071067811865476))
    pdf = jnp.exp(-0.5 * values * values) * 0.3989422804014327
    return values * cdf, cdf + values * pdf


class Plan:
    def __init__(self, mesh, images, length):
        self.dp = mesh.shape["dp"]
        self.seq = mesh.shape["seq"]
        self.images = images
        self.piece = length // self.seq
        self.share = self.seq // images
        self.rows = images * self.piece
        self.groups = [
            [block * self.share + part for part in range(self.share)]
            for block in range(self.dp // self.share)
        ]

    def hops(self, turn):
        pairs = []
        for dp in range(self.dp):
            for seq in range(self.seq):
                local = (seq % self.images + turn) % self.images
                to_dp = dp // self.share * self.share + seq // self.images
                to_seq = dp % self.share * self.images + local
                pairs.append((dp * self.seq + seq, to_dp * self.seq + to_seq))
        return pairs

    def to_images(self, pieces):
        seq = lax.axis_index("seq") % self.images
        got = []
        for turn in range(self.images):
            piece = lax.dynamic_index_in_dim(pieces, (seq + turn) % self.images, 0, False)
            got.append(lax.ppermute(piece, ("dp", "seq"), self.hops(turn)))
        got = jnp.stack(got)
        return jnp.stack(
            [
                lax.dynamic_index_in_dim(got, (seq - slot) % self.images, 0, False)
                for slot in range(self.images)
            ]
        )

    def to_pieces(self, slots):
        seq = lax.axis_index("seq") % self.images
        got = []
        for turn in range(self.images):
            slot = lax.dynamic_index_in_dim(slots, (seq - turn) % self.images, 0, False)
            back = [(to, source) for source, to in self.hops(turn)]
            got.append(lax.ppermute(slot, ("dp", "seq"), back))
        got = jnp.stack(got)
        return jnp.stack(
            [
                lax.dynamic_index_in_dim(got, (local - seq) % self.images, 0, False)
                for local in range(self.images)
            ]
        )


def attention_scores(queries, keys_all, length):
    scores = mm("qhd,khd->hqk", heads_of(queries), heads_of(keys_all)) * HEAD ** (-0.5)
    valid = jnp.arange(keys_all.shape[0]) < length
    return jnp.where(valid[None, None, :], scores, NEG)


def build(mesh):
    def shards(
        tokens,
        cotangent,
        routes,
        token_mask,
        ln1_gain,
        ln1_bias,
        qkv_weight,
        out_weight,
        ln2_gain,
        ln2_bias,
        router_weight,
        expert_in,
        expert_out,
    ):
        images, piece, width = tokens.shape
        levels, experts = expert_in.shape[:2]
        length_all = token_mask.shape[1]
        plan = Plan(mesh, images, length_all)
        rows = plan.rows
        slice_hid = expert_out.shape[2]
        wide = experts * slice_hid
        part = lax.axis_index("dp") % plan.share

        start = lax.axis_index("seq") * piece
        local_valid = lax.dynamic_slice_in_dim(token_mask, start, piece, 1)
        chosen_all = jnp.sum(
            (routes[..., None] == jnp.arange(experts, dtype=jnp.int32)).astype(F32), -2
        )
        chosen_rows = jnp.transpose(chosen_all, (1, 0, 3, 2)).reshape(images, levels * experts, piece)
        lengths = jnp.sum(token_mask, -1)
        meta = jnp.zeros((images, META, width), F32)
        meta = meta.at[:, : levels * experts, :piece].set(chosen_rows)
        meta = meta.at[:, levels * experts, 0].set((lengths // 4).astype(F32))
        meta = meta.at[:, levels * experts + 1, 0].set((lengths % 4).astype(F32))
        masked = cotangent * local_valid[..., None].astype(BF16)
        slots = plan.to_images(jnp.concatenate([tokens, meta.astype(BF16), masked], 1))
        state = slots[:, :piece].reshape(rows, width).astype(F32)
        grad = slots[:, piece + META :].reshape(rows, width).astype(F32)
        meta = slots[:, piece : piece + META].astype(F32)
        chosen_in = meta[:, : levels * experts, :piece]
        chosen_in = jnp.transpose(
            chosen_in.reshape(images, levels, experts, piece), (1, 0, 3, 2)
        ).reshape(levels, rows, experts)
        length = meta[0, levels * experts, 0] * 4.0 + meta[0, levels * experts + 1, 0]
        length = length.astype(jnp.int32)

        vectors = jnp.stack([ln1_gain, ln1_bias, ln2_gain, ln2_bias], -1)
        dense = lax.all_gather(
            jnp.concatenate([qkv_weight, out_weight, vectors, router_weight], -1),
            "dp",
            axis=1,
            tiled=True,
        )
        proj_packed_all = dense[..., : 3 * width]
        proj_out_all = dense[..., 3 * width : 4 * width]
        vectors = jnp.swapaxes(dense[..., 4 * width : 4 * width + 4], 1, 2)
        router_all = dense[..., 4 * width + 4 :]
        up_all = lax.all_to_all(expert_in, "dp", split_axis=3, concat_axis=2, tiled=True)
        up_all = jnp.swapaxes(up_all, 1, 2).reshape(levels, width, wide)
        down_all = expert_out.reshape(levels, wide, width)

        saved = []
        for level in range(levels):
            gain_one, bias_one, gain_two, bias_two = vectors[level]
            unit_one, inverse_one = normalize(state)
            normed = (unit_one * gain_one + bias_one).astype(BF16)
            packed = mm("ld,de->le", normed, proj_packed_all[level]).astype(BF16)
            keys_values = lax.all_gather(
                packed[:, width:], "dp", axis=0, tiled=True, axis_index_groups=plan.groups
            )
            queries = packed[:, :width]
            keys_all, values_all = keys_values[:, :width], keys_values[:, width:]
            scores = attention_scores(queries, keys_all, length)
            highest = jnp.max(scores, -1, keepdims=True)
            expo = jnp.exp(scores - highest)
            totals = jnp.sum(expo, -1, keepdims=True)
            log_total = highest + jnp.log(totals)
            weights = (expo / totals).astype(BF16)
            mixed = mm("hqk,khd->qhd", weights, heads_of(values_all)).reshape(rows, width).astype(BF16)
            middle = state + mm("ld,de->le", mixed, proj_out_all[level])
            unit_two, inverse_two = normalize(middle)
            normed_two = (unit_two * gain_two + bias_two).astype(BF16)
            logits = mm("ld,de->le", normed_two, router_all[level])
            gates = jax.nn.softmax(logits, -1)
            chosen = chosen_in[level]
            combine = gates * chosen
            all_two = lax.all_gather(normed_two, "dp", axis=0, tiled=True)
            all_combine = lax.all_gather(combine, "dp", axis=0, tiled=True)
            spread = jnp.repeat(all_combine, slice_hid, axis=1)
            act, slope = gelu_and_slope(mm("td,dh->th", all_two, up_all[level]))
            act, slope = act.astype(BF16), slope.astype(BF16)
            scaled = (act * spread).astype(BF16)
            update = lax.psum_scatter(
                mm("th,hd->td", scaled, down_all[level]).astype(BF16),
                "dp",
                scatter_dimension=0,
                tiled=True,
            )
            state = middle + update.astype(F32)
            saved.append(
                dict(
                    unit_one=unit_one,
                    inverse_one=inverse_one,
                    normed=normed,
                    queries=queries,
                    keys_all=keys_all,
                    values_all=values_all,
                    log_total=log_total,
                    mixed=mixed,
                    unit_two=unit_two,
                    inverse_two=inverse_two,
                    normed_two=normed_two,
                    gates=gates,
                    chosen=chosen,
                    spread=spread,
                    all_two=all_two,
                    act=act,
                    slope=slope,
                    scaled=scaled,
                )
            )
        output = plan.to_pieces(state.astype(BF16).reshape(images, piece, width))

        grads = [None] * levels
        for level in reversed(range(levels)):
            kept = saved[level]
            gain_one, bias_one, gain_two, bias_two = vectors[level]
            all_grad = lax.all_gather(grad.astype(BF16), "dp", axis=0, tiled=True)
            grad_act = mm("td,hd->th", all_grad, down_all[level])
            grad_combine = jnp.sum(
                (grad_act * kept["act"]).reshape(-1, experts, slice_hid), -1
            )
            grad_pre = (grad_act * kept["spread"] * kept["slope"]).astype(BF16)
            up_grad = mm("td,th->dh", kept["all_two"], grad_pre)
            down_grad = mm("th,td->hd", kept["scaled"], all_grad)
            back = lax.psum_scatter(
                mm("th,dh->td", grad_pre, up_all[level]).astype(BF16),
                "dp",
                scatter_dimension=0,
                tiled=True,
            ).astype(F32)
            grad_combine = lax.psum_scatter(grad_combine, "dp", scatter_dimension=0, tiled=True)
            gates = kept["gates"]
            grad_gates = grad_combine * kept["chosen"]
            grad_logits = gates * (grad_gates - jnp.sum(gates * grad_gates, -1, keepdims=True))
            router = router_all[level].astype(F32)
            back = back + jnp.dot(grad_logits, router.T, precision=lax.Precision.HIGHEST)
            router_grad = jnp.dot(
                kept["normed_two"].astype(F32).T, grad_logits, precision=lax.Precision.HIGHEST
            )
            unit_two = kept["unit_two"]
            gain_two_grad = jnp.sum(back * unit_two, 0)
            bias_two_grad = jnp.sum(back, 0)
            grad_middle = grad + norm_back(back * gain_two, unit_two, kept["inverse_two"])
            grad_branch = grad_middle.astype(BF16)
            out_grad = mm("ld,le->de", kept["mixed"], grad_branch)
            grad_mixed = mm("le,de->ld", grad_branch, proj_out_all[level]).astype(BF16)
            queries, keys_all, values_all = kept["queries"], kept["keys_all"], kept["values_all"]
            probs = jnp.exp(attention_scores(queries, keys_all, length) - kept["log_total"])
            grad_split = heads_of(grad_mixed)
            grad_v = mm("hqk,qhd->khd", probs.astype(BF16), grad_split)
            grad_probs = mm("qhd,khd->hqk", grad_split, heads_of(values_all))
            grad_scores = (
                probs * (grad_probs - jnp.sum(probs * grad_probs, -1, keepdims=True))
            ).astype(BF16)
            scale = HEAD ** (-0.5)
            grad_q = scale * mm("hqk,khd->qhd", grad_scores, heads_of(keys_all))
            grad_k = scale * mm("hqk,qhd->khd", grad_scores, heads_of(queries))
            grad_kv = jnp.concatenate(
                [grad_k.reshape(length_all, width), grad_v.reshape(length_all, width)], -1
            )
            grad_kv = lax.psum_scatter(
                grad_kv.astype(BF16),
                "dp",
                scatter_dimension=0,
                tiled=True,
                axis_index_groups=plan.groups,
            )
            grad_packed = jnp.concatenate([grad_q.reshape(rows, width).astype(BF16), grad_kv], -1)
            back_one = mm("le,de->ld", grad_packed, proj_packed_all[level])
            packed_grad = mm("ld,le->de", kept["normed"], grad_packed)
            unit_one = kept["unit_one"]
            gain_one_grad = jnp.sum(back_one * unit_one, 0)
            bias_one_grad = jnp.sum(back_one, 0)
            grad = grad_middle + norm_back(back_one * gain_one, unit_one, kept["inverse_one"])
            vector_grads = jnp.stack(
                [gain_one_grad, bias_one_grad, gain_two_grad, bias_two_grad], -1
            )
            dense_grad = jnp.concatenate([packed_grad, out_grad, vector_grads, router_grad], -1)
            dense_grad = lax.psum_scatter(
                dense_grad.astype(BF16), "dp", scatter_dimension=0, tiled=True
            )
            up_grad = jnp.swapaxes(up_grad.astype(BF16).reshape(width, experts, slice_hid), 0, 1)
            up_grad = lax.all_to_all(up_grad, "dp", split_axis=1, concat_axis=2, tiled=True)
            grads[level] = (
                lax.psum(dense_grad, "seq").astype(F32),
                lax.psum(up_grad, "seq").astype(F32),
                lax.psum(
                    down_grad.astype(BF16).reshape(experts, slice_hid, width), "seq"
                ).astype(F32),
            )
        token_grad = plan.to_pieces(grad.astype(BF16).reshape(images, piece, width)).astype(F32)
        dense_grad, up_grad, down_grad = (jnp.stack(items) for items in zip(*grads))
        vector_grads = dense_grad[..., 4 * width : 4 * width + 4]
        return (
            output,
            token_grad,
            vector_grads[..., 0],
            vector_grads[..., 1],
            dense_grad[..., : 3 * width],
            dense_grad[..., 3 * width : 4 * width],
            vector_grads[..., 2],
            vector_grads[..., 3],
            dense_grad[..., 4 * width + 4 :],
            up_grad,
            down_grad,
        )

    return shards


def solution(mesh):
    return jax.shard_map(
        build(mesh),
        mesh=mesh,
        in_specs=(
            P("dp", "seq", None),
            P("dp", "seq", None),
            P(None, "dp", "seq", None),
            P("dp", None),
            P(None, "dp"),
            P(None, "dp"),
            P(None, "dp", None),
            P(None, "dp", None),
            P(None, "dp"),
            P(None, "dp"),
            P(None, "dp", None),
            P(None, None, "dp", None),
            P(None, None, "dp", None),
        ),
        out_specs=(
            P("dp", "seq", None),
            P("dp", "seq", None),
            P(None, "dp"),
            P(None, "dp"),
            P(None, "dp", None),
            P(None, "dp", None),
            P(None, "dp"),
            P(None, "dp"),
            P(None, "dp", None),
            P(None, None, "dp", None),
            P(None, None, "dp", None),
        ),
        check_vma=False,
    )
```

```python
import jax
import jax.numpy as jnp
from jax import lax
from jax.experimental import pallas as pl
from jax.experimental.pallas import tpu as pltpu
from jax.sharding import PartitionSpec as P

HEAD = 64
EPS = 1e-06
NEG = -1e30
META = 16
F32 = jnp.float32
BF16 = jnp.bfloat16


def normalize(values):
    center = values - jnp.mean(values, -1, keepdims=True)
    inverse = lax.rsqrt(jnp.mean(center * center, -1, keepdims=True) + EPS)
    return center * inverse, inverse


def norm_back(grad_unit, unit, inverse):
    return inverse * (
        grad_unit
        - jnp.mean(grad_unit, -1, keepdims=True)
        - unit * jnp.mean(grad_unit * unit, -1, keepdims=True)
    )


def heads_of(values):
    return values.reshape(values.shape[0], values.shape[1] // HEAD, HEAD)


def mm(form, left, right):
    return jnp.einsum(form, left, right, preferred_element_type=F32)


MESH = pl.DeviceIdType.MESH
VMEM_LIMIT = 60 * 1024 * 1024


def in_vmem():
    return pl.BlockSpec(memory_space=pltpu.VMEM)


def in_any():
    return pl.BlockSpec(memory_space=pl.ANY)


def greet(peers):
    barrier = pltpu.get_barrier_semaphore()
    for peer in peers:
        pl.semaphore_signal(barrier, inc=1, device_id=peer, device_id_type=MESH)
    pl.semaphore_wait(barrier, len(peers))


def remote(src, dst, send, recv, peer):
    return pltpu.make_async_remote_copy(
        src_ref=src, dst_ref=dst, send_sem=send, recv_sem=recv, device_id=peer, device_id_type=MESH
    )


def split_rows(rows8):
    high = rows8.astype(BF16).astype(F32)
    return jnp.concatenate([high, rows8 - high], 0).astype(BF16)


def join_rows(rows16):
    wide = rows16.astype(F32)
    return wide[:8] + wide[8:]


def gelu_parts(u):
    x = jnp.abs(u) * 0.7071067811865476
    bell = jnp.exp(-x * x)
    t = 1.0 / (1.0 + 0.3275911 * x)
    poly = t * (
        0.254829592 + t * (-0.284496736 + t * (1.421413741 + t * (-1.453152027 + t * 1.061405429)))
    )
    half = 0.5 * poly * bell
    cdf = jnp.where(u >= 0, 1.0 - half, half)
    return u * cdf, cdf + u * bell * 0.3989422804014327


def dot(left, right, dims=((1,), (0,))):
    return lax.dot_general(left, right, (dims, ((), ())), preferred_element_type=F32)


class Group:
    def __init__(self, size):
        self.size = size
        self.pairs = size // 2

    def peers(self):
        me = lax.axis_index("dp")
        return [{"dp": me ^ 1}] + [{"dp": me ^ (2 * pair)} for pair in range(1, self.pairs)]

    def scratch(self, rows, tail, width):
        full = rows + tail
        return [
            pltpu.VMEM((self.pairs, rows, width), F32),
            pltpu.VMEM((self.pairs, 16, width), F32),
            pltpu.VMEM((self.pairs, full, width), BF16),
            pltpu.VMEM((self.pairs, full, width), BF16),
            pltpu.VMEM((self.pairs, full, width), BF16),
            pltpu.VMEM((self.pairs, full, width), BF16),
            pltpu.SemaphoreType.DMA((self.size,)),
            pltpu.SemaphoreType.DMA((self.size,)),
            pltpu.SemaphoreType.DMA((self.size,)),
            pltpu.SemaphoreType.DMA((self.pairs,)),
            pltpu.SemaphoreType.DMA((self.pairs,)),
            pltpu.SemaphoreType.DMA((self.pairs,)),
            pltpu.SemaphoreType.DMA((self.pairs,)),
        ]

    def run(self, slots, scratch, rows, tail, compute):
        own, own_tail, give, take, pay, due, send, recv, hand, g_send, g_recv, p_send, p_recv = scratch
        me = lax.axis_index("dp")
        next_core = {"dp": me ^ 1}

        def block(slot, peer):
            return remote(slots.at[0], slots.at[slot], send.at[slot], recv.at[slot], peer)

        def handed(slot):
            return remote(slots.at[slot], slots.at[slot + 1], hand.at[slot], recv.at[slot + 1], next_core)

        def given(pair):
            return remote(give.at[pair], take.at[pair], g_send.at[pair], g_recv.at[pair], next_core)

        def paid(pair):
            owner = {"dp": me ^ (2 * pair)}
            return remote(pay.at[pair], due.at[pair], p_send.at[pair], p_recv.at[pair], owner)

        def settle(pair):
            given(pair).wait_recv()
            own[pair] += take[pair, :rows].astype(F32)
            if tail:
                own_tail[pair, :8] += join_rows(take[pair, rows:])

            @pl.when(pair > 0)
            def _():
                pay[pair, :rows] = own[pair].astype(BF16)
                if tail:
                    pay[pair, rows:] = split_rows(own_tail[pair, :8])
                paid(pair).start()

        block(1, next_core).start()
        for pair in range(1, self.pairs):
            block(2 * pair, {"dp": me ^ (2 * pair)}).start()

        def step(slot, carry):
            pair = slot // 2
            even = lax.rem(slot, 2) == 0

            @pl.when(slot > 0)
            def _():
                block(slot, next_core).wait_recv()

            @pl.when(even & (slot > 0))
            def _():
                handed(slot).start()

            total, total_tail = compute(slot)

            @pl.when(even)
            def _():
                own[pair] = total
                if tail:
                    own_tail[pair, :8] = total_tail

            @pl.when(jnp.logical_not(even))
            def _():
                give[pair, :rows] = total.astype(BF16)
                if tail:
                    give[pair, rows:] = split_rows(total_tail)
                given(pair).start()

            @pl.when(even & (slot > 0))
            def _():
                settle(pair - 1)

            return carry

        lax.fori_loop(0, self.size, step, 0)
        settle(self.pairs - 1)

    def collect(self, scratch, slots, rows, tail):
        own, own_tail, give, take, pay, due, send, recv, hand, g_send, g_recv, p_send, p_recv = scratch
        me = lax.axis_index("dp")
        next_core = {"dp": me ^ 1}
        for pair in range(1, self.pairs):
            remote(pay.at[pair], due.at[pair], p_send.at[pair], p_recv.at[pair], next_core).wait_recv()
            own[0] += due[pair, :rows].astype(F32)
            if tail:
                own_tail[0, :8] += join_rows(due[pair, rows:])
        for pair in range(self.pairs):
            remote(give.at[pair], take.at[pair], g_send.at[pair], g_recv.at[pair], next_core).wait_send()
            if pair:
                remote(
                    pay.at[pair], due.at[pair], p_send.at[pair], p_recv.at[pair], next_core
                ).wait_send()
                slot = 2 * pair
                remote(
                    slots.at[slot], slots.at[slot], send.at[slot], recv.at[slot], next_core
                ).wait_send()
                remote(
                    slots.at[slot], slots.at[slot], hand.at[slot], recv.at[slot], next_core
                ).wait_send()
        remote(slots.at[1], slots.at[1], send.at[1], recv.at[1], next_core).wait_send()


def experts_forward(message, middle, up, down, size, experts):
    rows, width = middle.shape
    wide = up.shape[1]
    hid = wide // experts
    group = Group(size)

    def kernel(msg_ref, mid_ref, up_ref, down_ref, out_ref, all_ref, act_ref, slope_ref, *scratch):
        slots, act, slope, scaled, save_sem = scratch[:5]
        scratch = scratch[5:]
        greet(group.peers())
        slots[0] = msg_ref[...]

        def saves(slot):
            return (
                pltpu.make_async_copy(slots.at[slot], all_ref.at[slot], save_sem.at[slot, 0]),
                pltpu.make_async_copy(act.at[slot], act_ref.at[slot], save_sem.at[slot, 1]),
                pltpu.make_async_copy(slope.at[slot], slope_ref.at[slot], save_sem.at[slot, 2]),
            )

        def compute(slot):
            gates = jnp.transpose(join_rows(slots[slot, rows:]))[:rows]
            for expert in range(experts):
                cols = slice(expert * hid, (expert + 1) * hid)
                value, grade = gelu_parts(dot(slots[slot, :rows], up_ref[:, cols]))
                value = value.astype(BF16)
                act[slot, :, cols] = value
                slope[slot, :, cols] = grade.astype(BF16)
                scaled[:, cols] = (value.astype(F32) * gates[:, expert : expert + 1]).astype(BF16)
            for save in saves(slot):
                save.start()
            return dot(scaled[...], down_ref[...]), None

        group.run(slots, scratch, rows, 0, compute)
        group.collect(scratch, slots, rows, 0)
        out_ref[...] = mid_ref[...] + scratch[0][0]
        for slot in range(size):
            for save in saves(slot):
                save.wait()

    return pl.pallas_call(
        kernel,
        out_shape=(
            jax.ShapeDtypeStruct((rows, width), F32),
            jax.ShapeDtypeStruct((size, rows + META, width), BF16),
            jax.ShapeDtypeStruct((size, rows, wide), BF16),
            jax.ShapeDtypeStruct((size, rows, wide), BF16),
        ),
        in_specs=[in_vmem()] * 4,
        out_specs=(in_vmem(), in_any(), in_any(), in_any()),
        scratch_shapes=[
            pltpu.VMEM((size, rows + META, width), BF16),
            pltpu.VMEM((size, rows, wide), BF16),
            pltpu.VMEM((size, rows, wide), BF16),
            pltpu.VMEM((rows, wide), BF16),
            pltpu.SemaphoreType.DMA((size, 3)),
        ]
        + group.scratch(rows, 0, width),
        compiler_params=pltpu.CompilerParams(
            collective_id=1, has_side_effects=True, vmem_limit_bytes=VMEM_LIMIT
        ),
        name="experts_forward",
    )(message, middle, up, down)


def experts_backward(grad, blocks, act, slope, up, down, size, experts):
    rows, width = grad.shape
    wide = up.shape[1]
    hid = wide // experts
    group = Group(size)

    def kernel(
        grad_ref, blocks_ref, act_ref, slope_ref, up_ref, down_ref,
        out_ref, tail_ref, up_out, down_out, *scratch,
    ):
        slots, blocks, act, slope, weighed, scaled, pre, load_sem = scratch[:8]
        scratch = scratch[8:]

        def loads(slot):
            two = lax.rem(slot, 2)
            return (
                pltpu.make_async_copy(blocks_ref.at[slot], blocks.at[slot], load_sem.at[two, 0]),
                pltpu.make_async_copy(act_ref.at[slot], act.at[two], load_sem.at[two, 1]),
                pltpu.make_async_copy(slope_ref.at[slot], slope.at[two], load_sem.at[two, 2]),
            )

        for load in loads(0):
            load.start()
        greet(group.peers())
        slots[0] = grad_ref[...]
        lane = lax.broadcasted_iota(jnp.int32, (16, wide), 1) // hid
        pick = (lane == lax.broadcasted_iota(jnp.int32, (16, wide), 0)).astype(F32).astype(BF16)

        def compute(slot):
            two = lax.rem(slot, 2)

            @pl.when(slot + 1 < size)
            def _():
                for load in loads(slot + 1):
                    load.start()

            for load in loads(slot):
                load.wait()
            gates = jnp.transpose(join_rows(blocks[slot, rows:]))[:rows]
            place = pl.ds(pl.multiple_of(slot * rows, 16), rows)
            for expert in range(experts):
                cols = slice(expert * hid, (expert + 1) * hid)
                gate = gates[:, expert : expert + 1]
                pull = dot(slots[slot], down_ref[cols, :], ((1,), (1,)))
                value = act[two, :, cols].astype(F32)
                weighed[:, cols] = (pull * value).astype(BF16)
                scaled[place, cols] = (value * gate).astype(BF16)
                pre[place, cols] = (pull * gate * slope[two, :, cols].astype(F32)).astype(BF16)
            by_expert = dot(pick, weighed[...], ((1,), (1,)))[:8]
            if rows < width:
                by_expert = jnp.concatenate([by_expert, jnp.zeros((8, width - rows), F32)], 1)
            return dot(pre[place, :], up_ref[...], ((1,), (1,))), by_expert

        group.run(slots, scratch, rows, 16, compute)

        for expert in range(experts):
            cols = slice(expert * hid, (expert + 1) * hid)
            up_sum = jnp.zeros((width, hid), F32)
            down_sum = jnp.zeros((hid, width), F32)

            def add(slot, sums):
                place = pl.ds(pl.multiple_of(slot * rows, 16), rows)
                return (
                    sums[0] + dot(blocks[slot, :rows], pre[place, cols], ((0,), (0,))),
                    sums[1] + dot(scaled[place, cols], slots[slot], ((0,), (0,))),
                )

            up_sum, down_sum = lax.fori_loop(0, size, add, (up_sum, down_sum))
            up_out[:, cols] = up_sum.astype(BF16)
            down_out[cols, :] = down_sum.astype(BF16)

        group.collect(scratch, slots, rows, 16)
        out_ref[...] = scratch[0][0]
        tail_ref[...] = scratch[1][0, :8]

    return pl.pallas_call(
        kernel,
        out_shape=(
            jax.ShapeDtypeStruct((rows, width), F32),
            jax.ShapeDtypeStruct((8, width), F32),
            jax.ShapeDtypeStruct((width, wide), BF16),
            jax.ShapeDtypeStruct((wide, width), BF16),
        ),
        in_specs=[in_vmem(), in_any(), in_any(), in_any(), in_vmem(), in_vmem()],
        out_specs=(in_vmem(),) * 4,
        scratch_shapes=[
            pltpu.VMEM((size, rows, width), BF16),
            pltpu.VMEM((size, rows + META, width), BF16),
            pltpu.VMEM((2, rows, wide), BF16),
            pltpu.VMEM((2, rows, wide), BF16),
            pltpu.VMEM((rows, wide), BF16),
            pltpu.VMEM((size * rows, wide), BF16),
            pltpu.VMEM((size * rows, wide), BF16),
            pltpu.SemaphoreType.DMA((2, 3)),
        ]
        + group.scratch(rows, 16, width),
        compiler_params=pltpu.CompilerParams(
            collective_id=2, has_side_effects=True, vmem_limit_bytes=VMEM_LIMIT
        ),
        name="experts_backward",
    )(grad, blocks, act, slope, up, down)


class Plan:
    def __init__(self, mesh, images, length):
        self.dp = mesh.shape["dp"]
        self.seq = mesh.shape["seq"]
        self.images = images
        self.piece = length // self.seq
        self.share = self.seq // images
        self.rows = images * self.piece
        self.groups = [
            [block * self.share + part for part in range(self.share)]
            for block in range(self.dp // self.share)
        ]

    def hops(self, turn):
        pairs = []
        for dp in range(self.dp):
            for seq in range(self.seq):
                local = (seq % self.images + turn) % self.images
                to_dp = dp // self.share * self.share + seq // self.images
                to_seq = dp % self.share * self.images + local
                pairs.append((dp * self.seq + seq, to_dp * self.seq + to_seq))
        return pairs

    def to_images(self, pieces):
        seq = lax.axis_index("seq") % self.images
        got = []
        for turn in range(self.images):
            piece = lax.dynamic_index_in_dim(pieces, (seq + turn) % self.images, 0, False)
            got.append(lax.ppermute(piece, ("dp", "seq"), self.hops(turn)))
        got = jnp.stack(got)
        return jnp.stack(
            [
                lax.dynamic_index_in_dim(got, (seq - slot) % self.images, 0, False)
                for slot in range(self.images)
            ]
        )

    def to_pieces(self, slots):
        seq = lax.axis_index("seq") % self.images
        got = []
        for turn in range(self.images):
            slot = lax.dynamic_index_in_dim(slots, (seq - turn) % self.images, 0, False)
            back = [(to, source) for source, to in self.hops(turn)]
            got.append(lax.ppermute(slot, ("dp", "seq"), back))
        got = jnp.stack(got)
        return jnp.stack(
            [
                lax.dynamic_index_in_dim(got, (local - seq) % self.images, 0, False)
                for local in range(self.images)
            ]
        )


def attention_scores(queries, keys_all, length):
    scores = mm("qhd,khd->hqk", heads_of(queries), heads_of(keys_all)) * HEAD ** (-0.5)
    valid = jnp.arange(keys_all.shape[0]) < length
    return jnp.where(valid[None, None, :], scores, NEG)


def build(mesh):
    def shards(
        tokens,
        cotangent,
        routes,
        token_mask,
        ln1_gain,
        ln1_bias,
        qkv_weight,
        out_weight,
        ln2_gain,
        ln2_bias,
        router_weight,
        expert_in,
        expert_out,
    ):
        images, piece, width = tokens.shape
        levels, experts = expert_in.shape[:2]
        length_all = token_mask.shape[1]
        plan = Plan(mesh, images, length_all)
        rows = plan.rows
        slice_hid = expert_out.shape[2]
        wide = experts * slice_hid
        part = lax.axis_index("dp") % plan.share

        start = lax.axis_index("seq") * piece
        local_valid = lax.dynamic_slice_in_dim(token_mask, start, piece, 1)
        chosen_all = jnp.sum(
            (routes[..., None] == jnp.arange(experts, dtype=jnp.int32)).astype(F32), -2
        )
        chosen_rows = jnp.transpose(chosen_all, (1, 0, 3, 2)).reshape(images, levels * experts, piece)
        lengths = jnp.sum(token_mask, -1)
        meta = jnp.zeros((images, META, width), F32)
        meta = meta.at[:, : levels * experts, :piece].set(chosen_rows)
        meta = meta.at[:, levels * experts, 0].set((lengths // 4).astype(F32))
        meta = meta.at[:, levels * experts + 1, 0].set((lengths % 4).astype(F32))
        masked = cotangent * local_valid[..., None].astype(BF16)
        slots = plan.to_images(jnp.concatenate([tokens, meta.astype(BF16), masked], 1))
        state = slots[:, :piece].reshape(rows, width).astype(F32)
        grad = slots[:, piece + META :].reshape(rows, width).astype(F32)
        meta = slots[:, piece : piece + META].astype(F32)
        chosen_in = meta[:, : levels * experts, :piece]
        chosen_in = jnp.transpose(
            chosen_in.reshape(images, levels, experts, piece), (1, 0, 3, 2)
        ).reshape(levels, rows, experts)
        length = meta[0, levels * experts, 0] * 4.0 + meta[0, levels * experts + 1, 0]
        length = length.astype(jnp.int32)

        vectors = jnp.stack([ln1_gain, ln1_bias, ln2_gain, ln2_bias], -1)
        dense = lax.all_gather(
            jnp.concatenate([qkv_weight, out_weight, vectors, router_weight], -1),
            "dp",
            axis=1,
            tiled=True,
        )
        proj_packed_all = dense[..., : 3 * width]
        proj_out_all = dense[..., 3 * width : 4 * width]
        vectors = jnp.swapaxes(dense[..., 4 * width : 4 * width + 4], 1, 2)
        router_all = dense[..., 4 * width + 4 :]
        up_all = lax.all_to_all(expert_in, "dp", split_axis=3, concat_axis=2, tiled=True)
        up_all = jnp.swapaxes(up_all, 1, 2).reshape(levels, width, wide)
        down_all = expert_out.reshape(levels, wide, width)

        saved = []
        for level in range(levels):
            gain_one, bias_one, gain_two, bias_two = vectors[level]
            unit_one, inverse_one = normalize(state)
            normed = (unit_one * gain_one + bias_one).astype(BF16)
            packed = mm("ld,de->le", normed, proj_packed_all[level]).astype(BF16)
            keys_values = lax.all_gather(
                packed[:, width:], "dp", axis=0, tiled=True, axis_index_groups=plan.groups
            )
            queries = packed[:, :width]
            keys_all, values_all = keys_values[:, :width], keys_values[:, width:]
            scores = attention_scores(queries, keys_all, length)
            highest = jnp.max(scores, -1, keepdims=True)
            expo = jnp.exp(scores - highest)
            totals = jnp.sum(expo, -1, keepdims=True)
            log_total = highest + jnp.log(totals)
            weights = (expo / totals).astype(BF16)
            mixed = mm("hqk,khd->qhd", weights, heads_of(values_all)).reshape(rows, width).astype(BF16)
            middle = state + mm("ld,de->le", mixed, proj_out_all[level])
            unit_two, inverse_two = normalize(middle)
            normed_two = (unit_two * gain_two + bias_two).astype(BF16)
            logits = mm("ld,de->le", normed_two, router_all[level])
            gates = jax.nn.softmax(logits, -1)
            chosen = chosen_in[level]
            combine = gates * chosen
            gate_rows = jnp.zeros((8, width), F32).at[:experts, :rows].set(combine.T)
            message = jnp.concatenate([normed_two, split_rows(gate_rows)], 0)
            state, blocks, act, slope = experts_forward(
                message, middle, up_all[level], down_all[level], plan.dp, experts
            )
            saved.append(
                dict(
                    unit_one=unit_one,
                    inverse_one=inverse_one,
                    normed=normed,
                    queries=queries,
                    keys_all=keys_all,
                    values_all=values_all,
                    log_total=log_total,
                    mixed=mixed,
                    unit_two=unit_two,
                    inverse_two=inverse_two,
                    normed_two=normed_two,
                    gates=gates,
                    chosen=chosen,
                    blocks=blocks,
                    act=act,
                    slope=slope,
                )
            )
        output = plan.to_pieces(state.astype(BF16).reshape(images, piece, width))

        grads = [None] * levels
        for level in reversed(range(levels)):
            kept = saved[level]
            gain_one, bias_one, gain_two, bias_two = vectors[level]
            back, back_tail, up_grad, down_grad = experts_backward(
                grad.astype(BF16),
                kept["blocks"],
                kept["act"],
                kept["slope"],
                up_all[level],
                down_all[level],
                plan.dp,
                experts,
            )
            grad_combine = back_tail[:experts, :rows].T
            gates = kept["gates"]
            grad_gates = grad_combine * kept["chosen"]
            grad_logits = gates * (grad_gates - jnp.sum(gates * grad_gates, -1, keepdims=True))
            router = router_all[level].astype(F32)
            back = back + jnp.dot(grad_logits, router.T, precision=lax.Precision.HIGHEST)
            router_grad = jnp.dot(
                kept["normed_two"].astype(F32).T, grad_logits, precision=lax.Precision.HIGHEST
            )
            unit_two = kept["unit_two"]
            gain_two_grad = jnp.sum(back * unit_two, 0)
            bias_two_grad = jnp.sum(back, 0)
            grad_middle = grad + norm_back(back * gain_two, unit_two, kept["inverse_two"])
            grad_branch = grad_middle.astype(BF16)
            out_grad = mm("ld,le->de", kept["mixed"], grad_branch)
            grad_mixed = mm("le,de->ld", grad_branch, proj_out_all[level]).astype(BF16)
            queries, keys_all, values_all = kept["queries"], kept["keys_all"], kept["values_all"]
            probs = jnp.exp(attention_scores(queries, keys_all, length) - kept["log_total"])
            grad_split = heads_of(grad_mixed)
            grad_v = mm("hqk,qhd->khd", probs.astype(BF16), grad_split)
            grad_probs = mm("qhd,khd->hqk", grad_split, heads_of(values_all))
            grad_scores = (
                probs * (grad_probs - jnp.sum(probs * grad_probs, -1, keepdims=True))
            ).astype(BF16)
            scale = HEAD ** (-0.5)
            grad_q = scale * mm("hqk,khd->qhd", grad_scores, heads_of(keys_all))
            grad_k = scale * mm("hqk,qhd->khd", grad_scores, heads_of(queries))
            grad_kv = jnp.concatenate(
                [grad_k.reshape(length_all, width), grad_v.reshape(length_all, width)], -1
            )
            grad_kv = lax.psum_scatter(
                grad_kv.astype(BF16),
                "dp",
                scatter_dimension=0,
                tiled=True,
                axis_index_groups=plan.groups,
            )
            grad_packed = jnp.concatenate([grad_q.reshape(rows, width).astype(BF16), grad_kv], -1)
            back_one = mm("le,de->ld", grad_packed, proj_packed_all[level])
            packed_grad = mm("ld,le->de", kept["normed"], grad_packed)
            unit_one = kept["unit_one"]
            gain_one_grad = jnp.sum(back_one * unit_one, 0)
            bias_one_grad = jnp.sum(back_one, 0)
            grad = grad_middle + norm_back(back_one * gain_one, unit_one, kept["inverse_one"])
            vector_grads = jnp.stack(
                [gain_one_grad, bias_one_grad, gain_two_grad, bias_two_grad], -1
            )
            dense_grad = jnp.concatenate([packed_grad, out_grad, vector_grads, router_grad], -1)
            dense_grad = lax.psum_scatter(
                dense_grad.astype(BF16), "dp", scatter_dimension=0, tiled=True
            )
            up_grad = jnp.swapaxes(up_grad.astype(BF16).reshape(width, experts, slice_hid), 0, 1)
            up_grad = lax.all_to_all(up_grad, "dp", split_axis=1, concat_axis=2, tiled=True)
            grads[level] = (
                lax.psum(dense_grad, "seq").astype(F32),
                lax.psum(up_grad, "seq").astype(F32),
                lax.psum(
                    down_grad.astype(BF16).reshape(experts, slice_hid, width), "seq"
                ).astype(F32),
            )
        token_grad = plan.to_pieces(grad.astype(BF16).reshape(images, piece, width)).astype(F32)
        dense_grad, up_grad, down_grad = (jnp.stack(items) for items in zip(*grads))
        vector_grads = dense_grad[..., 4 * width : 4 * width + 4]
        return (
            output,
            token_grad,
            vector_grads[..., 0],
            vector_grads[..., 1],
            dense_grad[..., : 3 * width],
            dense_grad[..., 3 * width : 4 * width],
            vector_grads[..., 2],
            vector_grads[..., 3],
            dense_grad[..., 4 * width + 4 :],
            up_grad,
            down_grad,
        )

    return shards


def solution(mesh):
    return jax.shard_map(
        build(mesh),
        mesh=mesh,
        in_specs=(
            P("dp", "seq", None),
            P("dp", "seq", None),
            P(None, "dp", "seq", None),
            P("dp", None),
            P(None, "dp"),
            P(None, "dp"),
            P(None, "dp", None),
            P(None, "dp", None),
            P(None, "dp"),
            P(None, "dp"),
            P(None, "dp", None),
            P(None, None, "dp", None),
            P(None, None, "dp", None),
        ),
        out_specs=(
            P("dp", "seq", None),
            P("dp", "seq", None),
            P(None, "dp"),
            P(None, "dp"),
            P(None, "dp", None),
            P(None, "dp", None),
            P(None, "dp"),
            P(None, "dp"),
            P(None, "dp", None),
            P(None, None, "dp", None),
            P(None, None, "dp", None),
        ),
        check_vma=False,
    )
```

```python
import jax
import jax.numpy as jnp
from jax import lax
from jax.experimental import pallas as pl
from jax.experimental.pallas import tpu as pltpu
from jax.sharding import PartitionSpec as P

HEAD = 64
EPS = 1e-06
NEG = -1e30
META = 16
F32 = jnp.float32
BF16 = jnp.bfloat16


def normalize(values):
    center = values - jnp.mean(values, -1, keepdims=True)
    inverse = lax.rsqrt(jnp.mean(center * center, -1, keepdims=True) + EPS)
    return center * inverse, inverse


def norm_back(grad_unit, unit, inverse):
    return inverse * (
        grad_unit
        - jnp.mean(grad_unit, -1, keepdims=True)
        - unit * jnp.mean(grad_unit * unit, -1, keepdims=True)
    )


MESH = pl.DeviceIdType.MESH
VMEM_LIMIT = 60 * 1024 * 1024


def in_vmem():
    return pl.BlockSpec(memory_space=pltpu.VMEM)


def in_any():
    return pl.BlockSpec(memory_space=pl.ANY)


def greet(peers):
    barrier = pltpu.get_barrier_semaphore()
    for peer in peers:
        pl.semaphore_signal(barrier, inc=1, device_id=peer, device_id_type=MESH)
    pl.semaphore_wait(barrier, len(peers))


def remote(src, dst, send, recv, peer):
    return pltpu.make_async_remote_copy(
        src_ref=src, dst_ref=dst, send_sem=send, recv_sem=recv, device_id=peer, device_id_type=MESH
    )


def split_rows(rows8):
    high = rows8.astype(BF16).astype(F32)
    return jnp.concatenate([high, rows8 - high], 0).astype(BF16)


def join_rows(rows16):
    wide = rows16.astype(F32)
    return wide[:8] + wide[8:]


def gelu_parts(u):
    x = jnp.abs(u) * 0.7071067811865476
    bell = jnp.exp(-x * x)
    t = 1.0 / (1.0 + 0.3275911 * x)
    poly = t * (
        0.254829592 + t * (-0.284496736 + t * (1.421413741 + t * (-1.453152027 + t * 1.061405429)))
    )
    half = 0.5 * poly * bell
    cdf = jnp.where(u >= 0, 1.0 - half, half)
    return u * cdf, cdf + u * bell * 0.3989422804014327


def dot(left, right, dims=((1,), (0,))):
    return lax.dot_general(left, right, (dims, ((), ())), preferred_element_type=F32)


class Group:
    def __init__(self, size):
        self.size = size
        self.pairs = size // 2

    def peers(self):
        me = lax.axis_index("dp")
        return [{"dp": me ^ 1}] + [{"dp": me ^ (2 * pair)} for pair in range(1, self.pairs)]

    def scratch(self, rows, tail, width):
        full = rows + tail
        return [
            pltpu.VMEM((self.pairs, rows, width), F32),
            pltpu.VMEM((self.pairs, 16, width), F32),
            pltpu.VMEM((self.pairs, full, width), BF16),
            pltpu.VMEM((self.pairs, full, width), BF16),
            pltpu.VMEM((self.pairs, full, width), BF16),
            pltpu.VMEM((self.pairs, full, width), BF16),
            pltpu.SemaphoreType.DMA((self.size,)),
            pltpu.SemaphoreType.DMA((self.size,)),
            pltpu.SemaphoreType.DMA((self.size,)),
            pltpu.SemaphoreType.DMA((self.pairs,)),
            pltpu.SemaphoreType.DMA((self.pairs,)),
            pltpu.SemaphoreType.DMA((self.pairs,)),
            pltpu.SemaphoreType.DMA((self.pairs,)),
        ]

    def run(self, slots, scratch, rows, tail, compute):
        own, own_tail, give, take, pay, due, send, recv, hand, g_send, g_recv, p_send, p_recv = scratch
        me = lax.axis_index("dp")
        next_core = {"dp": me ^ 1}

        def block(slot, peer):
            return remote(slots.at[0], slots.at[slot], send.at[slot], recv.at[slot], peer)

        def handed(slot):
            return remote(slots.at[slot], slots.at[slot + 1], hand.at[slot], recv.at[slot + 1], next_core)

        def given(pair):
            return remote(give.at[pair], take.at[pair], g_send.at[pair], g_recv.at[pair], next_core)

        def paid(pair):
            owner = {"dp": me ^ (2 * pair)}
            return remote(pay.at[pair], due.at[pair], p_send.at[pair], p_recv.at[pair], owner)

        def settle(pair):
            given(pair).wait_recv()
            own[pair] += take[pair, :rows].astype(F32)
            if tail:
                own_tail[pair, :8] += join_rows(take[pair, rows:])

            @pl.when(pair > 0)
            def _():
                pay[pair, :rows] = own[pair].astype(BF16)
                if tail:
                    pay[pair, rows:] = split_rows(own_tail[pair, :8])
                paid(pair).start()

        block(1, next_core).start()
        for pair in range(1, self.pairs):
            block(2 * pair, {"dp": me ^ (2 * pair)}).start()

        def step(slot, carry):
            pair = slot // 2
            even = lax.rem(slot, 2) == 0

            @pl.when(slot > 0)
            def _():
                block(slot, next_core).wait_recv()

            @pl.when(even & (slot > 0))
            def _():
                handed(slot).start()

            total, total_tail = compute(slot)

            @pl.when(even)
            def _():
                own[pair] = total
                if tail:
                    own_tail[pair, :8] = total_tail

            @pl.when(jnp.logical_not(even))
            def _():
                give[pair, :rows] = total.astype(BF16)
                if tail:
                    give[pair, rows:] = split_rows(total_tail)
                given(pair).start()

            @pl.when(even & (slot > 0))
            def _():
                settle(pair - 1)

            return carry

        lax.fori_loop(0, self.size, step, 0)
        settle(self.pairs - 1)

    def collect(self, scratch, slots, rows, tail):
        own, own_tail, give, take, pay, due, send, recv, hand, g_send, g_recv, p_send, p_recv = scratch
        me = lax.axis_index("dp")
        next_core = {"dp": me ^ 1}
        for pair in range(1, self.pairs):
            remote(pay.at[pair], due.at[pair], p_send.at[pair], p_recv.at[pair], next_core).wait_recv()
            own[0] += due[pair, :rows].astype(F32)
            if tail:
                own_tail[0, :8] += join_rows(due[pair, rows:])
        for pair in range(self.pairs):
            remote(give.at[pair], take.at[pair], g_send.at[pair], g_recv.at[pair], next_core).wait_send()
            if pair:
                remote(
                    pay.at[pair], due.at[pair], p_send.at[pair], p_recv.at[pair], next_core
                ).wait_send()
                slot = 2 * pair
                remote(
                    slots.at[slot], slots.at[slot], send.at[slot], recv.at[slot], next_core
                ).wait_send()
                remote(
                    slots.at[slot], slots.at[slot], hand.at[slot], recv.at[slot], next_core
                ).wait_send()
        remote(slots.at[1], slots.at[1], send.at[1], recv.at[1], next_core).wait_send()


def experts_forward(message, middle, up, down, size, experts):
    rows, width = middle.shape
    wide = up.shape[1]
    hid = wide // experts
    group = Group(size)

    def kernel(msg_ref, mid_ref, up_ref, down_ref, out_ref, all_ref, act_ref, slope_ref, *scratch):
        slots, act, slope, scaled, save_sem = scratch[:5]
        scratch = scratch[5:]
        greet(group.peers())
        slots[0] = msg_ref[...]

        def saves(slot):
            return (
                pltpu.make_async_copy(slots.at[slot], all_ref.at[slot], save_sem.at[slot, 0]),
                pltpu.make_async_copy(act.at[slot], act_ref.at[slot], save_sem.at[slot, 1]),
                pltpu.make_async_copy(slope.at[slot], slope_ref.at[slot], save_sem.at[slot, 2]),
            )

        def compute(slot):
            gates = jnp.transpose(join_rows(slots[slot, rows:]))[:rows]
            for expert in range(experts):
                cols = slice(expert * hid, (expert + 1) * hid)
                value, grade = gelu_parts(dot(slots[slot, :rows], up_ref[:, cols]))
                value = value.astype(BF16)
                act[slot, :, cols] = value
                slope[slot, :, cols] = grade.astype(BF16)
                scaled[:, cols] = (value.astype(F32) * gates[:, expert : expert + 1]).astype(BF16)
            for save in saves(slot):
                save.start()
            return dot(scaled[...], down_ref[...]), None

        group.run(slots, scratch, rows, 0, compute)
        group.collect(scratch, slots, rows, 0)
        out_ref[...] = mid_ref[...] + scratch[0][0]
        for slot in range(size):
            for save in saves(slot):
                save.wait()

    return pl.pallas_call(
        kernel,
        out_shape=(
            jax.ShapeDtypeStruct((rows, width), F32),
            jax.ShapeDtypeStruct((size, rows + META, width), BF16),
            jax.ShapeDtypeStruct((size, rows, wide), BF16),
            jax.ShapeDtypeStruct((size, rows, wide), BF16),
        ),
        in_specs=[in_vmem()] * 4,
        out_specs=(in_vmem(), in_any(), in_any(), in_any()),
        scratch_shapes=[
            pltpu.VMEM((size, rows + META, width), BF16),
            pltpu.VMEM((size, rows, wide), BF16),
            pltpu.VMEM((size, rows, wide), BF16),
            pltpu.VMEM((rows, wide), BF16),
            pltpu.SemaphoreType.DMA((size, 3)),
        ]
        + group.scratch(rows, 0, width),
        compiler_params=pltpu.CompilerParams(
            collective_id=1, has_side_effects=True, vmem_limit_bytes=VMEM_LIMIT
        ),
        name="experts_forward",
    )(message, middle, up, down)


def experts_backward(grad, blocks, act, slope, up, down, size, experts, job):
    rows, width = grad.shape
    wide = up.shape[1]
    hid = wide // experts
    group = Group(size)

    def kernel(grad_ref, blocks_ref, act_ref, slope_ref, up_ref, down_ref, *rest):
        stages = []
        if job:
            job_refs, rest = rest[:3], rest[3:]
        (out_ref, tail_ref, up_out, down_out), rest = rest[:4], rest[4:]
        if job:
            stages = job.stages(job_refs, rest[:3], rest[-len(job.scratch_shapes) :])
            rest = rest[3 : -len(job.scratch_shapes)]
        slots, blocks, act, slope, weighed, scaled, pre, load_sem = rest[:8]
        scratch = rest[8:]

        def loads(slot):
            two = lax.rem(slot, 2)
            return (
                pltpu.make_async_copy(blocks_ref.at[slot], blocks.at[slot], load_sem.at[two, 0]),
                pltpu.make_async_copy(act_ref.at[slot], act.at[two], load_sem.at[two, 1]),
                pltpu.make_async_copy(slope_ref.at[slot], slope.at[two], load_sem.at[two, 2]),
            )

        for load in loads(0):
            load.start()
        job.greet() if job else greet(group.peers())
        slots[0] = grad_ref[...]
        lane = lax.broadcasted_iota(jnp.int32, (16, wide), 1) // hid
        pick = (lane == lax.broadcasted_iota(jnp.int32, (16, wide), 0)).astype(F32).astype(BF16)

        def compute(slot):
            two = lax.rem(slot, 2)

            @pl.when(slot + 1 < size)
            def _():
                for load in loads(slot + 1):
                    load.start()

            for load in loads(slot):
                load.wait()
            gates = jnp.transpose(join_rows(blocks[slot, rows:]))[:rows]
            place = pl.ds(pl.multiple_of(slot * rows, 16), rows)
            for expert in range(experts):
                cols = slice(expert * hid, (expert + 1) * hid)
                gate = gates[:, expert : expert + 1]
                pull = dot(slots[slot], down_ref[cols, :], ((1,), (1,)))
                value = act[two, :, cols].astype(F32)
                weighed[:, cols] = (pull * value).astype(BF16)
                scaled[place, cols] = (value * gate).astype(BF16)
                pre[place, cols] = (pull * gate * slope[two, :, cols].astype(F32)).astype(BF16)
            for at, stage in enumerate(stages[:-1]):
                pl.when(slot == at)(stage)
            by_expert = dot(pick, weighed[...], ((1,), (1,)))[:8]
            if rows < width:
                by_expert = jnp.concatenate([by_expert, jnp.zeros((8, width - rows), F32)], 1)
            return dot(pre[place, :], up_ref[...], ((1,), (1,))), by_expert

        group.run(slots, scratch, rows, 16, compute)

        for expert in range(experts):
            cols = slice(expert * hid, (expert + 1) * hid)
            up_sum = jnp.zeros((width, hid), F32)
            down_sum = jnp.zeros((hid, width), F32)

            def add(slot, sums):
                place = pl.ds(pl.multiple_of(slot * rows, 16), rows)
                return (
                    sums[0] + dot(blocks[slot, :rows], pre[place, cols], ((0,), (0,))),
                    sums[1] + dot(scaled[place, cols], slots[slot], ((0,), (0,))),
                )

            up_sum, down_sum = lax.fori_loop(0, size, add, (up_sum, down_sum))
            up_out[:, cols] = up_sum.astype(BF16)
            down_out[cols, :] = down_sum.astype(BF16)

        group.collect(scratch, slots, rows, 16)
        out_ref[...] = scratch[0][0]
        tail_ref[...] = scratch[1][0, :8]
        if job:
            stages[-1]()

    return pl.pallas_call(
        kernel,
        out_shape=(
            jax.ShapeDtypeStruct((rows, width), F32),
            jax.ShapeDtypeStruct((8, width), F32),
            jax.ShapeDtypeStruct((width, wide), BF16),
            jax.ShapeDtypeStruct((wide, width), BF16),
        )
        + (job.out_shape if job else ()),
        in_specs=[in_vmem(), in_any(), in_any(), in_any(), in_vmem(), in_vmem()]
        + ([in_vmem()] * 3 if job else []),
        out_specs=(in_vmem(),) * 4 + ((in_any(),) * 3 if job else ()),
        scratch_shapes=[
            pltpu.VMEM((size, rows, width), BF16),
            pltpu.VMEM((size, rows + META, width), BF16),
            pltpu.VMEM((2, rows, wide), BF16),
            pltpu.VMEM((2, rows, wide), BF16),
            pltpu.VMEM((rows, wide), BF16),
            pltpu.VMEM((size * rows, wide), BF16),
            pltpu.VMEM((size * rows, wide), BF16),
            pltpu.SemaphoreType.DMA((2, 3)),
        ]
        + group.scratch(rows, 16, width)
        + (job.scratch_shapes if job else []),
        compiler_params=pltpu.CompilerParams(
            collective_id=4 if job else 2, has_side_effects=True, vmem_limit_bytes=VMEM_LIMIT
        ),
        name="experts_backward_and_sums" if job else "experts_backward",
    )(grad, blocks, act, slope, up, down, *(job.args if job else ()))


class LineSums:
    PAIRS = (("down", 0), ("down", 1), ("up", 0), ("up", 1), ("dense", 0))

    def __init__(self, dp, up, down, dense):
        self.dp = dp
        self.args = (up, down, dense)
        self.chunk = {
            "up": (dp,) + up.shape[2:],
            "down": down.shape[1:],
            "dense": (dense.shape[2] // 2, dense.shape[3]),
        }
        self.half = {"up": 2, "down": 2, "dense": 1}
        chips = dp // 2
        whole = dense.shape[2:]
        self.out_shape = tuple(
            jax.ShapeDtypeStruct((2 * self.half[kind],) + self.chunk[kind], BF16)
            for kind in ("up", "down", "dense")
        )
        self.boxes = []
        for kind in ("up", "down", "dense"):
            half, chunk = self.half[kind], self.chunk[kind]
            self.boxes += [
                pltpu.VMEM((2 * half,) + chunk, BF16),
                pltpu.VMEM((half,) + chunk, BF16),
                pltpu.VMEM((half,) + chunk, BF16),
                pltpu.VMEM((2 * half,) + chunk, BF16),
                pltpu.SemaphoreType.DMA((2, 2 * half)),
                pltpu.SemaphoreType.DMA((2, half)),
                pltpu.SemaphoreType.DMA((2, 2 * half)),
                pltpu.SemaphoreType.DMA((half,)),
            ]
        self.scratch_shapes = self.boxes + [
            pltpu.VMEM((2,) + self.chunk["up"], BF16),
            pltpu.SemaphoreType.DMA((2, 2, dp)),
            pltpu.VMEM((chips,) + whole, BF16),
            pltpu.VMEM((chips,) + whole, BF16),
            pltpu.VMEM((chips,) + whole, BF16),
            pltpu.VMEM((2,) + self.chunk["dense"], BF16),
            pltpu.SemaphoreType.DMA((2,)),
            pltpu.SemaphoreType.DMA((2, chips)),
            pltpu.SemaphoreType.DMA((3,)),
        ]

    def greet(self):
        me, mine = lax.axis_index("dp"), lax.axis_index("seq")
        barrier = pltpu.get_barrier_semaphore()
        middle = (mine == 1) | (mine == 2)
        for r in range(1, self.dp):
            pl.semaphore_signal(barrier, inc=1, device_id={"dp": me ^ r}, device_id_type=MESH)
        pl.semaphore_signal(
            barrier, inc=1, device_id={"seq": jnp.where(middle, 3 - mine, 1 + mine // 2)}, device_id_type=MESH
        )

        @pl.when(middle)
        def _():
            pl.semaphore_signal(barrier, inc=1, device_id={"seq": 3 * (mine - 1)}, device_id_type=MESH)
            pl.semaphore_wait(barrier, self.dp + 1)

        @pl.when(jnp.logical_not(middle))
        def _():
            pl.semaphore_wait(barrier, self.dp)

    def stages(self, refs, outs, scratch):
        kinds = ("up", "down", "dense")
        boxes = {kind: scratch[8 * at : 8 * at + 8] for at, kind in enumerate(kinds)}
        up_mine, up_sem, near_got, near, far_got, dense_mine, near_sem, far_sem, out_sem = scratch[24:]
        up, down, dense = refs
        me, mine = lax.axis_index("dp"), lax.axis_index("seq")
        core = lax.rem(me, 2)
        next_core = {"dp": me ^ 1}
        middle = (mine == 1) | (mine == 2)
        at_end = jnp.logical_not(middle)
        inner = {"seq": jnp.where(middle, 3 - mine, 1 + mine // 2)}
        outer = {"seq": jnp.where(middle, 3 * (mine - 1), mine)}
        owned = jnp.where(mine == 2, 1, 0)
        chips = range(1, self.dp // 2)
        spans = range(1, self.dp)

        def source(kind, c):
            return {"up": lambda: up.at[:, c], "down": lambda: down.at[c], "dense": lambda: dense_mine.at[c]}[
                kind
            ]()

        def inward(kind, c):
            box, sem = boxes[kind][0], boxes[kind][4]
            return remote(source(kind, c), box.at[c], sem.at[0, c], sem.at[1, c], inner)

        def across(kind, p):
            sem = boxes[kind][5]
            return remote(boxes[kind][2].at[p], boxes[kind][1].at[p], sem.at[0, p], sem.at[1, p], inner)

        def outward(kind, c):
            box, sem = boxes[kind][3], boxes[kind][6]
            return remote(box.at[c], box.at[c], sem.at[0, c], sem.at[1, c], outer)

        def between(kind, c, p):
            box = boxes[kind][3]
            return remote(box.at[c], box.at[c], boxes[kind][7].at[p], boxes[kind][6].at[1, c], inner)

        def span(p, c, r):
            return remote(
                up_mine.at[p, me ^ r], boxes["up"][3].at[c, me], up_sem.at[0, p, r], up_sem.at[1, p, r],
                {"dp": me ^ r},
            )

        def near_copy():
            return remote(dense.at[:, 1 - core], near_got, near_sem.at[0], near_sem.at[1], next_core)

        def far(m):
            return remote(
                near.at[(me // 2) ^ m], far_got.at[m], far_sem.at[0, m], far_sem.at[1, m], {"dp": me ^ (2 * m)}
            )

        def chunk_of(kind, p, own):
            side = owned if own else 1 - owned
            return p + side * self.half[kind]

        def begin():
            near_copy().start()

            @pl.when(at_end)
            def _():
                for kind, p in self.PAIRS[:-1]:
                    inward(kind, p).start()
                    inward(kind, p + self.half[kind]).start()

        def near_sum():
            near_copy().wait_recv()
            for at in range(self.dp // 2):
                near[at] = (dense[at, core].astype(F32) + near_got[at].astype(F32)).astype(BF16)
            for m in chips:
                far(m).start()

        def far_sum():
            for m in chips:
                far(m).wait_recv()
            rows = self.chunk["dense"][0]
            for at in range(2):
                place = slice(at * rows, (at + 1) * rows)
                total = near[me // 2, place].astype(F32)
                for m in chips:
                    total += far_got[m, place].astype(F32)
                dense_mine[at] = total.astype(BF16)

            @pl.when(at_end)
            def _():
                inward("dense", 0).start()
                inward("dense", 1).start()

        def relay(kind, p):
            @pl.when(middle)
            def _():
                c = chunk_of(kind, p, False)
                inward(kind, c).wait_recv()
                boxes[kind][2][p] = (source(kind, c)[...].astype(F32) + boxes[kind][0][c].astype(F32)).astype(BF16)
                across(kind, p).start()

        def total(kind, p):
            @pl.when(middle)
            def _():
                c = chunk_of(kind, p, True)
                inward(kind, c).wait_recv()
                across(kind, p).wait_recv()
                whole = (
                    source(kind, c)[...].astype(F32)
                    + boxes[kind][0][c].astype(F32)
                    + boxes[kind][1][p].astype(F32)
                ).astype(BF16)
                if kind == "up":
                    up_mine[p] = whole
                    boxes[kind][3][c, me] = up_mine[p, me]
                    for r in spans:
                        span(p, c, r).start()
                else:
                    boxes[kind][3][c] = whole
                    between(kind, c, p).start()
                    outward(kind, c).start()

        def turn(p):
            @pl.when(middle)
            def _():
                c = chunk_of("up", p, True)
                for r in spans:
                    span(p, c, r).wait_recv()
                between("up", c, p).start()
                outward("up", c).start()

        def forward(kind, p):
            @pl.when(middle)
            def _():
                c = chunk_of(kind, p, False)
                outward(kind, c).wait_recv()
                outward(kind, c).start()

        def finish():
            @pl.when(at_end)
            def _():
                for kind, p in self.PAIRS:
                    outward(kind, p).wait_recv()
                    outward(kind, p + self.half[kind]).wait_recv()
                    inward(kind, p).wait_send()
                    inward(kind, p + self.half[kind]).wait_send()

            copies = [
                pltpu.make_async_copy(boxes[kind][3], outs[at], out_sem.at[at]) for at, kind in enumerate(kinds)
            ]
            for copy in copies:
                copy.start()

            @pl.when(middle)
            def _():
                for kind, p in self.PAIRS:
                    across(kind, p).wait_send()
                    between(kind, chunk_of(kind, p, True), p).wait_send()
                    outward(kind, p).wait_send()
                    outward(kind, p + self.half[kind]).wait_send()
                    if kind == "up":
                        for r in spans:
                            span(p, chunk_of(kind, p, True), r).wait_send()

            near_copy().wait_send()
            for m in chips:
                far(m).wait_send()
            for copy in copies:
                copy.wait()

        def both(*parts):
            def stage():
                for part, *of in parts:
                    part(*of)

            return stage

        return [
            begin,
            both((near_sum,), (relay, "down", 0)),
            both((total, "down", 0), (far_sum,)),
            both((relay, "down", 1), (forward, "down", 0)),
            both((total, "down", 1), (relay, "up", 0)),
            both((total, "up", 0), (forward, "down", 1)),
            both((relay, "up", 1), (turn, 0)),
            both(
                (total, "up", 1), (forward, "up", 0), (relay, "dense", 0), (turn, 1), (total, "dense", 0),
                (forward, "up", 1), (forward, "dense", 0), (finish,),
            ),
        ]


def sum_weights(job):
    def kernel(*refs):
        job.greet()
        for stage in job.stages(refs[:3], refs[3:6], refs[6:]):
            stage()

    return pl.pallas_call(
        kernel,
        out_shape=job.out_shape,
        in_specs=[in_vmem()] * 3,
        out_specs=(in_any(),) * 3,
        scratch_shapes=job.scratch_shapes,
        compiler_params=pltpu.CompilerParams(
            collective_id=3, has_side_effects=True, vmem_limit_bytes=VMEM_LIMIT
        ),
        name="sum_weights",
    )(*job.args)


def sum_weights_plainly(dp, up, down, dense):
    dense = lax.psum_scatter(dense.reshape(dp, -1, dense.shape[-1]), "dp", scatter_dimension=0, tiled=True)
    up = lax.all_to_all(up, "dp", split_axis=0, concat_axis=0, tiled=True)
    return [lax.psum(jnp.swapaxes(up, 0, 1), "seq"), lax.psum(down, "seq"), lax.psum(dense, "seq")]


NT = ((1,), (1,))
TN = ((0,), (0,))


def row_sums(values):
    return jnp.sum(values, 0, keepdims=True)


def pad_lanes(values, lanes):
    if values.shape[1] == lanes:
        return values
    return jnp.concatenate([values, jnp.zeros((values.shape[0], lanes - values.shape[1]), values.dtype)], 1)


def one_head(pair, parity):
    lane = lax.broadcasted_iota(jnp.int32, pair.shape, 1) // HEAD
    return jnp.where(lane == parity, pair.astype(F32), 0.0).astype(BF16)


class Keys:
    def __init__(self, share):
        self.share = share

    def peers(self):
        me = lax.axis_index("dp")
        return [{"dp": me ^ k} for k in range(1, self.share)]


def attention_forward(state, proj_packed, proj_out, vectors, router, chosen, length, share):
    rows, width = state.shape
    keys_len = rows * share
    heads = width // HEAD
    experts = 4
    keys = Keys(share)

    def kernel(
        state_ref, packed_ref, out_w_ref, vec_ref, router_ref, chosen_ref, length_ref,
        message, middle, queries, kv, log_total, mixed, gates_ref,
        all_kv, values_t, send, recv, save,
    ):
        me = lax.axis_index("dp")
        part = lax.rem(me, share)
        unit, _ = normalize(state_ref[...])
        normed = (unit * vec_ref[0:1] + vec_ref[1:2]).astype(BF16)
        all_kv[part] = dot(normed, packed_ref[:, width:]).astype(BF16)
        greet(keys.peers())
        copies = [
            remote(all_kv.at[part], all_kv.at[part], send.at[k], recv.at[k], {"dp": me ^ k})
            for k in range(1, share)
        ]
        for copy in copies:
            copy.start()
        queries[...] = (dot(normed, packed_ref[:, :width]) * HEAD ** (-0.5)).astype(BF16)
        for copy in copies:
            copy.wait()
        saving = pltpu.make_async_copy(all_kv, kv, save)
        saving.start()
        for at in range(share):
            values_t[:, at * rows : (at + 1) * rows] = jnp.transpose(
                all_kv[at, :, width:].astype(F32)
            ).astype(BF16)
        valid = lax.broadcasted_iota(jnp.int32, (keys_len, rows), 0) < length_ref[0]

        def pair_of_heads(pair, carry):
            lanes = pl.ds(pl.multiple_of(pair * 128, 128), 128)
            keys_pair = all_kv[:, :, lanes].reshape(keys_len, 128)
            queries_pair = queries[:, lanes]
            for parity in range(2):
                head = 2 * pair + parity
                scores = dot(keys_pair, one_head(queries_pair, parity), NT)
                scores = jnp.where(valid, scores, NEG)
                highest = jnp.max(scores, 0, keepdims=True)
                expo = jnp.exp(scores - highest)
                totals = row_sums(expo)
                log_total[head] = highest + jnp.log(totals)
                place = pl.ds(pl.multiple_of(head * HEAD, HEAD), HEAD)
                mixed[place, :] = (dot(values_t[place, :], expo.astype(BF16)) / totals).astype(BF16)
            return carry

        lax.fori_loop(0, heads // 2, pair_of_heads, 0)
        middle[...] = state_ref[...] + dot(mixed[...], out_w_ref[...], TN)
        unit, _ = normalize(middle[...])
        normed = (unit * vec_ref[2:3] + vec_ref[3:4]).astype(BF16)
        message[:rows] = normed
        logits = dot(router_ref[...], normed, NT)[:8]
        row = lax.broadcasted_iota(jnp.int32, logits.shape, 0)
        logits = jnp.where(row < experts, logits, NEG)
        expo = jnp.exp(logits - jnp.max(logits, 0, keepdims=True))
        gates = expo / row_sums(expo)
        gates_ref[...] = gates
        message[rows:] = split_rows(pad_lanes(gates * chosen_ref[...], width))
        saving.wait()

    return pl.pallas_call(
        kernel,
        out_shape=(
            jax.ShapeDtypeStruct((rows + META, width), BF16),
            jax.ShapeDtypeStruct((rows, width), F32),
            jax.ShapeDtypeStruct((rows, width), BF16),
            jax.ShapeDtypeStruct((share, rows, 2 * width), BF16),
            jax.ShapeDtypeStruct((heads, 1, rows), F32),
            jax.ShapeDtypeStruct((width, rows), BF16),
            jax.ShapeDtypeStruct((8, rows), F32),
        ),
        in_specs=[in_vmem()] * 6 + [pl.BlockSpec(memory_space=pltpu.SMEM)],
        out_specs=(in_vmem(),) * 3 + (in_any(),) + (in_vmem(),) * 3,
        scratch_shapes=[
            pltpu.VMEM((share, rows, 2 * width), BF16),
            pltpu.VMEM((width, keys_len), BF16),
            pltpu.SemaphoreType.DMA((share,)),
            pltpu.SemaphoreType.DMA((share,)),
            pltpu.SemaphoreType.DMA,
        ],
        compiler_params=pltpu.CompilerParams(
            collective_id=5, has_side_effects=True, vmem_limit_bytes=VMEM_LIMIT
        ),
        name="attention_forward",
    )(state, proj_packed, proj_out, vectors, router, chosen, length)


def attention_backward(
    grad, back, back_tail, state, middle, message, gates, chosen, queries, kv, log_total, mixed,
    proj_packed, proj_out, vectors, router, length, share,
):
    rows, width = state.shape
    keys_len = rows * share
    heads = width // HEAD
    columns = 4 * width + 128
    keys = Keys(share)

    def kernel(
        grad_ref, back_ref, tail_ref, state_ref, mid_ref, msg_ref, gates_ref, chosen_ref, queries, kv,
        log_total, mixed, packed_ref, out_w_ref, vec_ref, router_ref, length_ref,
        new_ref, new_low_ref, dense,
        keys_t, normed_ref, grad_mid, grad_heads, grad_q, kv_grads, kv_got, grad_packed, send, recv,
    ):
        me = lax.axis_index("dp")
        part = lax.rem(me, share)
        gates = gates_ref[...]
        grad_gates = tail_ref[:, :rows] * chosen_ref[...]
        grad_logits = split_rows(gates * (grad_gates - row_sums(gates * grad_gates)))
        twice = jnp.concatenate([router_ref[:8].astype(F32)] * 2, 0).astype(BF16)
        grad_normed = back_ref[...] + dot(grad_logits, twice, TN)
        router_grad = dot(grad_logits, msg_ref[:rows])
        router_grad = router_grad[:8] + router_grad[8:]
        unit, inverse = normalize(mid_ref[...])
        gain_two = row_sums(grad_normed * unit)
        bias_two = row_sums(grad_normed)
        grad_mid[...] = grad_ref[...] + norm_back(grad_normed * vec_ref[2:3], unit, inverse)
        low = grad_mid[...].astype(BF16)
        dense[:, 3 * width : 4 * width] = dot(mixed[...], low).astype(BF16)
        grad_heads[...] = dot(low, out_w_ref[...], NT).astype(BF16)
        for at in range(share):
            keys_t[:, at * rows : (at + 1) * rows] = jnp.transpose(kv[at, :, :width].astype(F32)).astype(BF16)
        valid = lax.broadcasted_iota(jnp.int32, (keys_len, rows), 0) < length_ref[0]

        def pair_of_heads(pair, carry):
            lanes = pl.ds(pl.multiple_of(pair * 128, 128), 128)
            value_lanes = pl.ds(pl.multiple_of(width + pair * 128, 128), 128)
            keys_pair = kv[:, :, lanes].reshape(keys_len, 128)
            values_pair = kv[:, :, value_lanes].reshape(keys_len, 128)
            grad_k = jnp.zeros((keys_len, 128), F32)
            grad_v = jnp.zeros((keys_len, 128), F32)
            for parity in range(2):
                head = 2 * pair + parity
                query = one_head(queries[:, lanes], parity)
                pull = one_head(grad_heads[:, lanes], parity)
                scores = dot(keys_pair, query, NT)
                probs = jnp.where(valid, jnp.exp(scores - log_total[head]), 0.0)
                grad_probs = dot(values_pair, pull, NT)
                grad_scores = probs * (grad_probs - row_sums(probs * grad_probs))
                grad_scores = grad_scores.astype(BF16)
                grad_v += dot(probs.astype(BF16), pull)
                grad_k += dot(grad_scores, query)
                place = pl.ds(pl.multiple_of(head * HEAD, HEAD), HEAD)
                grad_q[place, :] = dot(keys_t[place, :], grad_scores) * HEAD ** (-0.5)
            kv_grads[:, :, lanes] = grad_k.astype(BF16).reshape(share, rows, 128)
            kv_grads[:, :, value_lanes] = grad_v.astype(BF16).reshape(share, rows, 128)
            return carry

        lax.fori_loop(0, heads // 2, pair_of_heads, 0)
        greet(keys.peers())
        copies = [
            remote(kv_grads.at[part ^ k], kv_got.at[k], send.at[k], recv.at[k], {"dp": me ^ k})
            for k in range(1, share)
        ]
        for copy in copies:
            copy.start()
        unit, inverse = normalize(state_ref[...])
        normed_ref[...] = (unit * vec_ref[0:1] + vec_ref[1:2]).astype(BF16)
        grad_packed[:, :width] = jnp.transpose(grad_q[...]).astype(BF16)
        for copy in copies:
            copy.wait()
        total = kv_grads[part].astype(F32)
        for k in range(1, share):
            total += kv_got[k].astype(F32)
        grad_packed[:, width:] = total.astype(BF16)
        grad_normed = dot(grad_packed[...], packed_ref[...], NT)
        for block in range(3):
            cols = slice(block * width, (block + 1) * width)
            dense[:, cols] = dot(normed_ref[...], grad_packed[:, cols], TN).astype(BF16)
        gain_one = row_sums(grad_normed * unit)
        bias_one = row_sums(grad_normed)
        new = grad_mid[...] + norm_back(grad_normed * vec_ref[0:1], unit, inverse)
        new_ref[...] = new
        new_low_ref[...] = new.astype(BF16)
        tail = jnp.concatenate([gain_one, bias_one, gain_two, bias_two, router_grad[:4]], 0)
        dense[:, 4 * width :] = pad_lanes(jnp.transpose(tail), 128).astype(BF16)

    return pl.pallas_call(
        kernel,
        out_shape=(
            jax.ShapeDtypeStruct((rows, width), F32),
            jax.ShapeDtypeStruct((rows, width), BF16),
            jax.ShapeDtypeStruct((width, columns), BF16),
        ),
        in_specs=[in_vmem()] * 16 + [pl.BlockSpec(memory_space=pltpu.SMEM)],
        out_specs=(in_vmem(),) * 3,
        scratch_shapes=[
            pltpu.VMEM((width, keys_len), BF16),
            pltpu.VMEM((rows, width), BF16),
            pltpu.VMEM((rows, width), F32),
            pltpu.VMEM((rows, width), BF16),
            pltpu.VMEM((width, rows), F32),
            pltpu.VMEM((share, rows, 2 * width), BF16),
            pltpu.VMEM((share, rows, 2 * width), BF16),
            pltpu.VMEM((rows, 3 * width), BF16),
            pltpu.SemaphoreType.DMA((share,)),
            pltpu.SemaphoreType.DMA((share,)),
        ],
        compiler_params=pltpu.CompilerParams(
            collective_id=6, has_side_effects=True, vmem_limit_bytes=VMEM_LIMIT
        ),
        name="attention_backward",
    )(
        grad, back, back_tail, state, middle, message, gates, chosen, queries, kv, log_total, mixed,
        proj_packed, proj_out, vectors, router, length,
    )


class Plan:
    def __init__(self, mesh, images, length):
        self.dp = mesh.shape["dp"]
        self.seq = mesh.shape["seq"]
        self.images = images
        self.piece = length // self.seq
        self.share = self.seq // images
        self.rows = images * self.piece
        self.groups = [
            [block * self.share + part for part in range(self.share)]
            for block in range(self.dp // self.share)
        ]

    def hops(self, turn):
        pairs = []
        for dp in range(self.dp):
            for seq in range(self.seq):
                local = (seq % self.images + turn) % self.images
                to_dp = dp // self.share * self.share + seq // self.images
                to_seq = dp % self.share * self.images + local
                pairs.append((dp * self.seq + seq, to_dp * self.seq + to_seq))
        return pairs

    def to_images(self, pieces):
        seq = lax.axis_index("seq") % self.images
        got = []
        for turn in range(self.images):
            piece = lax.dynamic_index_in_dim(pieces, (seq + turn) % self.images, 0, False)
            got.append(lax.ppermute(piece, ("dp", "seq"), self.hops(turn)))
        got = jnp.stack(got)
        return jnp.stack(
            [
                lax.dynamic_index_in_dim(got, (seq - slot) % self.images, 0, False)
                for slot in range(self.images)
            ]
        )

    def to_pieces(self, slots):
        seq = lax.axis_index("seq") % self.images
        got = []
        for turn in range(self.images):
            slot = lax.dynamic_index_in_dim(slots, (seq - turn) % self.images, 0, False)
            back = [(to, source) for source, to in self.hops(turn)]
            got.append(lax.ppermute(slot, ("dp", "seq"), back))
        got = jnp.stack(got)
        return jnp.stack(
            [
                lax.dynamic_index_in_dim(got, (local - seq) % self.images, 0, False)
                for local in range(self.images)
            ]
        )


def build(mesh):
    def shards(
        tokens,
        cotangent,
        routes,
        token_mask,
        ln1_gain,
        ln1_bias,
        qkv_weight,
        out_weight,
        ln2_gain,
        ln2_bias,
        router_weight,
        expert_in,
        expert_out,
    ):
        images, piece, width = tokens.shape
        levels, experts = expert_in.shape[:2]
        length_all = token_mask.shape[1]
        plan = Plan(mesh, images, length_all)
        rows = plan.rows
        slice_hid = expert_out.shape[2]
        wide = experts * slice_hid
        part = lax.axis_index("dp") % plan.share

        start = lax.axis_index("seq") * piece
        local_valid = lax.dynamic_slice_in_dim(token_mask, start, piece, 1)
        chosen_all = jnp.sum(
            (routes[..., None] == jnp.arange(experts, dtype=jnp.int32)).astype(F32), -2
        )
        chosen_rows = jnp.transpose(chosen_all, (1, 0, 3, 2)).reshape(images, levels * experts, piece)
        lengths = jnp.sum(token_mask, -1)
        meta = jnp.zeros((images, META, width), F32)
        meta = meta.at[:, : levels * experts, :piece].set(chosen_rows)
        meta = meta.at[:, levels * experts, 0].set((lengths // 4).astype(F32))
        meta = meta.at[:, levels * experts + 1, 0].set((lengths % 4).astype(F32))
        masked = cotangent * local_valid[..., None].astype(BF16)
        slots = plan.to_images(jnp.concatenate([tokens, meta.astype(BF16), masked], 1))
        state = slots[:, :piece].reshape(rows, width).astype(F32)
        grad = slots[:, piece + META :].reshape(rows, width).astype(F32)
        meta = slots[:, piece : piece + META].astype(F32)
        chosen_in = jnp.transpose(meta[:, : levels * experts, :piece], (1, 0, 2))
        chosen_in = chosen_in.reshape(levels, experts, rows)
        chosen_in = jnp.pad(chosen_in, ((0, 0), (0, 8 - experts), (0, 0)))
        length = meta[0, levels * experts, 0] * 4.0 + meta[0, levels * experts + 1, 0]
        length = length.astype(jnp.int32).reshape(1)

        vectors = jnp.stack([ln1_gain, ln1_bias, ln2_gain, ln2_bias], -1)
        dense = lax.all_gather(
            jnp.concatenate([qkv_weight, out_weight, vectors, router_weight], -1),
            "dp",
            axis=1,
            tiled=True,
        )
        proj_packed_all = dense[..., : 3 * width]
        proj_out_all = dense[..., 3 * width : 4 * width]
        tails = jnp.swapaxes(dense[..., 4 * width : 4 * width + 8], 1, 2)
        vectors = tails[:, :4].astype(F32)
        router_all = jnp.pad(tails[:, 4 : 4 + experts], ((0, 0), (0, 16 - experts), (0, 0)))
        up_all = lax.all_to_all(expert_in, "dp", split_axis=3, concat_axis=2, tiled=True)
        up_all = jnp.swapaxes(up_all, 1, 2).reshape(levels, width, wide)
        down_all = expert_out.reshape(levels, wide, width)

        saved = []
        for level in range(levels):
            weights = (proj_packed_all[level], proj_out_all[level], vectors[level], router_all[level])
            message, middle, queries, kv, log_total, mixed, gates = attention_forward(
                state, *weights, chosen_in[level], length, plan.share
            )
            new_state, blocks, act, slope = experts_forward(
                message, middle, up_all[level], down_all[level], plan.dp, experts
            )
            attended = (
                state, middle, message, gates, chosen_in[level], queries, kv, log_total, mixed
            ) + weights
            saved.append((attended, (blocks, act, slope)))
            state = new_state
        output = plan.to_pieces(state.astype(BF16).reshape(images, piece, width))

        grads = [None] * levels
        job = None
        grad_low = grad.astype(BF16)
        for level in reversed(range(levels)):
            attended, routed = saved[level]
            back, back_tail, up_grad, down_grad, *sums = experts_backward(
                grad_low, *routed, up_all[level], down_all[level], plan.dp, experts, job
            )
            if job:
                grads[level + 1] = sums
            grad, grad_low, dense_grad = attention_backward(
                grad, back, back_tail, *attended, length, plan.share
            )
            strip = width // plan.dp // 4
            weight_grads = (
                up_grad.reshape(plan.dp, 4, strip, wide),
                down_grad.reshape(4, wide // 4, width),
                dense_grad.reshape(plan.dp // 2, 2, width // plan.dp, -1),
            )
            if plan.seq == 4:
                job = LineSums(plan.dp, *weight_grads)
            else:
                grads[level] = sum_weights_plainly(plan.dp, *weight_grads)
        if job:
            grads[0] = sum_weights(job)
        token_grad = plan.to_pieces(grad_low.reshape(images, piece, width)).astype(F32)
        up_grad, down_grad, dense_grad = (jnp.stack(items).astype(F32) for items in zip(*grads))
        up_grad = up_grad.reshape(levels, 4, plan.dp, strip, experts, slice_hid)
        up_grad = jnp.transpose(up_grad, (0, 4, 1, 3, 2, 5)).reshape(expert_in.shape)
        down_grad = down_grad.reshape(expert_out.shape)
        dense_grad = dense_grad.reshape(levels, width // plan.dp, -1)
        vector_grads = dense_grad[..., 4 * width : 4 * width + 4]
        return (
            output,
            token_grad,
            vector_grads[..., 0],
            vector_grads[..., 1],
            dense_grad[..., : 3 * width],
            dense_grad[..., 3 * width : 4 * width],
            vector_grads[..., 2],
            vector_grads[..., 3],
            dense_grad[..., 4 * width + 4 : 4 * width + 4 + experts],
            up_grad,
            down_grad,
        )

    return shards


def solution(mesh):
    return jax.shard_map(
        build(mesh),
        mesh=mesh,
        in_specs=(
            P("dp", "seq", None),
            P("dp", "seq", None),
            P(None, "dp", "seq", None),
            P("dp", None),
            P(None, "dp"),
            P(None, "dp"),
            P(None, "dp", None),
            P(None, "dp", None),
            P(None, "dp"),
            P(None, "dp"),
            P(None, "dp", None),
            P(None, None, "dp", None),
            P(None, None, "dp", None),
        ),
        out_specs=(
            P("dp", "seq", None),
            P("dp", "seq", None),
            P(None, "dp"),
            P(None, "dp"),
            P(None, "dp", None),
            P(None, "dp", None),
            P(None, "dp"),
            P(None, "dp"),
            P(None, "dp", None),
            P(None, None, "dp", None),
            P(None, None, "dp", None),
        ),
        check_vma=False,
    )
```

```python
import jax
import jax.numpy as jnp
from jax import lax
from jax.experimental import pallas as pl
from jax.experimental.pallas import tpu as pltpu
from jax.sharding import PartitionSpec as P

HEAD = 64
EPS = 1e-06
NEG = -1e30
F32 = jnp.float32
BF16 = jnp.bfloat16
MESH = pl.DeviceIdType.MESH
VMEM_LIMIT = 60 * 1024 * 1024
NT = ((1,), (1,))
TN = ((0,), (0,))


def normalize(values):
    center = values - jnp.mean(values, -1, keepdims=True)
    inverse = lax.rsqrt(jnp.mean(center * center, -1, keepdims=True) + EPS)
    return center * inverse, inverse


def norm_back(grad_unit, unit, inverse):
    return inverse * (
        grad_unit
        - jnp.mean(grad_unit, -1, keepdims=True)
        - unit * jnp.mean(grad_unit * unit, -1, keepdims=True)
    )


def in_vmem():
    return pl.BlockSpec(memory_space=pltpu.VMEM)


def in_any():
    return pl.BlockSpec(memory_space=pl.ANY)


def greet(*peers):
    barrier = pltpu.get_barrier_semaphore()
    count = 0
    for peer, condition in peers:

        def signal(peer=peer):
            pl.semaphore_signal(barrier, inc=1, device_id=peer, device_id_type=MESH)

        if condition is None:
            signal()
            count += 1
        else:
            pl.when(condition)(signal)
            count += condition.astype(jnp.int32)
    pl.semaphore_wait(barrier, count)


def remote(src, dst, send, recv, peer):
    return pltpu.make_async_remote_copy(
        src_ref=src, dst_ref=dst, send_sem=send, recv_sem=recv, device_id=peer, device_id_type=MESH
    )


def split_rows(rows8):
    high = rows8.astype(BF16).astype(F32)
    return jnp.concatenate([high, rows8 - high], 0).astype(BF16)


def join_rows(rows16):
    wide = rows16.astype(F32)
    return wide[:8] + wide[8:]


def gelu_parts(u):
    bell = jnp.exp2(u * u * -0.7213475204444817)
    t = pl.reciprocal(1.0 + 0.23164190 * jnp.abs(u), approx=True)
    poly = t * (
        0.127414796 + t * (-0.142248368 + t * (0.7107068705 + t * (-0.7265760135 + t * 0.5307027145)))
    )
    half = poly * bell
    cdf = jnp.where(u >= 0, 1.0 - half, half)
    return u * cdf, cdf + u * 0.3989422804014327 * bell


def dot(left, right, dims=((1,), (0,))):
    return lax.dot_general(left, right, (dims, ((), ())), preferred_element_type=F32)


def row_sums(values):
    return jnp.sum(values, 0, keepdims=True)


def pad_lanes(values, lanes):
    if values.shape[1] == lanes:
        return values
    return jnp.concatenate([values, jnp.zeros((values.shape[0], lanes - values.shape[1]), values.dtype)], 1)


def one_head(pair, parity):
    lane = lax.broadcasted_iota(jnp.int32, pair.shape, 1) // HEAD
    return jnp.where(lane == parity, pair.astype(F32), 0.0).astype(BF16)


def weight_rows(dense_ref):
    width = dense_ref.shape[0]
    return jnp.transpose(dense_ref[:, 4 * width :].astype(F32))


class Plan:
    def __init__(self, mesh, images, length):
        self.dp = mesh.shape["dp"]
        self.seq = mesh.shape["seq"]
        self.images = images
        self.piece = length // self.seq
        self.share = self.seq // images
        self.rows = images * self.piece


class Swap:
    def __init__(self, plan):
        self.plan = plan

    def where(self, k):
        me, mine = lax.axis_index("dp"), lax.axis_index("seq")
        share, images = self.plan.share, self.plan.images
        part = lax.rem(me, share)
        peer = {"dp": me - part + mine // images, "seq": part * images + k}
        stays = (part == mine // images) & (lax.rem(mine, images) == k)
        return peer, stays

    def peers(self):
        both = [self.where(k) for k in range(self.plan.images)]
        return [(peer, jnp.logical_not(stays)) for peer, stays in both]

    def start(self, src, dst, sems):
        slot = lax.rem(lax.axis_index("seq"), self.plan.images)
        for k in range(self.plan.images):
            peer, stays = self.where(k)

            @pl.when(jnp.logical_not(stays))
            def _():
                remote(src.at[k], dst.at[slot], sems.at[0, k], sems.at[1, slot], peer).start()

            @pl.when(stays)
            def _():
                pltpu.make_async_copy(src.at[k], dst.at[k], sems.at[1, k]).start()

    def wait(self, src, dst, sems):
        for k in range(self.plan.images):
            peer, stays = self.where(k)
            moved = remote(src.at[k], dst.at[k], sems.at[0, k], sems.at[1, k], peer)

            @pl.when(jnp.logical_not(stays))
            def _():
                moved.wait_recv()
                moved.wait_send()

            @pl.when(stays)
            def _():
                pltpu.make_async_copy(src.at[k], dst.at[k], sems.at[1, k]).wait()


class Slots:
    def __init__(self, ref):
        self.ref = ref
        self.rows = ref.shape[1]

    def at(self, slot, part, device):
        return self.ref.at[slot, part]


class Strips:
    def __init__(self, ref, rows):
        self.ref = ref
        self.rows = rows

    def at(self, slot, part, device):
        first = pl.multiple_of((device ^ slot) * self.rows + part.start, 16)
        return self.ref.at[pl.ds(first, part.size)]


class Spread:
    def __init__(self, size):
        self.size = size
        self.pairs = size // 2
        self.order = sorted(range(self.pairs), key=lambda pair: (bin(pair).count("1"), pair))
        self.bits = [1 << k for k in range(self.pairs.bit_length() - 1)]

    def ways(self, pair):
        return (pair & -pair, 1 << (pair.bit_length() - 1))

    def pair_at(self, turn):
        if isinstance(turn, int):
            return self.order[turn]
        pair = turn
        for at, value in enumerate(self.order):
            if at != value:
                pair = jnp.where(turn == at, value, pair)
        return pair

    def peers(self):
        me = lax.axis_index("dp")
        return [({"dp": me ^ r}, None) for r in (1, *range(2, self.size, 2))]

    def semaphores(self):
        return [
            pltpu.SemaphoreType.DMA((2, self.pairs)),
            pltpu.SemaphoreType.DMA((2, self.size)),
            pltpu.SemaphoreType.DMA((self.pairs,)),
        ]

    def bind(self, slots, semaphores):
        self.slots = slots
        self.send, self.recv, self.hand = semaphores
        self.me = lax.axis_index("dp")
        cut = slots.rows // 32 * 16
        self.whole = pl.ds(0, slots.rows)
        self.halves = (pl.ds(0, cut), pl.ds(cut, slots.rows - cut))

    def move(self, slot, to_slot, part, peer, send, recv):
        return remote(
            self.slots.at(slot, part, self.me), self.slots.at(to_slot, part, peer), send, recv, {"dp": peer}
        )

    def block(self, pair):
        slot = 2 * pair
        return self.move(0, slot, self.whole, self.me ^ slot, self.send.at[0, pair], self.recv.at[0, slot])

    def half_block(self, pair, half):
        way = self.ways(pair)[half]
        return self.move(
            2 * (pair ^ way), 2 * pair, self.halves[half], self.me ^ (2 * way),
            self.send.at[half, pair], self.recv.at[half, 2 * pair],
        )

    def handed(self, pair):
        slot = 2 * pair
        return self.move(
            slot, slot + 1, self.whole, self.me ^ 1, self.hand.at[pair], self.recv.at[0, slot + 1]
        )

    def start(self):
        self.handed(0).start()
        for bit in self.bits:
            self.block(bit).start()

    def arrive(self, pair):
        for known in range(1, self.pairs):

            @pl.when(jnp.asarray(pair) == known)
            def _():
                if known in self.bits:
                    self.block(known).wait_recv()
                else:
                    self.half_block(known, 0).wait_recv()
                    self.half_block(known, 1).wait_recv()
                for far in range(1, self.pairs):
                    for half, way in enumerate(self.ways(far)):
                        if far not in self.bits and far ^ way == known:
                            self.half_block(far, half).start()

        self.handed(pair).start()

    def drain(self):
        for pair in range(self.pairs):
            self.handed(pair).wait_send()
            if pair in self.bits:
                self.block(pair).wait_send()
            elif pair:
                self.half_block(pair, 0).wait_send()
                self.half_block(pair, 1).wait_send()


def bring_in(plan, tokens, facts, dense):
    images, piece, width = tokens.shape
    rows, size = plan.rows, plan.dp
    strip, columns = dense.shape
    levels = facts.shape[1] // 8 - 2
    swap = Swap(plan)
    spread = Spread(size)

    def kernel(
        tokens_ref, facts_ref, dense_ref, state, chosen, length, dense_out,
        tok, fact, dense_all, tok_sem, fact_sem, *sems,
    ):
        me = lax.axis_index("dp")
        dense_all[pl.ds(pl.multiple_of(me * strip, 16), strip)] = dense_ref[...]
        greet(*swap.peers(), *spread.peers())
        spread.bind(Strips(dense_all, strip), sems[:3])
        spread.start()
        swap.start(facts_ref, fact, fact_sem)
        swap.start(tokens_ref, tok, tok_sem)
        for pair in spread.order[1:]:
            spread.arrive(pair)
        swap.wait(facts_ref, fact, fact_sem)
        total = fact[0].astype(F32)
        for k in range(1, images):
            total += fact[k].astype(F32)
        for level in range(levels):
            chosen[level] = total[8 * level : 8 * level + 8]
        whole = total[8 * levels : 8 * levels + 1, :1] * 4.0 + total[8 * levels + 1 : 8 * levels + 2, :1]
        length[...] = jnp.broadcast_to(whole, length.shape)
        swap.wait(tokens_ref, tok, tok_sem)
        for k in range(images):
            state[k * piece : (k + 1) * piece] = tok[k].astype(F32)
        for pair in spread.order:
            spread.handed(pair).wait_recv()
        keep = pltpu.make_async_copy(dense_all, dense_out, sems[3])
        keep.start()
        spread.drain()
        keep.wait()

    swap_sem = pltpu.SemaphoreType.DMA((2, images))
    return pl.pallas_call(
        kernel,
        out_shape=(
            jax.ShapeDtypeStruct((rows, width), F32),
            jax.ShapeDtypeStruct((levels, 8, width), F32),
            jax.ShapeDtypeStruct((8, 128), F32),
            jax.ShapeDtypeStruct((size * strip, columns), BF16),
        ),
        in_specs=[in_vmem()] * 3,
        out_specs=(in_vmem(),) * 3 + (in_any(),),
        scratch_shapes=[
            pltpu.VMEM((images, piece, width), BF16),
            pltpu.VMEM(facts.shape, BF16),
            pltpu.VMEM((size * strip, columns), BF16),
            swap_sem,
            swap_sem,
        ]
        + spread.semaphores()
        + [pltpu.SemaphoreType.DMA],
        compiler_params=pltpu.CompilerParams(
            collective_id=7, has_side_effects=True, vmem_limit_bytes=VMEM_LIMIT
        ),
        name="bring_in",
    )(tokens, facts, dense)


class Group(Spread):
    def scratch(self, rows, tail, width):
        full = rows + tail
        return self.semaphores() + [
            pltpu.VMEM((self.pairs, rows, width), F32),
            pltpu.VMEM((self.pairs, 8, width), F32),
            pltpu.VMEM((self.pairs, full, width), BF16),
            pltpu.VMEM((self.pairs, full, width), BF16),
            pltpu.VMEM((self.pairs, full, width), BF16),
            pltpu.VMEM((self.pairs, full, width), BF16),
            pltpu.SemaphoreType.DMA((self.pairs,)),
            pltpu.SemaphoreType.DMA((self.pairs,)),
            pltpu.SemaphoreType.DMA((self.pairs,)),
            pltpu.SemaphoreType.DMA((self.pairs,)),
        ]

    def given(self, pair):
        return remote(
            self.give.at[pair], self.take.at[pair], self.g_send.at[pair], self.g_recv.at[pair], {"dp": self.me ^ 1}
        )

    def paid(self, pair):
        return remote(
            self.pay.at[pair], self.due.at[pair], self.p_send.at[pair], self.p_recv.at[pair],
            {"dp": self.me ^ (2 * pair)},
        )

    def run(self, slots, scratch, rows, tail, compute):
        self.bind(Slots(slots), scratch[:3])
        (
            self.own, self.own_tail, self.give, self.take, self.pay, self.due,
            self.g_send, self.g_recv, self.p_send, self.p_recv,
        ) = scratch[3:]
        self.sizes = rows, tail

        def settle(pair):
            self.given(pair).wait_recv()
            self.own[pair] += self.take[pair, :rows].astype(F32)
            if tail:
                self.own_tail[pair] += join_rows(self.take[pair, rows:])

            @pl.when(jnp.asarray(pair) > 0)
            def _():
                self.pay[pair, :rows] = self.own[pair].astype(BF16)
                if tail:
                    self.pay[pair, rows:] = split_rows(self.own_tail[pair])
                self.paid(pair).start()

        self.start()

        def step(at, carry):
            turn = at // 2
            pair = self.pair_at(turn)
            even = lax.rem(at, 2) == 0
            slot = 2 * pair + lax.rem(at, 2)

            @pl.when(even & (turn > 0))
            def _():
                self.arrive(pair)
                settle(self.pair_at(turn - 1))

            @pl.when(jnp.logical_not(even))
            def _():
                self.handed(pair).wait_recv()

            total, total_tail = compute(slot, at)

            @pl.when(even)
            def _():
                self.own[pair] = total
                if tail:
                    self.own_tail[pair] = total_tail

            @pl.when(jnp.logical_not(even))
            def _():
                self.give[pair, :rows] = total.astype(BF16)
                if tail:
                    self.give[pair, rows:] = split_rows(total_tail)
                self.given(pair).start()

            return carry

        lax.fori_loop(0, self.size, step, 0)
        settle(self.order[-1])

    def collect(self):
        rows, tail = self.sizes
        for pair in range(1, self.pairs):
            self.paid(pair).wait_recv()
            self.own[0] += self.due[pair, :rows].astype(F32)
            if tail:
                self.own_tail[0] += join_rows(self.due[pair, rows:])
        for pair in range(self.pairs):
            self.given(pair).wait_send()
            if pair:
                self.paid(pair).wait_send()
        self.drain()


def experts_forward(message, middle, up, down, size):
    rows, width = middle.shape
    experts, _, hid = up.shape
    wide = experts * hid
    group = Group(size)

    def kernel(msg_ref, mid_ref, up_ref, down_ref, out_ref, low_ref, all_ref, act_ref, slope_ref, *scratch):
        slots, act, slope, scaled, save_sem = scratch[:5]
        scratch = scratch[5:]
        greet(*group.peers())
        slots[0] = msg_ref[...]

        def saves(slot):
            return (
                pltpu.make_async_copy(slots.at[slot], all_ref.at[slot], save_sem.at[slot, 0]),
                pltpu.make_async_copy(act.at[slot], act_ref.at[slot], save_sem.at[slot, 1]),
                pltpu.make_async_copy(slope.at[slot], slope_ref.at[slot], save_sem.at[slot, 2]),
            )

        def compute(slot, at):
            gates = jnp.transpose(join_rows(slots[slot, rows:]))[:rows]
            for expert in range(experts):
                cols = slice(expert * hid, (expert + 1) * hid)
                value, grade = gelu_parts(dot(slots[slot, :rows], up_ref[expert]))
                value = value.astype(BF16)
                act[slot, :, cols] = value
                slope[slot, :, cols] = grade.astype(BF16)
                scaled[:, cols] = (value.astype(F32) * gates[:, expert : expert + 1]).astype(BF16)
            for save in saves(slot):
                save.start()
            return dot(scaled[...], down_ref[...]), None

        group.run(slots, scratch, rows, 0, compute)
        group.collect()
        out = mid_ref[...] + group.own[0]
        out_ref[...] = out
        low_ref[...] = out.astype(BF16)
        for slot in range(size):
            for save in saves(slot):
                save.wait()

    return pl.pallas_call(
        kernel,
        out_shape=(
            jax.ShapeDtypeStruct((rows, width), F32),
            jax.ShapeDtypeStruct((rows, width), BF16),
            jax.ShapeDtypeStruct((size, rows + 16, width), BF16),
            jax.ShapeDtypeStruct((size, rows, wide), BF16),
            jax.ShapeDtypeStruct((size, rows, wide), BF16),
        ),
        in_specs=[in_vmem()] * 4,
        out_specs=(in_vmem(), in_vmem(), in_any(), in_any(), in_any()),
        scratch_shapes=[
            pltpu.VMEM((size, rows + 16, width), BF16),
            pltpu.VMEM((size, rows, wide), BF16),
            pltpu.VMEM((size, rows, wide), BF16),
            pltpu.VMEM((rows, wide), BF16),
            pltpu.SemaphoreType.DMA((size, 3)),
        ]
        + group.scratch(rows, 0, width),
        compiler_params=pltpu.CompilerParams(
            collective_id=1, has_side_effects=True, vmem_limit_bytes=VMEM_LIMIT
        ),
        name="experts_forward",
    )(message, middle, up, down)


class LineSums:
    def __init__(self, dp=0, **arrays):
        self.dp = dp
        self.kinds = list(arrays)
        self.args = tuple(arrays.values())
        self.dense = [kind for kind in self.kinds if kind[0] == "d" and kind[1] == "e"]
        self.chunk, self.count = {}, {}
        self.out_shape, self.scratch_shapes = (), []
        for kind, array in arrays.items():
            shape = array.shape
            if kind == "up":
                experts, _, quarters, r, hid = shape
                self.chunk[kind], self.count[kind] = (dp, r, hid), experts * quarters
                out = (experts, quarters * r, dp * hid)
                special = [
                    pltpu.VMEM((self.count[kind] // 2,) + self.chunk[kind], BF16),
                    pltpu.SemaphoreType.DMA((2, self.count[kind] // 2, dp)),
                    pltpu.VMEM(out, BF16),
                ]
            elif kind == "down":
                self.chunk[kind], self.count[kind] = shape[1:], shape[0]
                out, special = shape, []
            else:
                self.chunk[kind], self.count[kind] = (shape[2] // 2, shape[3]), 2
                out = (2,) + self.chunk[kind]
                whole = (dp // 2,) + shape[2:]
                special = [
                    pltpu.VMEM(whole, BF16),
                    pltpu.VMEM(whole, BF16),
                    pltpu.VMEM((2,) + self.chunk[kind], BF16),
                    pltpu.SemaphoreType.DMA((2,)),
                    pltpu.SemaphoreType.DMA((2, dp // 2)),
                ]
            count, chunk = self.count[kind], self.chunk[kind]
            self.out_shape += (jax.ShapeDtypeStruct(out, BF16),)
            self.scratch_shapes += [
                pltpu.VMEM((count,) + chunk, BF16),
                pltpu.VMEM((count // 2,) + chunk, BF16),
                pltpu.VMEM((count // 2,) + chunk, BF16),
                pltpu.VMEM((count,) + chunk, BF16),
                pltpu.SemaphoreType.DMA((2, count)),
                pltpu.SemaphoreType.DMA((2, count // 2)),
                pltpu.SemaphoreType.DMA((2, count)),
                pltpu.SemaphoreType.DMA((count // 2,)),
                pltpu.SemaphoreType.DMA,
            ] + special
        self.pairs = [(kind, p) for kind in self.kinds for p in range(self.count[kind] // 2)]

    def peers(self):
        if not self.kinds:
            return []
        me, mine = lax.axis_index("dp"), lax.axis_index("seq")
        middle = (mine == 1) | (mine == 2)
        return [({"dp": me ^ r}, None) for r in range(1, self.dp)] + [
            ({"seq": jnp.where(middle, 3 - mine, 1 + mine // 2)}, None),
            ({"seq": jnp.where(middle, 3 * (mine - 1), mine)}, middle),
        ]

    def bind(self, refs, outs, scratch):
        self.refs = dict(zip(self.kinds, refs))
        self.outs = dict(zip(self.kinds, outs))
        self.boxes = {}
        for kind in self.kinds:
            held = 14 if kind in self.dense else 12 if kind == "up" else 9
            self.boxes[kind], scratch = scratch[:held], scratch[held:]
        self.me, self.mine = lax.axis_index("dp"), lax.axis_index("seq")
        self.middle = (self.mine == 1) | (self.mine == 2)
        self.inner = {"seq": jnp.where(self.middle, 3 - self.mine, 1 + self.mine // 2)}
        self.outer = {"seq": jnp.where(self.middle, 3 * (self.mine - 1), self.mine)}
        self.side = jnp.where(self.mine == 2, 1, 0)

    def source(self, kind, c):
        if kind == "up":
            return self.refs[kind].at[c // 4, :, lax.rem(c, 4)]
        return self.boxes[kind][11].at[c] if kind in self.dense else self.refs[kind].at[c]

    def inward(self, kind, c):
        box, sem = self.boxes[kind][0], self.boxes[kind][4]
        return remote(self.source(kind, c), box.at[c], sem.at[0, c], sem.at[1, c], self.inner)

    def across(self, kind, p):
        box, sem = self.boxes[kind], self.boxes[kind][5]
        return remote(box[2].at[p], box[1].at[p], sem.at[0, p], sem.at[1, p], self.inner)

    def outward(self, kind, c):
        box, sem = self.boxes[kind][3], self.boxes[kind][6]
        return remote(box.at[c], box.at[c], sem.at[0, c], sem.at[1, c], self.outer)

    def between(self, kind, c, p):
        box = self.boxes[kind]
        return remote(box[3].at[c], box[3].at[c], box[7].at[p], box[6].at[1, c], self.inner)

    def span(self, p, c, r):
        box = self.boxes["up"]
        return remote(
            box[9].at[p, self.me ^ r], box[3].at[c, self.me], box[10].at[0, p, r], box[10].at[1, p, r],
            {"dp": self.me ^ r},
        )

    def near_copy(self, kind):
        box = self.boxes[kind]
        away = self.refs[kind].at[:, 1 - lax.rem(self.me, 2)]
        return remote(away, box[9], box[12].at[0], box[12].at[1], {"dp": self.me ^ 1})

    def far(self, kind, m):
        box = self.boxes[kind]
        return remote(
            box[9].at[(self.me // 2) ^ m], box[10].at[m], box[13].at[0, m], box[13].at[1, m],
            {"dp": self.me ^ (2 * m)},
        )

    def begin(self):
        @pl.when(jnp.logical_not(self.middle))
        def _():
            for kind, p in self.pairs:
                if kind not in self.dense:
                    self.inward(kind, 2 * p).start()
                    self.inward(kind, 2 * p + 1).start()

    def dense_begin(self, kind):
        self.near_copy(kind).start()

    def dense_near(self, kind):
        self.near_copy(kind).wait_recv()
        box = self.boxes[kind]
        for at in range(self.dp // 2):
            box[9][at] = (
                self.refs[kind][at, lax.rem(self.me, 2)].astype(F32) + box[9][at].astype(F32)
            ).astype(BF16)
        for m in range(1, self.dp // 2):
            self.far(kind, m).start()

    def dense_far(self, kind):
        for m in range(1, self.dp // 2):
            self.far(kind, m).wait_recv()
        box = self.boxes[kind]
        rows = self.chunk[kind][0]
        for at in range(2):
            place = slice(at * rows, (at + 1) * rows)
            total = box[9][self.me // 2, place].astype(F32)
            for m in range(1, self.dp // 2):
                total += box[10][m, place].astype(F32)
            box[11][at] = total.astype(BF16)

        @pl.when(jnp.logical_not(self.middle))
        def _():
            self.inward(kind, 0).start()
            self.inward(kind, 1).start()

    def relay(self, kind, p):
        c = 2 * p + 1 - self.side
        box = self.boxes[kind]
        self.inward(kind, c).wait_recv()
        box[2][p] = (self.source(kind, c)[...].astype(F32) + box[0][c].astype(F32)).astype(BF16)
        self.across(kind, p).start()

    def total(self, kind, p):
        c = 2 * p + self.side
        box = self.boxes[kind]
        self.inward(kind, c).wait_recv()
        self.across(kind, p).wait_recv()
        whole = (
            self.source(kind, c)[...].astype(F32) + box[0][c].astype(F32) + box[1][p].astype(F32)
        ).astype(BF16)
        if kind == "up":
            box[9][p] = whole
            box[3][c, self.me] = box[9][p, self.me]
            for r in range(1, self.dp):
                self.span(p, c, r).start()
        else:
            box[3][c] = whole
            self.between(kind, c, p).start()
            self.outward(kind, c).start()

    def turn(self, p):
        c = 2 * p + self.side
        for r in range(1, self.dp):
            self.span(p, c, r).wait_recv()
        self.between("up", c, p).start()
        self.outward("up", c).start()

    def forward(self, kind, p):
        c = 2 * p + 1 - self.side
        self.outward(kind, c).wait_recv()
        self.outward(kind, c).start()

    def ticks(self):
        count = len(self.pairs)
        if not count:
            return []

        def tick(at):
            @pl.when(self.middle)
            def _():
                if at < count:
                    self.relay(*self.pairs[at])
                if 0 <= at - 1 < count:
                    self.total(*self.pairs[at - 1])
                if 0 <= at - 2 < count and self.pairs[at - 2][0] == "up":
                    self.turn(self.pairs[at - 2][1])
                for behind in (2, 3):
                    if 0 <= at - behind < count:
                        kind, p = self.pairs[at - behind]
                        if behind == (3 if kind == "up" else 2):
                            self.forward(kind, p)

        last = 4 if self.pairs[-1][0] == "up" else 3
        return [lambda at=at: tick(at) for at in range(count + last - 1)]

    def finish(self):
        if not self.kinds:
            return

        @pl.when(jnp.logical_not(self.middle))
        def _():
            for kind, p in self.pairs:
                for c in (2 * p, 2 * p + 1):
                    self.outward(kind, c).wait_recv()
                    self.inward(kind, c).wait_send()

        copies = []
        for kind in self.kinds:
            box = self.boxes[kind][3]
            if kind == "up":
                r, hid = self.chunk["up"][1:]
                laid = self.boxes[kind][11]
                for c in range(self.count[kind]):
                    for owner in range(self.dp):
                        laid[
                            c // 4, (c % 4) * r : (c % 4 + 1) * r, owner * hid : (owner + 1) * hid
                        ] = box[c, owner]
                box = laid
            copies.append(pltpu.make_async_copy(box, self.outs[kind], self.boxes[kind][8]))
            copies[-1].start()

        @pl.when(self.middle)
        def _():
            for kind, p in self.pairs:
                self.across(kind, p).wait_send()
                self.between(kind, 2 * p + self.side, p).wait_send()
                self.outward(kind, 2 * p).wait_send()
                self.outward(kind, 2 * p + 1).wait_send()
                if kind == "up":
                    for r in range(1, self.dp):
                        self.span(p, 2 * p + self.side, r).wait_send()

        for kind in self.dense:
            self.near_copy(kind).wait_send()
            for m in range(1, self.dp // 2):
                self.far(kind, m).wait_send()
        for copy in copies:
            copy.wait()


def sum_weights_plainly(dp, down, up, dense):
    dense = lax.psum_scatter(dense.reshape(dp, -1, dense.shape[-1]), "dp", scatter_dimension=0, tiled=True)
    up = lax.all_to_all(up, "dp", split_axis=1, concat_axis=1, tiled=True)
    experts, _, quarters, r, hid = up.shape
    up = jnp.transpose(up.reshape(experts, dp, quarters * r, hid), (0, 2, 1, 3))
    return lax.psum(down, "seq"), lax.psum(up.reshape(experts, quarters * r, -1), "seq"), lax.psum(dense, "seq")


def experts_backward(grad, blocks, act, slope, up, down, plan, job, leaving=None):
    rows, width = grad.shape
    experts, _, hid = up.shape
    wide = experts * hid
    size = plan.dp
    group = Group(size)
    swap = Swap(plan)
    extra = [] if leaving is None else [leaving]
    steps = {2: 0, 3: 1, 4: 2, 5: 3, 6: 4, 7: 5}

    def kernel(*refs):
        (grad_ref, blocks_ref, act_ref, slope_ref, up_ref, down_ref), refs = refs[:6], refs[6:]
        if extra:
            leaving_ref, refs = refs[0], refs[1:]
        job_refs, refs = refs[: len(job.args)], refs[len(job.args) :]
        (out_ref, tail_ref, up_out, down_out), refs = refs[:4], refs[4:]
        if extra:
            left_ref, refs = refs[0], refs[1:]
        job_outs, refs = refs[: len(job.args)], refs[len(job.args) :]
        slots, blocks, facts, act, slope, weighed, scaled, pre, flat, load_sem = refs[:10]
        refs = refs[10:]
        scratch, refs = refs[:13], refs[13:]
        if extra:
            (left, left_sem), refs = refs[:2], refs[2:]
        job.bind(job_refs, job_outs, refs)
        ticks = job.ticks()

        def loads(at):
            two = lax.rem(at, 2)
            slot = 2 * group.pair_at(at // 2) + two
            place = pl.ds(pl.multiple_of(slot * rows, 16), rows)
            return (
                pltpu.make_async_copy(blocks_ref.at[slot, pl.ds(0, rows)], blocks.at[place], load_sem.at[two, 0]),
                pltpu.make_async_copy(act_ref.at[slot], act.at[two], load_sem.at[two, 1]),
                pltpu.make_async_copy(slope_ref.at[slot], slope.at[two], load_sem.at[two, 2]),
                pltpu.make_async_copy(blocks_ref.at[slot, pl.ds(rows, 16)], facts.at[two], load_sem.at[two, 3]),
            )

        for load in loads(0):
            load.start()
        greet(*group.peers(), *job.peers(), *(swap.peers() if extra else []))
        slots[0] = grad_ref[...]
        if extra:
            swap.start(leaving_ref, left, left_sem)
        if ticks:
            job.begin()
        for expert in range(experts):
            flat[:, expert * hid : (expert + 1) * hid] = up_ref[expert]
        lane = lax.broadcasted_iota(jnp.int32, (16, wide), 1) // hid
        pick = (lane == lax.broadcasted_iota(jnp.int32, (16, wide), 0)).astype(F32).astype(BF16)

        def compute(slot, at):
            two = lax.rem(at, 2)

            @pl.when(at + 1 < size)
            def _():
                for load in loads(at + 1):
                    load.start()

            for load in loads(at):
                load.wait()
            gates = jnp.transpose(join_rows(facts[two]))[:rows]
            place = pl.ds(pl.multiple_of(slot * rows, 16), rows)
            for expert in range(experts):
                cols = slice(expert * hid, (expert + 1) * hid)
                gate = gates[:, expert : expert + 1]
                pull = dot(slots[slot], down_ref[cols, :], NT)
                value = act[two, :, cols].astype(F32)
                weighed[:, cols] = (pull * value).astype(BF16)
                scaled[place, cols] = (value * gate).astype(BF16)
                pre[place, cols] = (pull * gate * slope[two, :, cols].astype(F32)).astype(BF16)
            if ticks:
                for step, tick in steps.items():
                    pl.when(at == step)(ticks[tick])
            by_expert = pad_lanes(dot(pick, weighed[...], NT)[:8], width)
            return dot(pre[place, :], flat[...], NT), by_expert

        group.run(slots, scratch, rows, 16, compute)

        def weight_sums(expert, carry):
            cols = pl.ds(pl.multiple_of(expert * hid, 128), hid)
            down_out[cols, :] = dot(scaled[:, cols], slots[...].reshape(size * rows, width), TN).astype(BF16)
            up_out[expert] = dot(blocks[...], pre[:, cols], TN).astype(BF16)
            if ticks:
                pl.when(expert == 0)(ticks[6])
                pl.when(expert == 2)(ticks[7])
            return carry

        lax.fori_loop(0, experts, weight_sums, 0)
        for tick in ticks[8:10]:
            tick()
        group.collect()
        out_ref[...] = group.own[0]
        tail_ref[...] = group.own_tail[0]
        for tick in ticks[10:]:
            tick()
        job.finish()
        if extra:
            swap.wait(leaving_ref, left, left_sem)
            left_ref[...] = left[...]

    left_shape = [] if leaving is None else [jax.ShapeDtypeStruct(leaving.shape, BF16)]
    left_scratch = [
        pltpu.VMEM((plan.images, plan.piece, width), BF16),
        pltpu.SemaphoreType.DMA((2, plan.images)),
    ]
    return pl.pallas_call(
        kernel,
        out_shape=(
            jax.ShapeDtypeStruct((rows, width), F32),
            jax.ShapeDtypeStruct((8, width), F32),
            jax.ShapeDtypeStruct((experts, width, hid), BF16),
            jax.ShapeDtypeStruct((wide, width), BF16),
            *left_shape,
            *job.out_shape,
        ),
        in_specs=[in_vmem(), in_any(), in_any(), in_any(), in_vmem(), in_vmem()]
        + [in_vmem()] * (len(extra) + len(job.args)),
        out_specs=(in_vmem(),) * (4 + len(extra)) + (in_any(),) * len(job.args),
        scratch_shapes=[
            pltpu.VMEM((size, rows, width), BF16),
            pltpu.VMEM((size * rows, width), BF16),
            pltpu.VMEM((2, 16, width), BF16),
            pltpu.VMEM((2, rows, wide), BF16),
            pltpu.VMEM((2, rows, wide), BF16),
            pltpu.VMEM((rows, wide), BF16),
            pltpu.VMEM((size * rows, wide), BF16),
            pltpu.VMEM((size * rows, wide), BF16),
            pltpu.VMEM((width, wide), BF16),
            pltpu.SemaphoreType.DMA((2, 4)),
        ]
        + group.scratch(rows, 16, width)
        + (left_scratch if extra else [])
        + job.scratch_shapes,
        compiler_params=pltpu.CompilerParams(
            collective_id=3 if job.kinds else 2, has_side_effects=True, vmem_limit_bytes=VMEM_LIMIT
        ),
        name="experts_backward_and_sums" if job.kinds else "experts_backward",
    )(grad, blocks, act, slope, up, down, *extra, *job.args)


def attention_forward(state, dense, chosen, length, expert_in, level, plan, cotangent=None):
    rows, width = state.shape
    share, size = plan.share, plan.dp
    swap = Swap(plan)
    extra = [] if cotangent is None else [cotangent]
    keys_len = rows * share
    heads = width // HEAD
    _, experts, strip, hidden = expert_in.shape
    hid = hidden // size

    def kernel(state_ref, dense_ref, chosen_ref, length_ref, in_ref, *refs):
        cot_in, refs = refs[: len(extra)], refs[len(extra) :]
        (message, middle, queries, kv, log_total, mixed, gates_ref, up_ref), refs = refs[:8], refs[8:]
        grads, refs = refs[: 2 * len(extra)], refs[2 * len(extra) :]
        all_kv, values_t, up_all, send, recv, save, up_send, up_recv, *cot = refs
        me = lax.axis_index("dp")
        part = lax.rem(me, share)
        greet(*[({"dp": me ^ r}, None) for r in range(1, size)], *(swap.peers() if extra else []))

        def mine_of(owner):
            return in_ref.at[level, :, :, pl.ds(pl.multiple_of(owner * hid, 128), hid)]

        def shift(r):
            return remote(
                mine_of(me ^ r), up_all.at[:, pl.ds(pl.multiple_of(me * strip, 16), strip)],
                up_send.at[r], up_recv.at[r], {"dp": me ^ r},
            )

        for r in range(1, size):
            shift(r).start()
        stay = pltpu.make_async_copy(
            mine_of(me), up_all.at[:, pl.ds(pl.multiple_of(me * strip, 16), strip)], up_recv.at[0]
        )
        stay.start()
        if extra:
            swap.start(cot_in[0], *cot)
        rows_of = weight_rows(dense_ref)
        unit, _ = normalize(state_ref[...])
        normed = (unit * rows_of[0:1] + rows_of[1:2]).astype(BF16)
        all_kv[part] = dot(normed, dense_ref[:, width : 3 * width]).astype(BF16)
        copies = [
            remote(all_kv.at[part], all_kv.at[part], send.at[k], recv.at[k], {"dp": me ^ k})
            for k in range(1, share)
        ]
        for copy in copies:
            copy.start()
        queries[...] = (dot(normed, dense_ref[:, :width]) * HEAD ** (-0.5)).astype(BF16)
        for copy in copies:
            copy.wait()
        saving = pltpu.make_async_copy(all_kv, kv, save)
        saving.start()
        for at in range(share):
            values_t[:, at * rows : (at + 1) * rows] = jnp.transpose(
                all_kv[at, :, width:].astype(F32)
            ).astype(BF16)
        key = lax.broadcasted_iota(jnp.int32, (keys_len, rows), 0)
        valid = key.astype(F32) < length_ref[0:1, 0:1]

        def pair_of_heads(pair, carry):
            lanes = pl.ds(pl.multiple_of(pair * 128, 128), 128)
            keys_pair = all_kv[:, :, lanes].reshape(keys_len, 128)
            queries_pair = queries[:, lanes]
            for parity in range(2):
                head = 2 * pair + parity
                scores = dot(keys_pair, one_head(queries_pair, parity), NT)
                scores = jnp.where(valid, scores, NEG)
                highest = jnp.max(scores, 0, keepdims=True)
                expo = jnp.exp(scores - highest)
                totals = row_sums(expo)
                log_total[head] = highest + jnp.log(totals)
                place = pl.ds(pl.multiple_of(head * HEAD, HEAD), HEAD)
                mixed[place, :] = (dot(values_t[place, :], expo.astype(BF16)) / totals).astype(BF16)
            return carry

        lax.fori_loop(0, heads // 2, pair_of_heads, 0)
        middle[...] = state_ref[...] + dot(mixed[...], dense_ref[:, 3 * width : 4 * width], TN)
        unit, _ = normalize(middle[...])
        normed = (unit * rows_of[2:3] + rows_of[3:4]).astype(BF16)
        message[:rows] = normed
        router = jnp.concatenate([rows_of[4:8], jnp.zeros((12, width), F32)], 0).astype(BF16)
        logits = dot(router, normed, NT)[:8]
        row = lax.broadcasted_iota(jnp.int32, logits.shape, 0)
        logits = jnp.where(row < experts, logits, NEG)
        expo = jnp.exp(logits - jnp.max(logits, 0, keepdims=True))
        gates = expo / row_sums(expo)
        gates_ref[...] = gates
        message[rows:] = split_rows(pad_lanes(gates * chosen_ref[:, :rows], width))
        saving.wait()
        stay.wait()
        for r in range(1, size):
            remote(
                mine_of(me ^ r), up_all.at[:, pl.ds(pl.multiple_of(me * strip, 16), strip)],
                up_send.at[r], up_recv.at[r], {"dp": me ^ r},
            ).wait_recv()
        keep = pltpu.make_async_copy(up_all, up_ref, save)
        keep.start()
        if extra:
            grad, grad_low = grads
            swap.wait(cot_in[0], *cot)
            for k in range(plan.images):
                place = slice(k * plan.piece, (k + 1) * plan.piece)
                row = lax.broadcasted_iota(jnp.int32, (plan.piece, width), 0) + part * rows + k * plan.piece
                masked = jnp.where(row.astype(F32) < length_ref[0:1, 0:1], cot[0][k].astype(F32), 0.0)
                grad[place] = masked
                grad_low[place] = masked.astype(BF16)
        for r in range(1, size):
            shift(r).wait_send()
        keep.wait()

    return pl.pallas_call(
        kernel,
        out_shape=(
            jax.ShapeDtypeStruct((rows + 16, width), BF16),
            jax.ShapeDtypeStruct((rows, width), F32),
            jax.ShapeDtypeStruct((rows, width), BF16),
            jax.ShapeDtypeStruct((share, rows, 2 * width), BF16),
            jax.ShapeDtypeStruct((heads, 1, rows), F32),
            jax.ShapeDtypeStruct((width, rows), BF16),
            jax.ShapeDtypeStruct((8, rows), F32),
            jax.ShapeDtypeStruct((experts, width, hid), BF16),
            *([jax.ShapeDtypeStruct((rows, width), dtype) for dtype in (F32, BF16)] if extra else []),
        ),
        in_specs=[in_vmem()] * 4 + [in_any()] + [in_vmem()] * len(extra),
        out_specs=(in_vmem(),) * 3 + (in_any(),) + (in_vmem(),) * 3 + (in_any(),)
        + (in_vmem(),) * (2 * len(extra)),
        scratch_shapes=[
            pltpu.VMEM((share, rows, 2 * width), BF16),
            pltpu.VMEM((width, keys_len), BF16),
            pltpu.VMEM((experts, width, hid), BF16),
            pltpu.SemaphoreType.DMA((share,)),
            pltpu.SemaphoreType.DMA((share,)),
            pltpu.SemaphoreType.DMA,
            pltpu.SemaphoreType.DMA((size,)),
            pltpu.SemaphoreType.DMA((size,)),
        ]
        + (
            [
                pltpu.VMEM((plan.images, plan.piece, width), BF16),
                pltpu.SemaphoreType.DMA((2, plan.images)),
            ]
            if extra
            else []
        ),
        compiler_params=pltpu.CompilerParams(
            collective_id=5 + len(extra), has_side_effects=True, vmem_limit_bytes=VMEM_LIMIT
        ),
        name="attention_forward",
    )(state, dense, chosen, length, expert_in, *extra)


def attention_backward(
    grad, back, back_tail, state, middle, message, gates, chosen, queries, kv, log_total, mixed,
    dense, length, plan, job, last,
):
    rows, width = state.shape
    share = plan.share
    keys_len = rows * share
    heads = width // HEAD
    columns = dense.shape[1]
    swap = Swap(plan)
    strip = width // plan.dp
    dense_shape = (plan.dp // 2, 2, strip, columns)

    def kernel(*refs):
        (
            grad_ref, back_ref, tail_ref, state_ref, mid_ref, msg_ref, gates_ref, chosen_ref, queries, kv,
            log_total, mixed, weights, length_ref,
        ), refs = refs[:14], refs[14:]
        taken = len(job.args)
        job_refs, refs = refs[:taken], refs[taken:]
        (new_ref, new_low_ref, dense_ref), refs = refs[:3], refs[3:]
        job_outs, refs = refs[: len(job.out_shape)], refs[len(job.out_shape) :]
        (
            keys_t, normed_ref, grad_mid, grad_heads, grad_q, kv_grads, kv_got, grad_packed, send, recv,
        ), refs = refs[:10], refs[10:]
        if last:
            (pieces, piece_sem), refs = refs[:2], refs[2:]
            job_refs = job_refs + (dense_ref,) if job.kinds else ()
        job.bind(job_refs, job_outs, refs)
        ticks = job.ticks()
        me = lax.axis_index("dp")
        part = lax.rem(me, share)
        greet(
            *[({"dp": me ^ k}, None) for k in range(1, share)], *job.peers(), *(swap.peers() if last else [])
        )
        if ticks:
            job.begin()
            job.dense_begin(job.dense[0])
        rows_of = weight_rows(weights)
        gates = gates_ref[...]
        grad_gates = tail_ref[:, :rows] * chosen_ref[:, :rows]
        grad_logits = split_rows(gates * (grad_gates - row_sums(gates * grad_gates)))
        router = jnp.concatenate([rows_of[4:8], jnp.zeros((4, width), F32)], 0)
        twice = jnp.concatenate([router, router], 0).astype(BF16)
        grad_normed = back_ref[...] + dot(grad_logits, twice, TN)
        router_grad = dot(grad_logits, msg_ref[:rows])
        router_grad = router_grad[:8] + router_grad[8:]
        unit, inverse = normalize(mid_ref[...])
        gain_two = row_sums(grad_normed * unit)
        bias_two = row_sums(grad_normed)
        grad_mid[...] = grad_ref[...] + norm_back(grad_normed * rows_of[2:3], unit, inverse)
        low = grad_mid[...].astype(BF16)

        def put(columns_of, values):
            for at in range(plan.dp):
                dense_ref[at // 2, at % 2, :, columns_of] = values[at * strip : (at + 1) * strip].astype(BF16)

        put(slice(3 * width, 4 * width), dot(mixed[...], low))
        grad_heads[...] = dot(low, weights[:, 3 * width : 4 * width], NT).astype(BF16)
        for at in range(share):
            keys_t[:, at * rows : (at + 1) * rows] = jnp.transpose(kv[at, :, :width].astype(F32)).astype(BF16)
        key = lax.broadcasted_iota(jnp.int32, (keys_len, rows), 0)
        valid = key.astype(F32) < length_ref[0:1, 0:1]

        def pair_of_heads(pair, carry):
            lanes = pl.ds(pl.multiple_of(pair * 128, 128), 128)
            value_lanes = pl.ds(pl.multiple_of(width + pair * 128, 128), 128)
            keys_pair = kv[:, :, lanes].reshape(keys_len, 128)
            values_pair = kv[:, :, value_lanes].reshape(keys_len, 128)
            grad_k = jnp.zeros((keys_len, 128), F32)
            grad_v = jnp.zeros((keys_len, 128), F32)
            for parity in range(2):
                head = 2 * pair + parity
                query = one_head(queries[:, lanes], parity)
                pull = one_head(grad_heads[:, lanes], parity)
                scores = dot(keys_pair, query, NT)
                probs = jnp.where(valid, jnp.exp(scores - log_total[head]), 0.0)
                grad_probs = dot(values_pair, pull, NT)
                grad_scores = probs * (grad_probs - row_sums(probs * grad_probs))
                grad_scores = grad_scores.astype(BF16)
                grad_v += dot(probs.astype(BF16), pull)
                grad_k += dot(grad_scores, query)
                place = pl.ds(pl.multiple_of(head * HEAD, HEAD), HEAD)
                grad_q[place, :] = dot(keys_t[place, :], grad_scores) * HEAD ** (-0.5)
            kv_grads[:, :, lanes] = grad_k.astype(BF16).reshape(share, rows, 128)
            kv_grads[:, :, value_lanes] = grad_v.astype(BF16).reshape(share, rows, 128)
            if ticks:
                for at in range(3):
                    pl.when(pair == heads // 2 - 3 + at)(ticks[at])
                pl.when(pair == heads // 2 - 2)(lambda: job.dense_near(job.dense[0]))
            return carry

        lax.fori_loop(0, heads // 2, pair_of_heads, 0)
        if ticks:
            ticks[3]()
        copies = [
            remote(kv_grads.at[part ^ k], kv_got.at[k], send.at[k], recv.at[k], {"dp": me ^ k})
            for k in range(1, share)
        ]
        for copy in copies:
            copy.start()
        unit, inverse = normalize(state_ref[...])
        normed_ref[...] = (unit * rows_of[0:1] + rows_of[1:2]).astype(BF16)
        grad_packed[:, :width] = jnp.transpose(grad_q[...]).astype(BF16)
        for copy in copies:
            copy.wait()
        total = kv_grads[part].astype(F32)
        for k in range(1, share):
            total += kv_got[k].astype(F32)
        grad_packed[:, width:] = total.astype(BF16)
        grad_normed = dot(grad_packed[...], weights[:, : 3 * width], NT)
        for block in range(3):
            cols = slice(block * width, (block + 1) * width)
            put(cols, dot(normed_ref[...], grad_packed[:, cols], TN))
        gain_one = row_sums(grad_normed * unit)
        bias_one = row_sums(grad_normed)
        tail = jnp.concatenate([gain_one, bias_one, gain_two, bias_two, router_grad[:4]], 0)
        put(slice(4 * width, columns), pad_lanes(jnp.transpose(tail), columns - 4 * width))
        if ticks:
            ticks[4]()
            job.dense_begin(job.dense[1])
        new = grad_mid[...] + norm_back(grad_normed * rows_of[0:1], unit, inverse)
        if last:
            for k in range(plan.images):
                new_low_ref[k] = new[k * plan.piece : (k + 1) * plan.piece].astype(BF16)
            swap.start(new_low_ref, pieces, piece_sem)
        else:
            new_low_ref[...] = new.astype(BF16)
            new_ref[...] = new
        for at, tick in enumerate(ticks[5:], 5):
            if at == 5:
                job.dense_near(job.dense[1])
            if at == 10:
                job.dense_far(job.dense[0])
                job.dense_far(job.dense[1])
            tick()
        job.finish()
        if last:
            swap.wait(new_low_ref, pieces, piece_sem)
            for k in range(plan.images):
                new_ref[k] = pieces[k].astype(F32)

    image_shape = (plan.images, plan.piece, width) if last else (rows, width)
    last_scratch = [
        pltpu.VMEM((plan.images, plan.piece, width), BF16),
        pltpu.SemaphoreType.DMA((2, plan.images)),
    ]
    return pl.pallas_call(
        kernel,
        out_shape=(
            jax.ShapeDtypeStruct(image_shape, F32),
            jax.ShapeDtypeStruct(image_shape, BF16),
            jax.ShapeDtypeStruct(dense_shape, BF16),
            *job.out_shape,
        ),
        in_specs=[in_vmem()] * (14 + len(job.args)),
        out_specs=(in_vmem(),) * 3 + (in_any(),) * len(job.out_shape),
        scratch_shapes=[
            pltpu.VMEM((width, keys_len), BF16),
            pltpu.VMEM((rows, width), BF16),
            pltpu.VMEM((rows, width), F32),
            pltpu.VMEM((rows, width), BF16),
            pltpu.VMEM((width, rows), F32),
            pltpu.VMEM((share, rows, 2 * width), BF16),
            pltpu.VMEM((share, rows, 2 * width), BF16),
            pltpu.VMEM((rows, 3 * width), BF16),
            pltpu.SemaphoreType.DMA((share,)),
            pltpu.SemaphoreType.DMA((share,)),
        ]
        + (last_scratch if last else [])
        + job.scratch_shapes,
        compiler_params=pltpu.CompilerParams(
            collective_id=9 if last else 8, has_side_effects=True, vmem_limit_bytes=VMEM_LIMIT
        ),
        name="attention_backward_last" if last else "attention_backward",
    )(
        grad, back, back_tail, state, middle, message, gates, chosen, queries, kv, log_total, mixed,
        dense, length, *job.args,
    )


def build(mesh):
    def shards(
        tokens,
        cotangent,
        routes,
        token_mask,
        ln1_gain,
        ln1_bias,
        qkv_weight,
        out_weight,
        ln2_gain,
        ln2_bias,
        router_weight,
        expert_in,
        expert_out,
    ):
        images, piece, width = tokens.shape
        levels, experts = expert_in.shape[:2]
        plan = Plan(mesh, images, token_mask.shape[1])
        rows = plan.rows
        wide = experts * expert_out.shape[2]
        lined = plan.seq == 4

        mine = lax.rem(lax.axis_index("seq"), images)
        chosen = jnp.sum((routes[..., None] == jnp.arange(experts, dtype=jnp.int32)).astype(F32), -2)
        chosen = jnp.transpose(chosen, (1, 0, 3, 2))
        at_slot = (jnp.arange(images) == mine).astype(F32)[:, None]
        chosen = (chosen[..., None, :] * at_slot).reshape(images, levels, experts, rows)
        chosen = jnp.pad(chosen, ((0, 0), (0, 0), (0, 8 - experts), (0, width - rows)))
        lengths = jnp.where(mine == 0, jnp.sum(token_mask, -1), 0)
        lengths = jnp.stack([lengths // 4, lengths % 4], -1).astype(F32)
        lengths = jnp.pad(lengths, ((0, 0), (0, 14)))[:, :, None]
        facts = jnp.concatenate(
            [chosen.reshape(images, 8 * levels, width), jnp.broadcast_to(lengths, (images, 16, width))], 1
        ).astype(BF16)

        vectors = jnp.stack([ln1_gain, ln1_bias, ln2_gain, ln2_bias], -1)
        tails = jnp.concatenate([vectors, router_weight], -1)
        tails = jnp.pad(tails, ((0, 0), (0, 0), (0, 128 - tails.shape[-1])))
        dense_own = jnp.concatenate([qkv_weight, out_weight, tails], -1)
        state, chosen, length, dense_first = bring_in(plan, tokens, facts, dense_own[0])
        dense_all = [dense_first]
        for level in range(1, levels):
            dense_all.append(lax.all_gather(dense_own[level], "dp", axis=0, tiled=True))
        down_all = expert_out.reshape(levels, wide, width)

        saved = []
        for level in range(levels):
            message, middle, queries, kv, log_total, mixed, gates, up, *grads = attention_forward(
                state, dense_all[level], chosen[level], length, expert_in, level, plan,
                None if level else cotangent,
            )
            if grads:
                grad, grad_low = grads
            new_state, new_low, blocks, act, slope = experts_forward(
                message, middle, up, down_all[level], plan.dp
            )
            attended = (
                state, middle, message, gates, chosen[level], queries, kv, log_total, mixed,
                dense_all[level], length,
            )
            saved.append((attended, (blocks, act, slope, up, down_all[level])))
            state = new_state
        leaving = new_low.reshape(images, piece, width)

        sums = [None] * levels
        job = LineSums()
        for level in reversed(range(levels)):
            attended, routed = saved[level]
            last = level == 0
            back, back_tail, up_grad, down_grad, *others = experts_backward(
                grad_low, *routed, plan, job, leaving
            )
            if leaving is not None:
                output, *others = others
                leaving = None
            if job.kinds:
                downs, ups = others
            up_grad = up_grad.reshape(experts, plan.dp, 4, width // plan.dp // 4, -1)
            down_grad = down_grad.reshape(16, wide // 16, width)
            job = LineSums()
            if lined and last:
                more = {} if level + 1 == levels else {"dense_more": dense_grad}
                blank = jax.ShapeDtypeStruct((plan.dp // 2, 2, width // plan.dp, dense_own.shape[-1]), BF16)
                job = LineSums(plan.dp, down=down_grad, up=up_grad, **more, dense=blank)
                job.args = job.args[:-1]
            grad, grad_low, dense_grad, *others = attention_backward(
                grad, back, back_tail, *attended, plan, job, last
            )
            if not lined:
                sums[level] = sum_weights_plainly(plan.dp, down_grad, up_grad, dense_grad)
            elif last:
                sums[level] = (others[0], others[1], others[-1])
                sums[level + 1] = (downs, ups, others[2])
            else:
                job = LineSums(plan.dp, down=down_grad, up=up_grad)
        down_grad, up_grad, dense_grad = (
            jnp.stack([item.reshape(like.shape[1:]) for item in items]).astype(F32)
            for items, like in zip(zip(*sums), (expert_out, expert_in, dense_own))
        )
        return (
            output,
            grad,
            dense_grad[..., 4 * width],
            dense_grad[..., 4 * width + 1],
            dense_grad[..., : 3 * width],
            dense_grad[..., 3 * width : 4 * width],
            dense_grad[..., 4 * width + 2],
            dense_grad[..., 4 * width + 3],
            dense_grad[..., 4 * width + 4 : 4 * width + 4 + experts],
            up_grad,
            down_grad,
        )

    return shards


def solution(mesh):
    return jax.shard_map(
        build(mesh),
        mesh=mesh,
        in_specs=(
            P("dp", "seq", None),
            P("dp", "seq", None),
            P(None, "dp", "seq", None),
            P("dp", None),
            P(None, "dp"),
            P(None, "dp"),
            P(None, "dp", None),
            P(None, "dp", None),
            P(None, "dp"),
            P(None, "dp"),
            P(None, "dp", None),
            P(None, None, "dp", None),
            P(None, None, "dp", None),
        ),
        out_specs=(
            P("dp", "seq", None),
            P("dp", "seq", None),
            P(None, "dp"),
            P(None, "dp"),
            P(None, "dp", None),
            P(None, "dp", None),
            P(None, "dp"),
            P(None, "dp"),
            P(None, "dp", None),
            P(None, None, "dp", None),
            P(None, None, "dp", None),
        ),
        check_vma=False,
    )
```

```python
import itertools

import jax
import jax.numpy as jnp
from jax import lax
from jax.experimental import pallas as pl
from jax.experimental.pallas import tpu as pltpu
from jax.sharding import PartitionSpec as P

HEAD = 64
EPS = 1e-06
NEG = -1e30
F32 = jnp.float32
BF16 = jnp.bfloat16
MESH = pl.DeviceIdType.MESH
VMEM_LIMIT = 60 * 1024 * 1024
EXPERT_TICKS = ((0, 2, 1, 1, 1, 1, 1, 1), (1, 0, 1, 0), (1,), (1, 1, 0))
HEAD_TICKS = ((0, 1, 1, 1), (1,), (1,))
DENSE_TICKS = (5, 6, 14)
NT = ((1,), (1,))
TN = ((0,), (0,))


def normalize(values):
    center = values - jnp.mean(values, -1, keepdims=True)
    inverse = lax.rsqrt(jnp.mean(center * center, -1, keepdims=True) + EPS)
    return center * inverse, inverse


def norm_back(grad_unit, unit, inverse):
    return inverse * (
        grad_unit
        - jnp.mean(grad_unit, -1, keepdims=True)
        - unit * jnp.mean(grad_unit * unit, -1, keepdims=True)
    )


def in_vmem():
    return pl.BlockSpec(memory_space=pltpu.VMEM)


def in_any():
    return pl.BlockSpec(memory_space=pl.ANY)


def greet(*peers):
    barrier = pltpu.get_barrier_semaphore()
    count = 0
    for peer, condition in peers:

        def signal(peer=peer):
            pl.semaphore_signal(barrier, inc=1, device_id=peer, device_id_type=MESH)

        if condition is None:
            signal()
            count += 1
        else:
            pl.when(condition)(signal)
            count += condition.astype(jnp.int32)
    pl.semaphore_wait(barrier, count)


def remote(src, dst, send, recv, peer):
    return pltpu.make_async_remote_copy(
        src_ref=src, dst_ref=dst, send_sem=send, recv_sem=recv, device_id=peer, device_id_type=MESH
    )


def split_rows(rows8):
    high = rows8.astype(BF16).astype(F32)
    return jnp.concatenate([high, rows8 - high], 0).astype(BF16)


def join_rows(rows16):
    wide = rows16.astype(F32)
    return wide[:8] + wide[8:]


def gelu_parts(u):
    bell = jnp.exp2(u * u * -0.7213475204444817)
    t = pl.reciprocal(1.0 + 0.23164190 * jnp.abs(u), approx=True)
    poly = t * (
        0.127414796 + t * (-0.142248368 + t * (0.7107068705 + t * (-0.7265760135 + t * 0.5307027145)))
    )
    half = poly * bell
    cdf = jnp.where(u >= 0, 1.0 - half, half)
    return u * cdf, cdf + u * 0.3989422804014327 * bell


def dot(left, right, dims=((1,), (0,))):
    return lax.dot_general(left, right, (dims, ((), ())), preferred_element_type=F32)


def row_sums(values):
    return jnp.sum(values, 0, keepdims=True)


def pad_lanes(values, lanes):
    if values.shape[1] == lanes:
        return values
    return jnp.concatenate([values, jnp.zeros((values.shape[0], lanes - values.shape[1]), values.dtype)], 1)


def one_head(pair, parity):
    lane = lax.broadcasted_iota(jnp.int32, pair.shape, 1) // HEAD
    return jnp.where(lane == parity, pair.astype(F32), 0.0).astype(BF16)


def weight_rows(dense_ref):
    width = dense_ref.shape[0]
    return jnp.transpose(dense_ref[:, 4 * width :].astype(F32))


class Plan:
    def __init__(self, mesh, images, length):
        self.dp = mesh.shape["dp"]
        self.seq = mesh.shape["seq"]
        self.images = images
        self.piece = length // self.seq
        self.share = self.seq // images
        self.rows = images * self.piece


class Swap:
    def __init__(self, plan):
        self.plan = plan

    def where(self, k):
        me, mine = lax.axis_index("dp"), lax.axis_index("seq")
        share, images = self.plan.share, self.plan.images
        part = lax.rem(me, share)
        peer = {"dp": me - part + mine // images, "seq": part * images + k}
        stays = (part == mine // images) & (lax.rem(mine, images) == k)
        return peer, stays

    def peers(self):
        both = [self.where(k) for k in range(self.plan.images)]
        return [(peer, jnp.logical_not(stays)) for peer, stays in both]

    def start(self, src, dst, sems):
        slot = lax.rem(lax.axis_index("seq"), self.plan.images)
        for k in range(self.plan.images):
            peer, stays = self.where(k)

            @pl.when(jnp.logical_not(stays))
            def _():
                remote(src.at[k], dst.at[slot], sems.at[0, k], sems.at[1, slot], peer).start()

            @pl.when(stays)
            def _():
                pltpu.make_async_copy(src.at[k], dst.at[k], sems.at[1, k]).start()

    def wait(self, src, dst, sems):
        for k in range(self.plan.images):
            peer, stays = self.where(k)
            moved = remote(src.at[k], dst.at[k], sems.at[0, k], sems.at[1, k], peer)

            @pl.when(jnp.logical_not(stays))
            def _():
                moved.wait_recv()
                moved.wait_send()

            @pl.when(stays)
            def _():
                pltpu.make_async_copy(src.at[k], dst.at[k], sems.at[1, k]).wait()


class Slots:
    def __init__(self, ref):
        self.ref = ref
        self.rows = ref.shape[1]

    def at(self, slot, part, device):
        return self.ref.at[slot, part]


class Strips:
    def __init__(self, ref, rows):
        self.ref = ref
        self.rows = rows

    def at(self, slot, part, device):
        first = pl.multiple_of((device ^ slot) * self.rows + part.start, 16)
        return self.ref.at[pl.ds(first, part.size)]


class Spread:
    def __init__(self, size):
        self.size = size
        self.pairs = size // 2
        self.order = sorted(range(self.pairs), key=lambda pair: (bin(pair).count("1"), pair))
        self.bits = [1 << k for k in range(self.pairs.bit_length() - 1)]

    def ways(self, pair):
        return (pair & -pair, 1 << (pair.bit_length() - 1))

    def pair_at(self, turn):
        if isinstance(turn, int):
            return self.order[turn]
        pair = turn
        for at, value in enumerate(self.order):
            if at != value:
                pair = jnp.where(turn == at, value, pair)
        return pair

    def peers(self):
        me = lax.axis_index("dp")
        return [({"dp": me ^ r}, None) for r in (1, *range(2, self.size, 2))]

    def semaphores(self):
        return [
            pltpu.SemaphoreType.DMA((2, self.pairs)),
            pltpu.SemaphoreType.DMA((2, self.size)),
            pltpu.SemaphoreType.DMA((self.pairs,)),
        ]

    def bind(self, slots, semaphores):
        self.slots = slots
        self.send, self.recv, self.hand = semaphores
        self.me = lax.axis_index("dp")
        cut = slots.rows // 32 * 16
        self.whole = pl.ds(0, slots.rows)
        self.halves = (pl.ds(0, cut), pl.ds(cut, slots.rows - cut))

    def move(self, slot, to_slot, part, peer, send, recv):
        return remote(
            self.slots.at(slot, part, self.me), self.slots.at(to_slot, part, peer), send, recv, {"dp": peer}
        )

    def block(self, pair):
        slot = 2 * pair
        return self.move(0, slot, self.whole, self.me ^ slot, self.send.at[0, pair], self.recv.at[0, slot])

    def half_block(self, pair, half):
        way = self.ways(pair)[half]
        return self.move(
            2 * (pair ^ way), 2 * pair, self.halves[half], self.me ^ (2 * way),
            self.send.at[half, pair], self.recv.at[half, 2 * pair],
        )

    def handed(self, pair):
        slot = 2 * pair
        return self.move(
            slot, slot + 1, self.whole, self.me ^ 1, self.hand.at[pair], self.recv.at[0, slot + 1]
        )

    def start(self):
        self.handed(0).start()
        for bit in self.bits:
            self.block(bit).start()

    def arrive(self, pair):
        for known in range(1, self.pairs):

            @pl.when(jnp.asarray(pair) == known)
            def _():
                if known in self.bits:
                    self.block(known).wait_recv()
                else:
                    self.half_block(known, 0).wait_recv()
                    self.half_block(known, 1).wait_recv()
                for far in range(1, self.pairs):
                    for half, way in enumerate(self.ways(far)):
                        if far not in self.bits and far ^ way == known:
                            self.half_block(far, half).start()

        self.handed(pair).start()

    def drain(self):
        for pair in range(self.pairs):
            self.handed(pair).wait_send()
            if pair in self.bits:
                self.block(pair).wait_send()
            elif pair:
                self.half_block(pair, 0).wait_send()
                self.half_block(pair, 1).wait_send()


class Group(Spread):
    def scratch(self, rows, tail, width):
        full = rows + tail
        return self.semaphores() + [
            pltpu.VMEM((self.pairs, rows, width), F32),
            pltpu.VMEM((self.pairs, 8, width), F32),
            pltpu.VMEM((self.pairs, full, width), BF16),
            pltpu.VMEM((self.pairs, full, width), BF16),
            pltpu.VMEM((self.pairs, full, width), BF16),
            pltpu.VMEM((self.pairs, full, width), BF16),
            pltpu.SemaphoreType.DMA((self.pairs,)),
            pltpu.SemaphoreType.DMA((self.pairs,)),
            pltpu.SemaphoreType.DMA((self.pairs,)),
            pltpu.SemaphoreType.DMA((self.pairs,)),
        ]

    def given(self, pair):
        return remote(
            self.give.at[pair], self.take.at[pair], self.g_send.at[pair], self.g_recv.at[pair], {"dp": self.me ^ 1}
        )

    def paid(self, pair):
        return remote(
            self.pay.at[pair], self.due.at[pair], self.p_send.at[pair], self.p_recv.at[pair],
            {"dp": self.me ^ (2 * pair)},
        )

    def run(self, slots, scratch, rows, tail, compute):
        self.bind(Slots(slots), scratch[:3])
        (
            self.own, self.own_tail, self.give, self.take, self.pay, self.due,
            self.g_send, self.g_recv, self.p_send, self.p_recv,
        ) = scratch[3:]
        self.sizes = rows, tail

        def settle(pair):
            self.given(pair).wait_recv()
            self.own[pair] += self.take[pair, :rows].astype(F32)
            if tail:
                self.own_tail[pair] += join_rows(self.take[pair, rows:])

            @pl.when(jnp.asarray(pair) > 0)
            def _():
                self.pay[pair, :rows] = self.own[pair].astype(BF16)
                if tail:
                    self.pay[pair, rows:] = split_rows(self.own_tail[pair])
                self.paid(pair).start()

        self.start()

        def step(at, carry):
            turn = at // 2
            pair = self.pair_at(turn)
            even = lax.rem(at, 2) == 0
            slot = 2 * pair + lax.rem(at, 2)

            @pl.when(even & (turn > 0))
            def _():
                self.arrive(pair)
                settle(self.pair_at(turn - 1))

            @pl.when(jnp.logical_not(even))
            def _():
                self.handed(pair).wait_recv()

            total, total_tail = compute(slot, at)

            @pl.when(even)
            def _():
                self.own[pair] = total
                if tail:
                    self.own_tail[pair] = total_tail

            @pl.when(jnp.logical_not(even))
            def _():
                self.give[pair, :rows] = total.astype(BF16)
                if tail:
                    self.give[pair, rows:] = split_rows(total_tail)
                self.given(pair).start()

            return carry

        lax.fori_loop(0, self.size, step, 0)
        settle(self.order[-1])

    def collect(self, between=()):
        rows, tail = self.sizes
        for pair, steps in zip(self.order[1:], itertools.chain(between, itertools.repeat(()))):
            self.paid(pair).wait_recv()
            for step in steps:
                step()
            self.own[0] += self.due[pair, :rows].astype(F32)
            if tail:
                self.own_tail[0] += join_rows(self.due[pair, rows:])
        for pair in range(self.pairs):
            self.given(pair).wait_send()
            if pair:
                self.paid(pair).wait_send()
        self.drain()


def experts_forward(message, middle, up, down, size, strip=None):
    rows, width = middle.shape
    experts, _, hid = up.shape
    wide = experts * hid
    group = Group(size)
    spread = Spread(size)
    extra = [] if strip is None else [strip]

    def kernel(msg_ref, mid_ref, up_ref, down_ref, *refs):
        strip_ref, refs = refs[: len(extra)], refs[len(extra) :]
        (out_ref, low_ref, all_ref, act_ref, slope_ref), refs = refs[:5], refs[5:]
        dense_ref, refs = refs[: len(extra)], refs[len(extra) :]
        (slots, act, slope, scaled, save_sem), refs = refs[:5], refs[5:]
        scratch, refs = refs[:13], refs[13:]
        if extra:
            dense_all, keep_sem, *sems = refs
            me = lax.axis_index("dp")
            spread.bind(Strips(dense_all, strip.shape[0]), sems)
            dense_all[pl.ds(pl.multiple_of(me * strip.shape[0], 16), strip.shape[0])] = strip_ref[0][...]
        greet(*group.peers())
        slots[0] = msg_ref[...]

        def saves(slot):
            return (
                pltpu.make_async_copy(slots.at[slot], all_ref.at[slot], save_sem.at[slot, 0]),
                pltpu.make_async_copy(act.at[slot], act_ref.at[slot], save_sem.at[slot, 1]),
                pltpu.make_async_copy(slope.at[slot], slope_ref.at[slot], save_sem.at[slot, 2]),
            )

        def compute(slot, at):
            gates = jnp.transpose(join_rows(slots[slot, rows:]))[:rows]
            for expert in range(experts):
                cols = slice(expert * hid, (expert + 1) * hid)
                value, grade = gelu_parts(dot(slots[slot, :rows], up_ref[expert]))
                value = value.astype(BF16)
                act[slot, :, cols] = value
                slope[slot, :, cols] = grade.astype(BF16)
                scaled[:, cols] = (value.astype(F32) * gates[:, expert : expert + 1]).astype(BF16)
            for save in saves(slot):
                save.start()
            if extra:
                pl.when(at == 0)(spread.start)
                for turn, pair in enumerate(spread.order[1:], 1):
                    pl.when(at == (3 if pair in spread.bits else 5))(lambda pair=pair: spread.arrive(pair))
            return dot(scaled[...], down_ref[...]), None

        group.run(slots, scratch, rows, 0, compute)
        if extra:
            for pair in spread.order:
                spread.handed(pair).wait_recv()
            keep = pltpu.make_async_copy(dense_all, dense_ref[0], keep_sem)
            keep.start()
        group.collect()
        out = mid_ref[...] + group.own[0]
        out_ref[...] = out
        low_ref[...] = out.astype(BF16)
        for slot in range(size):
            for save in saves(slot):
                save.wait()
        if extra:
            spread.drain()
            keep.wait()

    return pl.pallas_call(
        kernel,
        out_shape=(
            jax.ShapeDtypeStruct((rows, width), F32),
            jax.ShapeDtypeStruct((rows, width), BF16),
            jax.ShapeDtypeStruct((size, rows + 16, width), BF16),
            jax.ShapeDtypeStruct((size, rows, wide), BF16),
            jax.ShapeDtypeStruct((size, rows, wide), BF16),
            *[jax.ShapeDtypeStruct((size * item.shape[0], item.shape[1]), BF16) for item in extra],
        ),
        in_specs=[in_vmem()] * (4 + len(extra)),
        out_specs=(in_vmem(), in_vmem(), in_any(), in_any(), in_any()) + (in_any(),) * len(extra),
        scratch_shapes=[
            pltpu.VMEM((size, rows + 16, width), BF16),
            pltpu.VMEM((size, rows, wide), BF16),
            pltpu.VMEM((size, rows, wide), BF16),
            pltpu.VMEM((rows, wide), BF16),
            pltpu.SemaphoreType.DMA((size, 3)),
        ]
        + group.scratch(rows, 0, width)
        + (
            [pltpu.VMEM((size * strip.shape[0], strip.shape[1]), BF16), pltpu.SemaphoreType.DMA]
            + spread.semaphores()
            if extra
            else []
        ),
        compiler_params=pltpu.CompilerParams(
            collective_id=10 if extra else 1, has_side_effects=True, vmem_limit_bytes=VMEM_LIMIT
        ),
        name="experts_forward",
    )(message, middle, up, down, *extra)


class Shift:
    def __init__(self, source):
        experts, self.dp, quarters, r, self.hid = source.shape
        self.experts = experts
        self.shape = (experts, quarters, r, self.dp * self.hid)
        self.scratch_shapes = [
            pltpu.VMEM(self.shape, BF16),
            pltpu.VMEM((self.dp, experts, quarters, r, self.hid), BF16),
            pltpu.SemaphoreType.DMA((2, self.dp)),
        ]

    def copy(self, src, dst, box, sems, r):
        me = lax.axis_index("dp")
        return remote(src.at[:, me ^ r], box.at[me], sems.at[0, r], sems.at[1, r], {"dp": me ^ r})

    def start(self, *refs):
        for r in range(1, self.dp):
            self.copy(*refs, r).start()

    def arrive(self, src, dst, box, sems):
        me = lax.axis_index("dp")
        box[me] = src[:, me]
        for r in range(1, self.dp):
            self.copy(src, dst, box, sems, r).wait_recv()
        for owner in range(self.dp):
            dst[:, :, :, owner * self.hid : (owner + 1) * self.hid] = box[owner]

    def drain(self, *refs):
        for r in range(1, self.dp):
            self.copy(*refs, r).wait_send()


class LineSums:
    def __init__(self, dp=0, down_chunks=None, **arrays):
        self.dp = dp
        self.first = down_chunks[0] if down_chunks else 0
        self.kinds = list(arrays)
        self.args = tuple(array for array in arrays.values() if not isinstance(array, jax.ShapeDtypeStruct))
        self.dense = [kind for kind in self.kinds if kind.startswith("dense")]
        self.chunk, self.count = {}, {}
        self.out_shape, self.scratch_shapes = (), []
        for kind, array in arrays.items():
            shape = array.shape
            special = []
            if kind == "up":
                self.chunk[kind], self.count[kind] = shape[2:], shape[0] * shape[1]
            elif kind == "down":
                self.chunk[kind] = shape[1:]
                self.count[kind] = down_chunks[1] - down_chunks[0] if down_chunks else shape[0]
            else:
                self.chunk[kind], self.count[kind] = (shape[2] // 4, shape[3]), 4
                whole = (dp // 2,) + shape[2:]
                special = [
                    pltpu.VMEM(whole, BF16),
                    pltpu.VMEM(whole, BF16),
                    pltpu.VMEM((4,) + self.chunk[kind], BF16),
                    pltpu.SemaphoreType.DMA((2,)),
                    pltpu.SemaphoreType.DMA((2, dp // 2)),
                ]
            count, chunk = self.count[kind], self.chunk[kind]
            self.out_shape += (jax.ShapeDtypeStruct((count,) + chunk, BF16),)
            self.scratch_shapes += [
                pltpu.VMEM((count,) + chunk, BF16),
                pltpu.VMEM((count // 2,) + chunk, BF16),
                pltpu.VMEM((count // 2,) + chunk, BF16),
                pltpu.VMEM((count,) + chunk, BF16),
                pltpu.SemaphoreType.DMA((2, count)),
                pltpu.SemaphoreType.DMA((2, count // 2)),
                pltpu.SemaphoreType.DMA((2, count)),
                pltpu.SemaphoreType.DMA((count // 2,)),
                pltpu.SemaphoreType.DMA,
            ] + special
        self.pairs = [(kind, p) for kind in self.kinds for p in range(self.count[kind] // 2)]

    def peers(self):
        if not self.kinds:
            return []
        mine = lax.axis_index("seq")
        middle = (mine == 1) | (mine == 2)
        return [
            ({"seq": jnp.where(middle, 3 - mine, 1 + mine // 2)}, None),
            ({"seq": jnp.where(middle, 3 * (mine - 1), mine)}, middle),
        ]

    def bind(self, refs, outs, scratch):
        self.refs = dict(zip(self.kinds, refs))
        self.outs = dict(zip(self.kinds, outs))
        self.boxes = {}
        for kind in self.kinds:
            held = 14 if kind in self.dense else 9
            self.boxes[kind], scratch = scratch[:held], scratch[held:]
        self.me, self.mine = lax.axis_index("dp"), lax.axis_index("seq")
        self.middle = (self.mine == 1) | (self.mine == 2)
        self.inner = {"seq": jnp.where(self.middle, 3 - self.mine, 1 + self.mine // 2)}
        self.outer = {"seq": jnp.where(self.middle, 3 * (self.mine - 1), self.mine)}
        self.side = jnp.where(self.mine == 2, 1, 0)

    def source(self, kind, c):
        if kind == "up":
            return self.refs[kind].at[c // 4, lax.rem(c, 4)]
        return self.boxes[kind][11].at[c] if kind in self.dense else self.refs[kind].at[self.first + c]

    def inward(self, kind, c):
        box, sem = self.boxes[kind][0], self.boxes[kind][4]
        return remote(self.source(kind, c), box.at[c], sem.at[0, c], sem.at[1, c], self.inner)

    def across(self, kind, p):
        box, sem = self.boxes[kind], self.boxes[kind][5]
        return remote(box[2].at[p], box[1].at[p], sem.at[0, p], sem.at[1, p], self.inner)

    def outward(self, kind, c):
        box, sem = self.boxes[kind][3], self.boxes[kind][6]
        return remote(box.at[c], box.at[c], sem.at[0, c], sem.at[1, c], self.outer)

    def between(self, kind, c, p):
        box = self.boxes[kind]
        return remote(box[3].at[c], box[3].at[c], box[7].at[p], box[6].at[1, c], self.inner)

    def near_copy(self, kind):
        box = self.boxes[kind]
        away = self.refs[kind].at[:, 1 - lax.rem(self.me, 2)]
        return remote(away, box[9], box[12].at[0], box[12].at[1], {"dp": self.me ^ 1})

    def far(self, kind, m):
        box = self.boxes[kind]
        return remote(
            box[9].at[(self.me // 2) ^ m], box[10].at[m], box[13].at[0, m], box[13].at[1, m],
            {"dp": self.me ^ (2 * m)},
        )

    def begin(self, *kinds):
        @pl.when(jnp.logical_not(self.middle))
        def _():
            for kind in kinds:
                for c in range(self.count[kind]):
                    self.inward(kind, c).start()

    def dense_begin(self, kind):
        self.near_copy(kind).start()

    def dense_near(self, kind):
        self.near_copy(kind).wait_recv()
        box = self.boxes[kind]
        for at in range(self.dp // 2):
            box[9][at] = (
                self.refs[kind][at, lax.rem(self.me, 2)].astype(F32) + box[9][at].astype(F32)
            ).astype(BF16)
        for m in range(1, self.dp // 2):
            self.far(kind, m).start()

    def dense_far(self, kind):
        for m in range(1, self.dp // 2):
            self.far(kind, m).wait_recv()
        box = self.boxes[kind]
        rows = self.chunk[kind][0]
        for at in range(4):
            place = slice(at * rows, (at + 1) * rows)
            total = box[9][self.me // 2, place].astype(F32)
            for m in range(1, self.dp // 2):
                total += box[10][m, place].astype(F32)
            box[11][at] = total.astype(BF16)
        self.begin(kind)

    def relay(self, kind, p):
        c = 2 * p + 1 - self.side
        box = self.boxes[kind]
        self.inward(kind, c).wait_recv()
        box[2][p] = (self.source(kind, c)[...].astype(F32) + box[0][c].astype(F32)).astype(BF16)
        self.across(kind, p).start()

    def total(self, kind, p):
        c = 2 * p + self.side
        box = self.boxes[kind]
        self.inward(kind, c).wait_recv()
        self.across(kind, p).wait_recv()
        box[3][c] = (
            self.source(kind, c)[...].astype(F32) + box[0][c].astype(F32) + box[1][p].astype(F32)
        ).astype(BF16)
        self.between(kind, c, p).start()
        self.outward(kind, c).start()

    def forward(self, kind, p):
        c = 2 * p + 1 - self.side
        self.outward(kind, c).wait_recv()
        self.outward(kind, c).start()

    def ticks(self):
        count = len(self.pairs)
        if not count:
            return []

        def tick(at):
            @pl.when(self.middle)
            def _():
                for act, behind in ((self.relay, 0), (self.total, 1), (self.forward, 2)):
                    if 0 <= at - behind < count:
                        act(*self.pairs[at - behind])

        return [lambda at=at: tick(at) for at in range(count + 2)]

    def share_out(self, places):
        ticks, shared = self.ticks(), []
        for counts in places:
            group = []
            for count in counts:
                group.append(ticks[:count])
                ticks = ticks[count:]
            shared.append(group)
        return (*shared, ticks)

    def finish(self):
        if not self.kinds:
            return

        @pl.when(jnp.logical_not(self.middle))
        def _():
            for kind in self.kinds:
                for c in range(self.count[kind]):
                    self.outward(kind, c).wait_recv()
                    self.inward(kind, c).wait_send()

        copies = [
            pltpu.make_async_copy(self.boxes[kind][3], self.outs[kind], self.boxes[kind][8]) for kind in self.kinds
        ]
        for copy in copies:
            copy.start()

        @pl.when(self.middle)
        def _():
            for kind, p in self.pairs:
                self.across(kind, p).wait_send()
                self.between(kind, 2 * p + self.side, p).wait_send()
                self.outward(kind, 2 * p).wait_send()
                self.outward(kind, 2 * p + 1).wait_send()

        for kind in self.dense:
            self.near_copy(kind).wait_send()
            for m in range(1, self.dp // 2):
                self.far(kind, m).wait_send()
        for copy in copies:
            copy.wait()


def sum_weights_plainly(dp, down, up, dense):
    dense = lax.psum_scatter(dense.reshape(dp, -1, dense.shape[-1]), "dp", scatter_dimension=0, tiled=True)
    up = lax.all_to_all(up, "dp", split_axis=1, concat_axis=1, tiled=True)
    experts, _, quarters, r, hid = up.shape
    up = jnp.transpose(up.reshape(experts, dp, quarters * r, hid), (0, 2, 1, 3))
    return lax.psum(down, "seq"), lax.psum(up.reshape(experts, quarters * r, -1), "seq"), lax.psum(dense, "seq")


def experts_backward(grad, blocks, act, slope, up, down, plan, job, leaving=None):
    rows, width = grad.shape
    experts, _, hid = up.shape
    wide = experts * hid
    size = plan.dp
    group = Group(size)
    swap = Swap(plan)
    extra = [] if leaving is None else [leaving]

    def kernel(*refs):
        (grad_ref, blocks_ref, act_ref, slope_ref, up_ref, down_ref), refs = refs[:6], refs[6:]
        if extra:
            leaving_ref, refs = refs[0], refs[1:]
        job_refs, refs = refs[: len(job.args)], refs[len(job.args) :]
        (out_ref, tail_ref, up_out, down_out), refs = refs[:4], refs[4:]
        if extra:
            left_ref, refs = refs[0], refs[1:]
        job_outs, refs = refs[: len(job.args)], refs[len(job.args) :]
        slots, blocks, facts, act, slope, weighed, scaled, pre, flat, load_sem = refs[:10]
        refs = refs[10:]
        scratch, refs = refs[:13], refs[13:]
        if extra:
            (left, left_sem), refs = refs[:2], refs[2:]
        job.bind(job_refs, job_outs, refs)
        in_steps, in_sums, before, between, rest = job.share_out(EXPERT_TICKS)

        def loads(at):
            two = lax.rem(at, 2)
            slot = 2 * group.pair_at(at // 2) + two
            place = pl.ds(pl.multiple_of(slot * rows, 16), rows)
            return (
                pltpu.make_async_copy(blocks_ref.at[slot, pl.ds(0, rows)], blocks.at[place], load_sem.at[two, 0]),
                pltpu.make_async_copy(act_ref.at[slot], act.at[two], load_sem.at[two, 1]),
                pltpu.make_async_copy(slope_ref.at[slot], slope.at[two], load_sem.at[two, 2]),
                pltpu.make_async_copy(blocks_ref.at[slot, pl.ds(rows, 16)], facts.at[two], load_sem.at[two, 3]),
            )

        for load in loads(0):
            load.start()
        greet(*group.peers(), *job.peers(), *(swap.peers() if extra else []))
        slots[0] = grad_ref[...]
        if extra:
            swap.start(leaving_ref, left, left_sem)
        for expert in range(experts):
            flat[:, expert * hid : (expert + 1) * hid] = up_ref[expert]
        lane = lax.broadcasted_iota(jnp.int32, (16, wide), 1) // hid
        pick = (lane == lax.broadcasted_iota(jnp.int32, (16, wide), 0)).astype(F32).astype(BF16)

        def compute(slot, at):
            two = lax.rem(at, 2)

            @pl.when(at + 1 < size)
            def _():
                for load in loads(at + 1):
                    load.start()

            for load in loads(at):
                load.wait()
            gates = jnp.transpose(join_rows(facts[two]))[:rows]
            place = pl.ds(pl.multiple_of(slot * rows, 16), rows)
            for expert in range(experts):
                cols = slice(expert * hid, (expert + 1) * hid)
                gate = gates[:, expert : expert + 1]
                pull = dot(slots[slot], down_ref[cols, :], NT)
                value = act[two, :, cols].astype(F32)
                weighed[:, cols] = (pull * value).astype(BF16)
                scaled[place, cols] = (value * gate).astype(BF16)
                pre[place, cols] = (pull * gate * slope[two, :, cols].astype(F32)).astype(BF16)
            if job.kinds:
                pl.when(at == 0)(lambda: job.begin(*job.kinds))
                for step, ticks in enumerate(in_steps):
                    for tick in ticks:
                        pl.when(at == step)(tick)
            by_expert = pad_lanes(dot(pick, weighed[...], NT)[:8], width)
            return dot(pre[place, :], flat[...], NT), by_expert

        group.run(slots, scratch, rows, 16, compute)

        def weight_sums(expert, carry):
            cols = pl.ds(pl.multiple_of(expert * hid, 128), hid)
            down_out[cols, :] = dot(scaled[:, cols], slots[...].reshape(size * rows, width), TN).astype(BF16)
            up_out[expert] = dot(blocks[...], pre[:, cols], TN).astype(BF16)
            for step, ticks in enumerate(in_sums):
                for tick in ticks:
                    pl.when(expert == step)(tick)
            return carry

        lax.fori_loop(0, experts, weight_sums, 0)
        for tick in before[0]:
            tick()
        group.collect(between)
        out_ref[...] = group.own[0]
        tail_ref[...] = group.own_tail[0]
        for tick in rest:
            tick()
        job.finish()
        if extra:
            swap.wait(leaving_ref, left, left_sem)
            left_ref[...] = left[...]

    left_shape = [] if leaving is None else [jax.ShapeDtypeStruct(leaving.shape, BF16)]
    left_scratch = [
        pltpu.VMEM((plan.images, plan.piece, width), BF16),
        pltpu.SemaphoreType.DMA((2, plan.images)),
    ]
    return pl.pallas_call(
        kernel,
        out_shape=(
            jax.ShapeDtypeStruct((rows, width), F32),
            jax.ShapeDtypeStruct((8, width), F32),
            jax.ShapeDtypeStruct((experts, width, hid), BF16),
            jax.ShapeDtypeStruct((wide, width), BF16),
            *left_shape,
            *job.out_shape,
        ),
        in_specs=[in_vmem(), in_any(), in_any(), in_any(), in_vmem(), in_vmem()]
        + [in_vmem()] * (len(extra) + len(job.args)),
        out_specs=(in_vmem(),) * (4 + len(extra)) + (in_any(),) * len(job.args),
        scratch_shapes=[
            pltpu.VMEM((size, rows, width), BF16),
            pltpu.VMEM((size * rows, width), BF16),
            pltpu.VMEM((2, 16, width), BF16),
            pltpu.VMEM((2, rows, wide), BF16),
            pltpu.VMEM((2, rows, wide), BF16),
            pltpu.VMEM((rows, wide), BF16),
            pltpu.VMEM((size * rows, wide), BF16),
            pltpu.VMEM((size * rows, wide), BF16),
            pltpu.VMEM((width, wide), BF16),
            pltpu.SemaphoreType.DMA((2, 4)),
        ]
        + group.scratch(rows, 16, width)
        + (left_scratch if extra else [])
        + job.scratch_shapes,
        compiler_params=pltpu.CompilerParams(
            collective_id=3 if job.kinds else 2, has_side_effects=True, vmem_limit_bytes=VMEM_LIMIT
        ),
        name="experts_backward_and_sums" if job.kinds else "experts_backward",
    )(grad, blocks, act, slope, up, down, *extra, *job.args)


def attention_forward(plan, level, expert_in, later=None, entry=None):
    first = entry is not None
    share, size, rows = plan.share, plan.dp, plan.rows
    swap = Swap(plan)
    levels, experts, strip, hidden = expert_in.shape
    spread = Spread(size)
    width = strip * size
    columns = (entry or later)[1 + first].shape[-1]
    keys_len = rows * share
    heads = width // HEAD
    hid = hidden // size

    def kernel(in_ref, *refs):
        taken, refs = refs[:4], refs[4:]
        (message, middle, queries, kv, log_total, mixed, gates_ref, up_ref), refs = refs[:8], refs[8:]
        if first:
            (grad, grad_low, state_ref, chosen_all, length_ref, dense_out), refs = refs[:6], refs[6:]
        (all_kv, values_t, up_all, whole, parts, send, recv, save, up_send, up_recv), refs = refs[:10], refs[10:]
        bring = pltpu.make_async_copy(in_ref.at[level], whole, save)
        bring.start()
        me = lax.axis_index("dp")
        part = lax.rem(me, share)
        greet(*[({"dp": me ^ r}, None) for r in range(1, size)], *(swap.peers() if first else []))

        def shift(r):
            return remote(
                parts.at[me ^ r], up_all.at[:, pl.ds(pl.multiple_of(me * strip, 16), strip)],
                up_send.at[r], up_recv.at[r], {"dp": me ^ r},
            )

        if first:
            tokens_ref, facts_ref, dense_ref, cot_ref = taken
            tok, fact, cot, dense_all, tok_sem, fact_sem, cot_sem, keep_sem, *sems = refs
            dense_all[pl.ds(pl.multiple_of(me * strip, 16), strip)] = dense_ref[...]
            spread.bind(Strips(dense_all, strip), sems)
            spread.start()
            swap.start(facts_ref, fact, fact_sem)
            swap.start(tokens_ref, tok, tok_sem)
        bring.wait()
        for owner in range(size):
            parts[owner] = whole[:, :, owner * hid : (owner + 1) * hid]
        up_all[:, pl.ds(pl.multiple_of(me * strip, 16), strip)] = parts[me]
        if first:
            for pair in spread.order[1:]:
                spread.arrive(pair)
            for r in range(1, size):
                shift(r).start()
            swap.start(cot_ref, cot, cot_sem)
            swap.wait(facts_ref, fact, fact_sem)
            total = fact[0].astype(F32)
            for k in range(1, plan.images):
                total += fact[k].astype(F32)
            for at in range(levels):
                chosen_all[at] = total[8 * at : 8 * at + 8]
            length = total[8 * levels : 8 * levels + 1, :1] * 4.0 + total[8 * levels + 1 : 8 * levels + 2, :1]
            length_ref[...] = jnp.broadcast_to(length, length_ref.shape)
            swap.wait(tokens_ref, tok, tok_sem)
            for k in range(plan.images):
                state_ref[k * plan.piece : (k + 1) * plan.piece] = tok[k].astype(F32)
            for pair in spread.order:
                spread.handed(pair).wait_recv()
            keep_dense = pltpu.make_async_copy(dense_all, dense_out, keep_sem)
            keep_dense.start()
            dense_ref, chosen_ref = dense_all, chosen_all.at[level]
        else:
            state_ref, dense_ref, chosen_ref, length_ref = taken
            for r in range(1, size):
                shift(r).start()
        rows_of = weight_rows(dense_ref)
        unit, _ = normalize(state_ref[...])
        normed = (unit * rows_of[0:1] + rows_of[1:2]).astype(BF16)
        all_kv[part] = dot(normed, dense_ref[:, width : 3 * width]).astype(BF16)
        copies = [
            remote(all_kv.at[part], all_kv.at[part], send.at[k], recv.at[k], {"dp": me ^ k})
            for k in range(1, share)
        ]
        for copy in copies:
            copy.start()
        queries[...] = (dot(normed, dense_ref[:, :width]) * HEAD ** (-0.5)).astype(BF16)
        for copy in copies:
            copy.wait()
        saving = pltpu.make_async_copy(all_kv, kv, save)
        saving.start()
        for at in range(share):
            values_t[:, at * rows : (at + 1) * rows] = jnp.transpose(
                all_kv[at, :, width:].astype(F32)
            ).astype(BF16)
        key = lax.broadcasted_iota(jnp.int32, (keys_len, rows), 0)
        valid = key.astype(F32) < length_ref[0:1, 0:1]

        def pair_of_heads(pair, carry):
            lanes = pl.ds(pl.multiple_of(pair * 128, 128), 128)
            keys_pair = all_kv[:, :, lanes].reshape(keys_len, 128)
            queries_pair = queries[:, lanes]
            for parity in range(2):
                head = 2 * pair + parity
                scores = dot(keys_pair, one_head(queries_pair, parity), NT)
                scores = jnp.where(valid, scores, NEG)
                highest = jnp.max(scores, 0, keepdims=True)
                expo = jnp.exp(scores - highest)
                totals = row_sums(expo)
                log_total[head] = highest + jnp.log(totals)
                place = pl.ds(pl.multiple_of(head * HEAD, HEAD), HEAD)
                mixed[place, :] = (dot(values_t[place, :], expo.astype(BF16)) / totals).astype(BF16)
            return carry

        lax.fori_loop(0, heads // 2, pair_of_heads, 0)
        middle[...] = state_ref[...] + dot(mixed[...], dense_ref[:, 3 * width : 4 * width], TN)
        unit, _ = normalize(middle[...])
        normed = (unit * rows_of[2:3] + rows_of[3:4]).astype(BF16)
        message[:rows] = normed
        router = jnp.concatenate([rows_of[4:8], jnp.zeros((12, width), F32)], 0).astype(BF16)
        logits = dot(router, normed, NT)[:8]
        row = lax.broadcasted_iota(jnp.int32, logits.shape, 0)
        logits = jnp.where(row < experts, logits, NEG)
        expo = jnp.exp(logits - jnp.max(logits, 0, keepdims=True))
        gates = expo / row_sums(expo)
        gates_ref[...] = gates
        message[rows:] = split_rows(pad_lanes(gates * chosen_ref[:, :rows], width))
        saving.wait()
        for r in range(1, size):
            shift(r).wait_recv()
        keep = pltpu.make_async_copy(up_all, up_ref, save)
        keep.start()
        if first:
            swap.wait(cot_ref, cot, cot_sem)
            for k in range(plan.images):
                place = slice(k * plan.piece, (k + 1) * plan.piece)
                row = lax.broadcasted_iota(jnp.int32, (plan.piece, width), 0) + part * rows + k * plan.piece
                masked = jnp.where(row.astype(F32) < length_ref[0:1, 0:1], cot[k].astype(F32), 0.0)
                grad[place] = masked
                grad_low[place] = masked.astype(BF16)
            spread.drain()
            keep_dense.wait()
        for r in range(1, size):
            shift(r).wait_send()
        keep.wait()

    pieces = pltpu.VMEM((plan.images, plan.piece, width), BF16)
    swap_sem = pltpu.SemaphoreType.DMA((2, plan.images))
    entry_out, entry_specs, entry_scratch = (), (), []
    if first:
        entry_out = (
            jax.ShapeDtypeStruct((rows, width), F32),
            jax.ShapeDtypeStruct((rows, width), BF16),
            jax.ShapeDtypeStruct((rows, width), F32),
            jax.ShapeDtypeStruct((levels, 8, width), F32),
            jax.ShapeDtypeStruct((8, 128), F32),
            jax.ShapeDtypeStruct((width, columns), BF16),
        )
        entry_specs = (in_vmem(),) * 5 + (in_any(),)
        entry_scratch = [
            pieces,
            pltpu.VMEM(entry[1].shape, BF16),
            pieces,
            pltpu.VMEM((width, columns), BF16),
            swap_sem,
            swap_sem,
            swap_sem,
            pltpu.SemaphoreType.DMA,
        ] + spread.semaphores()
    return pl.pallas_call(
        kernel,
        out_shape=(
            jax.ShapeDtypeStruct((rows + 16, width), BF16),
            jax.ShapeDtypeStruct((rows, width), F32),
            jax.ShapeDtypeStruct((rows, width), BF16),
            jax.ShapeDtypeStruct((share, rows, 2 * width), BF16),
            jax.ShapeDtypeStruct((heads, 1, rows), F32),
            jax.ShapeDtypeStruct((width, rows), BF16),
            jax.ShapeDtypeStruct((8, rows), F32),
            jax.ShapeDtypeStruct((experts, width, hid), BF16),
            *entry_out,
        ),
        in_specs=[in_any()] + [in_vmem()] * 4,
        out_specs=(in_vmem(),) * 3 + (in_any(),) + (in_vmem(),) * 3 + (in_any(),) + entry_specs,
        scratch_shapes=[
            pltpu.VMEM((share, rows, 2 * width), BF16),
            pltpu.VMEM((width, keys_len), BF16),
            pltpu.VMEM((experts, width, hid), BF16),
            pltpu.VMEM((experts, strip, hidden), BF16),
            pltpu.VMEM((size, experts, strip, hid), BF16),
            pltpu.SemaphoreType.DMA((share,)),
            pltpu.SemaphoreType.DMA((share,)),
            pltpu.SemaphoreType.DMA,
            pltpu.SemaphoreType.DMA((size,)),
            pltpu.SemaphoreType.DMA((size,)),
        ]
        + entry_scratch,
        compiler_params=pltpu.CompilerParams(
            collective_id=5 + first, has_side_effects=True, vmem_limit_bytes=VMEM_LIMIT
        ),
        name="attention_forward_first" if first else "attention_forward",
    )(expert_in, *(entry or later))


def attention_backward(
    grad, back, back_tail, state, middle, message, gates, chosen, queries, kv, log_total, mixed,
    dense, length, up_grad, plan, job, last,
):
    rows, width = state.shape
    share = plan.share
    keys_len = rows * share
    heads = width // HEAD
    columns = dense.shape[1]
    swap = Swap(plan)
    strip = width // plan.dp
    dense_shape = (plan.dp // 2, 2, strip, columns)
    moves = up_grad is not None
    shift = Shift(up_grad) if moves else None
    moved_out = moves and not last

    def kernel(*refs):
        (
            grad_ref, back_ref, tail_ref, state_ref, mid_ref, msg_ref, gates_ref, chosen_ref, queries, kv,
            log_total, mixed, weights, length_ref,
        ), refs = refs[:14], refs[14:]
        if moves:
            up_ref, refs = refs[0], refs[1:]
        taken = len(job.args)
        job_refs, refs = refs[:taken], refs[taken:]
        (new_ref, new_low_ref, dense_ref), refs = refs[:3], refs[3:]
        if moved_out:
            moved_ref, refs = refs[0], refs[1:]
        job_outs, refs = refs[: len(job.out_shape)], refs[len(job.out_shape) :]
        (
            keys_t, normed_ref, grad_mid, grad_heads, grad_q, kv_grads, kv_got, grad_packed, send, recv,
        ), refs = refs[:10], refs[10:]
        if moves:
            moving = (up_ref, *refs[:3])
            refs = refs[3:]
        if last:
            (pieces, piece_sem), refs = refs[:2], refs[2:]
            if job.kinds:
                job_refs = (job_refs[0], moving[1], *job_refs[1:], dense_ref)
        summing = last and job.kinds
        job.bind(job_refs, job_outs, refs)
        in_heads, after_heads, after_sums, rest = job.share_out(HEAD_TICKS)
        me = lax.axis_index("dp")
        part = lax.rem(me, share)
        greet(
            *[({"dp": me ^ k}, None) for k in range(1, plan.dp if moves else share)],
            *job.peers(),
            *(swap.peers() if last else []),
        )
        if moves:
            shift.start(*moving)
        if job.kinds:
            job.begin("down")
        if summing:
            job.dense_begin(job.dense[0])
        rows_of = weight_rows(weights)
        gates = gates_ref[...]
        grad_gates = tail_ref[:, :rows] * chosen_ref[:, :rows]
        grad_logits = split_rows(gates * (grad_gates - row_sums(gates * grad_gates)))
        router = jnp.concatenate([rows_of[4:8], jnp.zeros((4, width), F32)], 0)
        twice = jnp.concatenate([router, router], 0).astype(BF16)
        grad_normed = back_ref[...] + dot(grad_logits, twice, TN)
        router_grad = dot(grad_logits, msg_ref[:rows])
        router_grad = router_grad[:8] + router_grad[8:]
        unit, inverse = normalize(mid_ref[...])
        gain_two = row_sums(grad_normed * unit)
        bias_two = row_sums(grad_normed)
        grad_mid[...] = grad_ref[...] + norm_back(grad_normed * rows_of[2:3], unit, inverse)
        low = grad_mid[...].astype(BF16)

        def put(columns_of, values):
            for at in range(plan.dp):
                dense_ref[at // 2, at % 2, :, columns_of] = values[at * strip : (at + 1) * strip].astype(BF16)

        put(slice(3 * width, 4 * width), dot(mixed[...], low))
        grad_heads[...] = dot(low, weights[:, 3 * width : 4 * width], NT).astype(BF16)
        for at in range(share):
            keys_t[:, at * rows : (at + 1) * rows] = jnp.transpose(kv[at, :, :width].astype(F32)).astype(BF16)
        key = lax.broadcasted_iota(jnp.int32, (keys_len, rows), 0)
        valid = key.astype(F32) < length_ref[0:1, 0:1]

        def pair_of_heads(pair, carry):
            lanes = pl.ds(pl.multiple_of(pair * 128, 128), 128)
            value_lanes = pl.ds(pl.multiple_of(width + pair * 128, 128), 128)
            keys_pair = kv[:, :, lanes].reshape(keys_len, 128)
            values_pair = kv[:, :, value_lanes].reshape(keys_len, 128)
            grad_k = jnp.zeros((keys_len, 128), F32)
            grad_v = jnp.zeros((keys_len, 128), F32)
            for parity in range(2):
                head = 2 * pair + parity
                query = one_head(queries[:, lanes], parity)
                pull = one_head(grad_heads[:, lanes], parity)
                scores = dot(keys_pair, query, NT)
                probs = jnp.where(valid, jnp.exp(scores - log_total[head]), 0.0)
                grad_probs = dot(values_pair, pull, NT)
                grad_scores = probs * (grad_probs - row_sums(probs * grad_probs))
                grad_scores = grad_scores.astype(BF16)
                grad_v += dot(probs.astype(BF16), pull)
                grad_k += dot(grad_scores, query)
                place = pl.ds(pl.multiple_of(head * HEAD, HEAD), HEAD)
                grad_q[place, :] = dot(keys_t[place, :], grad_scores) * HEAD ** (-0.5)
            kv_grads[:, :, lanes] = grad_k.astype(BF16).reshape(share, rows, 128)
            kv_grads[:, :, value_lanes] = grad_v.astype(BF16).reshape(share, rows, 128)
            for at, ticks in enumerate(in_heads):
                for tick in ticks:
                    pl.when(pair == at)(tick)
            if summing:
                pl.when(pair == heads // 2 - 2)(lambda: job.dense_near(job.dense[0]))
            return carry

        lax.fori_loop(0, heads // 2, pair_of_heads, 0)
        for tick in after_heads[0]:
            tick()
        copies = [
            remote(kv_grads.at[part ^ k], kv_got.at[k], send.at[k], recv.at[k], {"dp": me ^ k})
            for k in range(1, share)
        ]
        for copy in copies:
            copy.start()
        unit, inverse = normalize(state_ref[...])
        normed_ref[...] = (unit * rows_of[0:1] + rows_of[1:2]).astype(BF16)
        grad_packed[:, :width] = jnp.transpose(grad_q[...]).astype(BF16)
        for copy in copies:
            copy.wait()
        total = kv_grads[part].astype(F32)
        for k in range(1, share):
            total += kv_got[k].astype(F32)
        grad_packed[:, width:] = total.astype(BF16)
        grad_normed = dot(grad_packed[...], weights[:, : 3 * width], NT)
        for block in range(3):
            cols = slice(block * width, (block + 1) * width)
            put(cols, dot(normed_ref[...], grad_packed[:, cols], TN))
        gain_one = row_sums(grad_normed * unit)
        bias_one = row_sums(grad_normed)
        tail = jnp.concatenate([gain_one, bias_one, gain_two, bias_two, router_grad[:4]], 0)
        put(slice(4 * width, columns), pad_lanes(jnp.transpose(tail), columns - 4 * width))
        for tick in after_sums[0]:
            tick()
        if summing:
            job.dense_begin(job.dense[1])
            shift.arrive(*moving)
            job.begin("up")
        new = grad_mid[...] + norm_back(grad_normed * rows_of[0:1], unit, inverse)
        if last:
            for k in range(plan.images):
                new_low_ref[k] = new[k * plan.piece : (k + 1) * plan.piece].astype(BF16)
            swap.start(new_low_ref, pieces, piece_sem)
        else:
            new_low_ref[...] = new.astype(BF16)
            new_ref[...] = new
        if moved_out:
            shift.arrive(*moving)
            moved_ref[...] = moving[1][...]
        for at, tick in enumerate(rest, sum(map(sum, HEAD_TICKS))):
            if summing and at == DENSE_TICKS[0]:
                job.dense_near(job.dense[1])
            if summing and at == DENSE_TICKS[1]:
                job.dense_far(job.dense[0])
            if summing and at == DENSE_TICKS[2]:
                job.dense_far(job.dense[1])
            tick()
        job.finish()
        if moves:
            shift.drain(*moving)
        if last:
            swap.wait(new_low_ref, pieces, piece_sem)
            for k in range(plan.images):
                new_ref[k] = pieces[k].astype(F32)

    image_shape = (plan.images, plan.piece, width) if last else (rows, width)
    last_scratch = [
        pltpu.VMEM((plan.images, plan.piece, width), BF16),
        pltpu.SemaphoreType.DMA((2, plan.images)),
    ]
    return pl.pallas_call(
        kernel,
        out_shape=(
            jax.ShapeDtypeStruct(image_shape, F32),
            jax.ShapeDtypeStruct(image_shape, BF16),
            jax.ShapeDtypeStruct(dense_shape, BF16),
            *([jax.ShapeDtypeStruct(shift.shape, BF16)] if moved_out else []),
            *job.out_shape,
        ),
        in_specs=[in_vmem()] * (14 + moves + len(job.args)),
        out_specs=(in_vmem(),) * (3 + moved_out) + (in_any(),) * len(job.out_shape),
        scratch_shapes=[
            pltpu.VMEM((width, keys_len), BF16),
            pltpu.VMEM((rows, width), BF16),
            pltpu.VMEM((rows, width), F32),
            pltpu.VMEM((rows, width), BF16),
            pltpu.VMEM((width, rows), F32),
            pltpu.VMEM((share, rows, 2 * width), BF16),
            pltpu.VMEM((share, rows, 2 * width), BF16),
            pltpu.VMEM((rows, 3 * width), BF16),
            pltpu.SemaphoreType.DMA((share,)),
            pltpu.SemaphoreType.DMA((share,)),
        ]
        + (shift.scratch_shapes if moves else [])
        + (last_scratch if last else [])
        + job.scratch_shapes,
        compiler_params=pltpu.CompilerParams(
            collective_id=9 if last else 8, has_side_effects=True, vmem_limit_bytes=VMEM_LIMIT
        ),
        name="attention_backward_last" if last else "attention_backward",
    )(
        grad, back, back_tail, state, middle, message, gates, chosen, queries, kv, log_total, mixed,
        dense, length, *([up_grad] if moves else []), *job.args,
    )


def build(mesh):
    def shards(
        tokens,
        cotangent,
        routes,
        token_mask,
        ln1_gain,
        ln1_bias,
        qkv_weight,
        out_weight,
        ln2_gain,
        ln2_bias,
        router_weight,
        expert_in,
        expert_out,
    ):
        images, piece, width = tokens.shape
        levels, experts = expert_in.shape[:2]
        plan = Plan(mesh, images, token_mask.shape[1])
        rows = plan.rows
        wide = experts * expert_out.shape[2]
        lined = plan.seq == 4

        mine = lax.rem(lax.axis_index("seq"), images)
        chosen = jnp.sum((routes[..., None] == jnp.arange(experts, dtype=jnp.int32)).astype(F32), -2)
        chosen = jnp.transpose(chosen, (1, 0, 3, 2))
        at_slot = (jnp.arange(images) == mine).astype(F32)[:, None]
        chosen = (chosen[..., None, :] * at_slot).reshape(images, levels, experts, rows)
        chosen = jnp.pad(chosen, ((0, 0), (0, 0), (0, 8 - experts), (0, width - rows)))
        lengths = jnp.where(mine == 0, jnp.sum(token_mask, -1), 0)
        lengths = jnp.stack([lengths // 4, lengths % 4], -1).astype(F32)
        lengths = jnp.pad(lengths, ((0, 0), (0, 14)))[:, :, None]
        facts = jnp.concatenate(
            [chosen.reshape(images, 8 * levels, width), jnp.broadcast_to(lengths, (images, 16, width))], 1
        ).astype(BF16)

        vectors = jnp.stack([ln1_gain, ln1_bias, ln2_gain, ln2_bias], -1)
        tails = jnp.concatenate([vectors, router_weight], -1)
        tails = jnp.pad(tails, ((0, 0), (0, 0), (0, 128 - tails.shape[-1])))
        dense_own = jnp.concatenate([qkv_weight, out_weight, tails], -1)
        down_all = expert_out.reshape(levels, wide, width)

        saved = []
        for level in range(levels):
            if level:
                made = attention_forward(
                    plan, level, expert_in, later=(state, dense, chosen[level], length)
                )
            else:
                *made, grad, grad_low, state, chosen, length, dense = attention_forward(
                    plan, level, expert_in, entry=(tokens, facts, dense_own[level], cotangent)
                )
            message, middle, queries, kv, log_total, mixed, gates, up = made
            new_state, new_low, blocks, act, slope, *next_dense = experts_forward(
                message, middle, up, down_all[level], plan.dp,
                dense_own[level + 1] if level + 1 < levels else None,
            )
            attended = (
                state, middle, message, gates, chosen[level], queries, kv, log_total, mixed,
                dense, length,
            )
            dense = next_dense[0] if next_dense else None
            saved.append((attended, (blocks, act, slope, up, down_all[level])))
            state = new_state
        leaving = new_low.reshape(images, piece, width)

        sums = [None] * levels
        job = LineSums()
        for level in reversed(range(levels)):
            attended, routed = saved[level]
            last = level == 0
            back, back_tail, up_grad, down_grad, *others = experts_backward(
                grad_low, *routed, plan, job, leaving
            )
            if leaving is not None:
                output, *others = others
                leaving = None
            if job.kinds:
                downs, ups = jnp.concatenate([first_downs, others[0]]), others[1]
            up_grad = up_grad.reshape(experts, plan.dp, 4, width // plan.dp // 4, -1)
            down_grad = down_grad.reshape(16, wide // 16, width)
            job = LineSums(plan.dp, (0, 8), down=down_grad) if lined else LineSums()
            if lined and last:
                more = {} if level + 1 == levels else {"dense_more": dense_grad}
                job = LineSums(
                    plan.dp,
                    None,
                    down=down_grad,
                    up=jax.ShapeDtypeStruct(Shift(up_grad).shape, BF16),
                    **more,
                    dense=jax.ShapeDtypeStruct((plan.dp // 2, 2, width // plan.dp, dense_own.shape[-1]), BF16),
                )
            grad, grad_low, dense_grad, *others = attention_backward(
                grad, back, back_tail, *attended, up_grad if lined else None, plan, job, last
            )
            if not lined:
                sums[level] = sum_weights_plainly(plan.dp, down_grad, up_grad, dense_grad)
            elif last:
                sums[level] = (others[0], others[1], others[-1])
                sums[level + 1] = (downs, ups, others[2])
            else:
                first_downs = others[1]
                job = LineSums(plan.dp, (8, 16), down=down_grad, up=others[0])
        down_grad, up_grad, dense_grad = (
            jnp.stack([item.reshape(like.shape[1:]) for item in items]).astype(F32)
            for items, like in zip(zip(*sums), (expert_out, expert_in, dense_own))
        )
        return (
            output,
            grad,
            dense_grad[..., 4 * width],
            dense_grad[..., 4 * width + 1],
            dense_grad[..., : 3 * width],
            dense_grad[..., 3 * width : 4 * width],
            dense_grad[..., 4 * width + 2],
            dense_grad[..., 4 * width + 3],
            dense_grad[..., 4 * width + 4 : 4 * width + 4 + experts],
            up_grad,
            down_grad,
        )

    return shards


def solution(mesh):
    return jax.shard_map(
        build(mesh),
        mesh=mesh,
        in_specs=(
            P("dp", "seq", None),
            P("dp", "seq", None),
            P(None, "dp", "seq", None),
            P("dp", None),
            P(None, "dp"),
            P(None, "dp"),
            P(None, "dp", None),
            P(None, "dp", None),
            P(None, "dp"),
            P(None, "dp"),
            P(None, "dp", None),
            P(None, None, "dp", None),
            P(None, None, "dp", None),
        ),
        out_specs=(
            P("dp", "seq", None),
            P("dp", "seq", None),
            P(None, "dp"),
            P(None, "dp"),
            P(None, "dp", None),
            P(None, "dp", None),
            P(None, "dp"),
            P(None, "dp"),
            P(None, "dp", None),
            P(None, None, "dp", None),
            P(None, None, "dp", None),
        ),
        check_vma=False,
    )
```

```python
import itertools

import jax
import jax.numpy as jnp
from jax import lax
from jax.experimental import pallas as pl
from jax.experimental.pallas import tpu as pltpu
from jax.sharding import PartitionSpec as P

HEAD = 64
EPS = 1e-06
NEG = -1e30
F32 = jnp.float32
BF16 = jnp.bfloat16
MESH = pl.DeviceIdType.MESH
VMEM_LIMIT = 60 * 1024 * 1024
EXPERT_TICKS = ((0, 2, 1, 1, 1, 1, 1, 1), (1, 0, 1, 0), (1,), (1, 1, 0))
HEAD_TICKS = ((0, 1, 1, 1), (1,), (1,))
DENSE_TICKS = (5, 6, 14)
EARLY_CHUNKS = 4
NT = ((1,), (1,))
TN = ((0,), (0,))


def normalize(values):
    center = values - jnp.mean(values, -1, keepdims=True)
    inverse = lax.rsqrt(jnp.mean(center * center, -1, keepdims=True) + EPS)
    return center * inverse, inverse


def norm_back(grad_unit, unit, inverse):
    return inverse * (
        grad_unit
        - jnp.mean(grad_unit, -1, keepdims=True)
        - unit * jnp.mean(grad_unit * unit, -1, keepdims=True)
    )


def in_vmem():
    return pl.BlockSpec(memory_space=pltpu.VMEM)


def in_any():
    return pl.BlockSpec(memory_space=pl.ANY)


def greet(*peers):
    barrier = pltpu.get_barrier_semaphore()
    count = 0
    for peer, condition in peers:

        def signal(peer=peer):
            pl.semaphore_signal(barrier, inc=1, device_id=peer, device_id_type=MESH)

        if condition is None:
            signal()
            count += 1
        else:
            pl.when(condition)(signal)
            count += condition.astype(jnp.int32)
    pl.semaphore_wait(barrier, count)


def remote(src, dst, send, recv, peer):
    return pltpu.make_async_remote_copy(
        src_ref=src, dst_ref=dst, send_sem=send, recv_sem=recv, device_id=peer, device_id_type=MESH
    )


def split_rows(rows8):
    high = rows8.astype(BF16).astype(F32)
    return jnp.concatenate([high, rows8 - high], 0).astype(BF16)


def join_rows(rows16):
    wide = rows16.astype(F32)
    return wide[:8] + wide[8:]


def gelu_parts(u):
    bell = jnp.exp2(u * u * -0.7213475204444817)
    t = pl.reciprocal(1.0 + 0.23164190 * jnp.abs(u), approx=True)
    poly = t * (
        0.127414796 + t * (-0.142248368 + t * (0.7107068705 + t * (-0.7265760135 + t * 0.5307027145)))
    )
    half = poly * bell
    cdf = jnp.where(u >= 0, 1.0 - half, half)
    return u * cdf, cdf + u * 0.3989422804014327 * bell


def dot(left, right, dims=((1,), (0,))):
    return lax.dot_general(left, right, (dims, ((), ())), preferred_element_type=F32)


def row_sums(values):
    return jnp.sum(values, 0, keepdims=True)


def pad_lanes(values, lanes):
    if values.shape[1] == lanes:
        return values
    return jnp.concatenate([values, jnp.zeros((values.shape[0], lanes - values.shape[1]), values.dtype)], 1)


def one_head(pair, parity):
    lane = lax.broadcasted_iota(jnp.int32, pair.shape, 1) // HEAD
    return jnp.where(lane == parity, pair.astype(F32), 0.0).astype(BF16)


def weight_rows(dense_ref):
    width = dense_ref.shape[0]
    return jnp.transpose(dense_ref[:, 4 * width :].astype(F32))


def lay_strip(refs, level, dense, place):
    packed, out, router, *vectors = refs
    strip, width = out.shape[1:]
    dense[place, : 3 * width] = packed[level]
    dense[place, 3 * width : 4 * width] = out[level]
    rows = [vector[...].astype(F32)[level : level + 1] for vector in vectors]
    rows = jnp.concatenate(rows + [jnp.zeros((4, strip), F32)], 0)
    columns = jnp.transpose(pad_lanes(rows, 128))[:strip, :4]
    tail = jnp.concatenate([columns, router[level].astype(F32)], 1)
    dense[place, 4 * width :] = pad_lanes(tail, 128).astype(BF16)


class Plan:
    def __init__(self, mesh, images, length):
        self.dp = mesh.shape["dp"]
        self.seq = mesh.shape["seq"]
        self.images = images
        self.piece = length // self.seq
        self.share = self.seq // images
        self.rows = images * self.piece


class Swap:
    def __init__(self, plan):
        self.plan = plan

    def where(self, k):
        me, mine = lax.axis_index("dp"), lax.axis_index("seq")
        share, images = self.plan.share, self.plan.images
        part = lax.rem(me, share)
        peer = {"dp": me - part + mine // images, "seq": part * images + k}
        stays = (part == mine // images) & (lax.rem(mine, images) == k)
        return peer, stays

    def peers(self):
        both = [self.where(k) for k in range(self.plan.images)]
        return [(peer, jnp.logical_not(stays)) for peer, stays in both]

    def start(self, src, dst, sems):
        slot = lax.rem(lax.axis_index("seq"), self.plan.images)
        for k in range(self.plan.images):
            peer, stays = self.where(k)

            @pl.when(jnp.logical_not(stays))
            def _():
                remote(src.at[k], dst.at[slot], sems.at[0, k], sems.at[1, slot], peer).start()

            @pl.when(stays)
            def _():
                pltpu.make_async_copy(src.at[k], dst.at[k], sems.at[1, k]).start()

    def wait(self, src, dst, sems):
        for k in range(self.plan.images):
            peer, stays = self.where(k)
            moved = remote(src.at[k], dst.at[k], sems.at[0, k], sems.at[1, k], peer)

            @pl.when(jnp.logical_not(stays))
            def _():
                moved.wait_recv()
                moved.wait_send()

            @pl.when(stays)
            def _():
                pltpu.make_async_copy(src.at[k], dst.at[k], sems.at[1, k]).wait()


class Slots:
    def __init__(self, ref):
        self.ref = ref
        self.rows = ref.shape[1]

    def at(self, slot, part, device):
        return self.ref.at[slot, part]


class Strips:
    def __init__(self, ref, rows):
        self.ref = ref
        self.rows = rows

    def at(self, slot, part, device):
        first = pl.multiple_of((device ^ slot) * self.rows + part.start, 16)
        return self.ref.at[pl.ds(first, part.size)]


class Spread:
    def __init__(self, size):
        self.size = size
        self.pairs = size // 2
        self.order = sorted(range(self.pairs), key=lambda pair: (bin(pair).count("1"), pair))
        self.bits = [1 << k for k in range(self.pairs.bit_length() - 1)]

    def ways(self, pair):
        return (pair & -pair, 1 << (pair.bit_length() - 1))

    def pair_at(self, turn):
        if isinstance(turn, int):
            return self.order[turn]
        pair = turn
        for at, value in enumerate(self.order):
            if at != value:
                pair = jnp.where(turn == at, value, pair)
        return pair

    def peers(self):
        me = lax.axis_index("dp")
        return [({"dp": me ^ r}, None) for r in (1, *range(2, self.size, 2))]

    def semaphores(self):
        return [
            pltpu.SemaphoreType.DMA((2, self.pairs)),
            pltpu.SemaphoreType.DMA((2, self.size)),
            pltpu.SemaphoreType.DMA((self.pairs,)),
        ]

    def bind(self, slots, semaphores):
        self.slots = slots
        self.send, self.recv, self.hand = semaphores
        self.me = lax.axis_index("dp")
        cut = slots.rows // 32 * 16
        self.whole = pl.ds(0, slots.rows)
        self.halves = (pl.ds(0, cut), pl.ds(cut, slots.rows - cut))

    def move(self, slot, to_slot, part, peer, send, recv):
        return remote(
            self.slots.at(slot, part, self.me), self.slots.at(to_slot, part, peer), send, recv, {"dp": peer}
        )

    def block(self, pair):
        slot = 2 * pair
        return self.move(0, slot, self.whole, self.me ^ slot, self.send.at[0, pair], self.recv.at[0, slot])

    def half_block(self, pair, half):
        way = self.ways(pair)[half]
        return self.move(
            2 * (pair ^ way), 2 * pair, self.halves[half], self.me ^ (2 * way),
            self.send.at[half, pair], self.recv.at[half, 2 * pair],
        )

    def handed(self, pair):
        slot = 2 * pair
        return self.move(
            slot, slot + 1, self.whole, self.me ^ 1, self.hand.at[pair], self.recv.at[0, slot + 1]
        )

    def start(self):
        self.handed(0).start()
        for bit in self.bits:
            self.block(bit).start()

    def arrive(self, pair):
        for known in range(1, self.pairs):

            @pl.when(jnp.asarray(pair) == known)
            def _():
                if known in self.bits:
                    self.block(known).wait_recv()
                else:
                    self.half_block(known, 0).wait_recv()
                    self.half_block(known, 1).wait_recv()
                for far in range(1, self.pairs):
                    for half, way in enumerate(self.ways(far)):
                        if far not in self.bits and far ^ way == known:
                            self.half_block(far, half).start()

        self.handed(pair).start()

    def drain(self):
        for pair in range(self.pairs):
            self.handed(pair).wait_send()
            if pair in self.bits:
                self.block(pair).wait_send()
            elif pair:
                self.half_block(pair, 0).wait_send()
                self.half_block(pair, 1).wait_send()


class Group(Spread):
    def scratch(self, rows, tail, width):
        full = rows + tail
        return self.semaphores() + [
            pltpu.VMEM((self.pairs, rows, width), F32),
            pltpu.VMEM((self.pairs, 8, width), F32),
            pltpu.VMEM((self.pairs, full, width), BF16),
            pltpu.VMEM((self.pairs, full, width), BF16),
            pltpu.VMEM((self.pairs, full, width), BF16),
            pltpu.VMEM((self.pairs, full, width), BF16),
            pltpu.SemaphoreType.DMA((self.pairs,)),
            pltpu.SemaphoreType.DMA((self.pairs,)),
            pltpu.SemaphoreType.DMA((self.pairs,)),
            pltpu.SemaphoreType.DMA((self.pairs,)),
        ]

    def given(self, pair):
        return remote(
            self.give.at[pair], self.take.at[pair], self.g_send.at[pair], self.g_recv.at[pair], {"dp": self.me ^ 1}
        )

    def paid(self, pair):
        return remote(
            self.pay.at[pair], self.due.at[pair], self.p_send.at[pair], self.p_recv.at[pair],
            {"dp": self.me ^ (2 * pair)},
        )

    def run(self, slots, scratch, rows, tail, compute):
        self.bind(Slots(slots), scratch[:3])
        (
            self.own, self.own_tail, self.give, self.take, self.pay, self.due,
            self.g_send, self.g_recv, self.p_send, self.p_recv,
        ) = scratch[3:]
        self.sizes = rows, tail

        def settle(pair):
            self.given(pair).wait_recv()
            self.own[pair] += self.take[pair, :rows].astype(F32)
            if tail:
                self.own_tail[pair] += join_rows(self.take[pair, rows:])

            @pl.when(jnp.asarray(pair) > 0)
            def _():
                self.pay[pair, :rows] = self.own[pair].astype(BF16)
                if tail:
                    self.pay[pair, rows:] = split_rows(self.own_tail[pair])
                self.paid(pair).start()

        self.start()

        def step(at, carry):
            turn = at // 2
            pair = self.pair_at(turn)
            odd = lax.rem(at, 2) == 0
            slot = 2 * pair + 1 - lax.rem(at, 2)

            @pl.when(odd & (turn == 1))
            def _():
                for bit in self.bits:
                    self.arrive(bit)

            @pl.when(odd & (turn > len(self.bits)))
            def _():
                self.arrive(pair)

            @pl.when(odd)
            def _():
                self.handed(pair).wait_recv()

            total, total_tail = compute(slot, at)

            @pl.when(odd)
            def _():
                self.give[pair, :rows] = total.astype(BF16)
                if tail:
                    self.give[pair, rows:] = split_rows(total_tail)
                self.given(pair).start()

            @pl.when(jnp.logical_not(odd))
            def _():
                self.own[pair] = total
                if tail:
                    self.own_tail[pair] = total_tail
                settle(pair)

            return carry

        lax.fori_loop(0, self.size, step, 0)

    def collect(self, between=()):
        rows, tail = self.sizes
        for pair, steps in zip(self.order[1:], itertools.chain(between, itertools.repeat(()))):
            self.paid(pair).wait_recv()
            for step in steps:
                step()
            self.own[0] += self.due[pair, :rows].astype(F32)
            if tail:
                self.own_tail[0] += join_rows(self.due[pair, rows:])
        for pair in range(self.pairs):
            self.given(pair).wait_send()
            if pair:
                self.paid(pair).wait_send()
        self.drain()


def experts_forward(message, middle, up, down, level, size, strips=()):
    rows, width = middle.shape
    experts, _, hid = up.shape
    wide = experts * hid
    group = Group(size)
    spread = Spread(size)
    extra = bool(strips)
    strip = width // size

    def kernel(msg_ref, mid_ref, up_ref, down_all, *refs):
        strip_refs, refs = refs[: len(strips)], refs[len(strips) :]
        (out_ref, low_ref, all_ref, act_ref, slope_ref), refs = refs[:5], refs[5:]
        if extra:
            dense_ref, refs = refs[0], refs[1:]
        (down_ref, down_sem, slots, act, slope, scaled, save_sem), refs = refs[:7], refs[7:]
        scratch, refs = refs[:13], refs[13:]
        bring = pltpu.make_async_copy(down_all.at[level], down_ref, down_sem)
        bring.start()
        if extra:
            dense_all, keep_sem, *sems = refs
            me = lax.axis_index("dp")
            spread.bind(Strips(dense_all, strip), sems)
            lay_strip(strip_refs, level + 1, dense_all, pl.ds(pl.multiple_of(me * strip, 16), strip))
        greet(*group.peers())
        slots[0] = msg_ref[...]
        bring.wait()

        def saves(slot):
            return (
                pltpu.make_async_copy(slots.at[slot], all_ref.at[slot], save_sem.at[slot, 0]),
                pltpu.make_async_copy(act.at[slot], act_ref.at[slot], save_sem.at[slot, 1]),
                pltpu.make_async_copy(slope.at[slot], slope_ref.at[slot], save_sem.at[slot, 2]),
            )

        def compute(slot, at):
            gates = jnp.transpose(join_rows(slots[slot, rows:]))[:rows]
            for expert in range(experts):
                cols = slice(expert * hid, (expert + 1) * hid)
                value, grade = gelu_parts(dot(slots[slot, :rows], up_ref[expert]))
                value = value.astype(BF16)
                act[slot, :, cols] = value
                slope[slot, :, cols] = grade.astype(BF16)
                scaled[:, cols] = (value.astype(F32) * gates[:, expert : expert + 1]).astype(BF16)
            for save in saves(slot):
                save.start()
            if extra:
                pl.when(at == 0)(spread.start)
                for turn, pair in enumerate(spread.order[1:], 1):
                    pl.when(at == (3 if pair in spread.bits else 5))(lambda pair=pair: spread.arrive(pair))
            return dot(scaled[...], down_ref[...]), None

        group.run(slots, scratch, rows, 0, compute)
        if extra:
            for pair in spread.order:
                spread.handed(pair).wait_recv()
            keep = pltpu.make_async_copy(dense_all, dense_ref, keep_sem)
            keep.start()
        group.collect()
        out = mid_ref[...] + group.own[0]
        out_ref[...] = out
        low_ref[...] = out.astype(BF16)
        for slot in range(size):
            for save in saves(slot):
                save.wait()
        if extra:
            spread.drain()
            keep.wait()

    return pl.pallas_call(
        kernel,
        out_shape=(
            jax.ShapeDtypeStruct((rows, width), F32),
            jax.ShapeDtypeStruct((rows, width), BF16),
            jax.ShapeDtypeStruct((size, rows + 16, width), BF16),
            jax.ShapeDtypeStruct((size, rows, wide), BF16),
            jax.ShapeDtypeStruct((size, rows, wide), BF16),
            *([jax.ShapeDtypeStruct((width, 4 * width + 128), BF16)] if extra else []),
        ),
        in_specs=[in_vmem()] * 3 + [in_any()] + [in_vmem()] * len(strips),
        out_specs=(in_vmem(), in_vmem(), in_any(), in_any(), in_any()) + (in_any(),) * extra,
        scratch_shapes=[
            pltpu.VMEM((wide, width), BF16),
            pltpu.SemaphoreType.DMA,
            pltpu.VMEM((size, rows + 16, width), BF16),
            pltpu.VMEM((size, rows, wide), BF16),
            pltpu.VMEM((size, rows, wide), BF16),
            pltpu.VMEM((rows, wide), BF16),
            pltpu.SemaphoreType.DMA((size, 3)),
        ]
        + group.scratch(rows, 0, width)
        + (
            [pltpu.VMEM((width, 4 * width + 128), BF16), pltpu.SemaphoreType.DMA]
            + spread.semaphores()
            if extra
            else []
        ),
        compiler_params=pltpu.CompilerParams(
            collective_id=10 if extra else 1, has_side_effects=True, vmem_limit_bytes=VMEM_LIMIT
        ),
        name="experts_forward",
    )(message, middle, up, down, *strips)


class Shift:
    def __init__(self, source):
        experts, self.dp, quarters, r, self.hid = source.shape
        self.experts = experts
        self.shape = (experts, quarters, r, self.dp * self.hid)
        self.scratch_shapes = [
            pltpu.VMEM(self.shape, BF16),
            pltpu.VMEM((self.dp, experts, quarters, r, self.hid), BF16),
            pltpu.SemaphoreType.DMA((2, self.dp)),
        ]

    def copy(self, src, dst, box, sems, r):
        me = lax.axis_index("dp")
        return remote(src.at[:, me ^ r], box.at[me], sems.at[0, r], sems.at[1, r], {"dp": me ^ r})

    def start(self, *refs):
        for r in range(1, self.dp):
            self.copy(*refs, r).start()

    def arrive(self, src, dst, box, sems):
        me = lax.axis_index("dp")
        box[me] = src[:, me]
        for r in range(1, self.dp):
            self.copy(src, dst, box, sems, r).wait_recv()
        for owner in range(self.dp):
            dst[:, :, :, owner * self.hid : (owner + 1) * self.hid] = box[owner]

    def drain(self, *refs):
        for r in range(1, self.dp):
            self.copy(*refs, r).wait_send()


class LineSums:
    def __init__(self, dp=0, down_chunks=None, kept=(), **arrays):
        self.dp = dp
        self.kept = kept
        self.first = down_chunks[0] if down_chunks else 0
        self.kinds = list(arrays)
        self.args = tuple(array for array in arrays.values() if not isinstance(array, jax.ShapeDtypeStruct))
        self.dense = [kind for kind in self.kinds if kind.startswith("dense")]
        self.chunk, self.count = {}, {}
        self.out_shape, self.scratch_shapes = (), []
        for kind, array in arrays.items():
            shape = array.shape
            special = []
            if kind == "up":
                self.chunk[kind], self.count[kind] = shape[2:], shape[0] * shape[1]
            elif kind == "down":
                self.chunk[kind] = shape[1:]
                self.count[kind] = down_chunks[1] - down_chunks[0] if down_chunks else shape[0]
            else:
                self.chunk[kind], self.count[kind] = (shape[2] // 4, shape[3]), 4
                whole = (dp // 2,) + shape[2:]
                special = [
                    pltpu.VMEM(whole, BF16),
                    pltpu.VMEM(whole, BF16),
                    pltpu.VMEM((4,) + self.chunk[kind], BF16),
                    pltpu.SemaphoreType.DMA((2,)),
                    pltpu.SemaphoreType.DMA((2, dp // 2)),
                ]
            count, chunk = self.count[kind], self.chunk[kind]
            if kind not in kept:
                self.out_shape += (jax.ShapeDtypeStruct((count,) + chunk, BF16),)
            self.scratch_shapes += [
                pltpu.VMEM((count,) + chunk, BF16),
                pltpu.VMEM((count // 2,) + chunk, BF16),
                pltpu.VMEM((count // 2,) + chunk, BF16),
                pltpu.VMEM((count,) + chunk, BF16),
                pltpu.SemaphoreType.DMA((2, count)),
                pltpu.SemaphoreType.DMA((2, count // 2)),
                pltpu.SemaphoreType.DMA((2, count)),
                pltpu.SemaphoreType.DMA((count // 2,)),
                pltpu.SemaphoreType.DMA,
            ] + special
        self.pairs = [(kind, p) for kind in self.kinds for p in range(self.count[kind] // 2)]

    def peers(self):
        if not self.kinds:
            return []
        mine = lax.axis_index("seq")
        middle = (mine == 1) | (mine == 2)
        return [
            ({"seq": jnp.where(middle, 3 - mine, 1 + mine // 2)}, None),
            ({"seq": jnp.where(middle, 3 * (mine - 1), mine)}, middle),
        ]

    def bind(self, refs, outs, scratch):
        self.refs = dict(zip(self.kinds, refs))
        self.outs = dict(zip((kind for kind in self.kinds if kind not in self.kept), outs))
        self.boxes = {}
        for kind in self.kinds:
            held = 14 if kind in self.dense else 9
            self.boxes[kind], scratch = scratch[:held], scratch[held:]
        self.me, self.mine = lax.axis_index("dp"), lax.axis_index("seq")
        self.middle = (self.mine == 1) | (self.mine == 2)
        self.inner = {"seq": jnp.where(self.middle, 3 - self.mine, 1 + self.mine // 2)}
        self.outer = {"seq": jnp.where(self.middle, 3 * (self.mine - 1), self.mine)}
        self.side = jnp.where(self.mine == 2, 1, 0)

    def source(self, kind, c):
        if kind == "up":
            return self.refs[kind].at[c // 4, lax.rem(c, 4)]
        return self.boxes[kind][11].at[c] if kind in self.dense else self.refs[kind].at[self.first + c]

    def inward(self, kind, c):
        box, sem = self.boxes[kind][0], self.boxes[kind][4]
        return remote(self.source(kind, c), box.at[c], sem.at[0, c], sem.at[1, c], self.inner)

    def across(self, kind, p):
        box, sem = self.boxes[kind], self.boxes[kind][5]
        return remote(box[2].at[p], box[1].at[p], sem.at[0, p], sem.at[1, p], self.inner)

    def outward(self, kind, c):
        box, sem = self.boxes[kind][3], self.boxes[kind][6]
        return remote(box.at[c], box.at[c], sem.at[0, c], sem.at[1, c], self.outer)

    def between(self, kind, c, p):
        box = self.boxes[kind]
        return remote(box[3].at[c], box[3].at[c], box[7].at[p], box[6].at[1, c], self.inner)

    def near_copy(self, kind):
        box = self.boxes[kind]
        away = self.refs[kind].at[:, 1 - lax.rem(self.me, 2)]
        return remote(away, box[9], box[12].at[0], box[12].at[1], {"dp": self.me ^ 1})

    def far(self, kind, m):
        box = self.boxes[kind]
        return remote(
            box[9].at[(self.me // 2) ^ m], box[10].at[m], box[13].at[0, m], box[13].at[1, m],
            {"dp": self.me ^ (2 * m)},
        )

    def begin(self, *kinds):
        @pl.when(jnp.logical_not(self.middle))
        def _():
            for kind in kinds:
                for c in range(self.count[kind]):
                    self.inward(kind, c).start()

    def dense_begin(self, kind):
        self.near_copy(kind).start()

    def dense_near(self, kind):
        self.near_copy(kind).wait_recv()
        box = self.boxes[kind]
        for at in range(self.dp // 2):
            box[9][at] = (
                self.refs[kind][at, lax.rem(self.me, 2)].astype(F32) + box[9][at].astype(F32)
            ).astype(BF16)
        for m in range(1, self.dp // 2):
            self.far(kind, m).start()

    def dense_far(self, kind):
        for m in range(1, self.dp // 2):
            self.far(kind, m).wait_recv()
        box = self.boxes[kind]
        rows = self.chunk[kind][0]
        for at in range(4):
            place = slice(at * rows, (at + 1) * rows)
            total = box[9][self.me // 2, place].astype(F32)
            for m in range(1, self.dp // 2):
                total += box[10][m, place].astype(F32)
            box[11][at] = total.astype(BF16)
        self.begin(kind)

    def relay(self, kind, p):
        c = 2 * p + 1 - self.side
        box = self.boxes[kind]
        self.inward(kind, c).wait_recv()
        box[2][p] = (self.source(kind, c)[...].astype(F32) + box[0][c].astype(F32)).astype(BF16)
        self.across(kind, p).start()

    def total(self, kind, p):
        c = 2 * p + self.side
        box = self.boxes[kind]
        self.inward(kind, c).wait_recv()
        self.across(kind, p).wait_recv()
        box[3][c] = (
            self.source(kind, c)[...].astype(F32) + box[0][c].astype(F32) + box[1][p].astype(F32)
        ).astype(BF16)
        self.between(kind, c, p).start()
        self.outward(kind, c).start()

    def forward(self, kind, p):
        c = 2 * p + 1 - self.side
        self.outward(kind, c).wait_recv()
        self.outward(kind, c).start()

    def ticks(self):
        count = len(self.pairs)
        if not count:
            return []

        def tick(at):
            @pl.when(self.middle)
            def _():
                for act, behind in ((self.relay, 0), (self.total, 1), (self.forward, 2)):
                    if 0 <= at - behind < count:
                        act(*self.pairs[at - behind])

        return [lambda at=at: tick(at) for at in range(count + 2)]

    def share_out(self, places):
        ticks, shared = self.ticks(), []
        for counts in places:
            group = []
            for count in counts:
                group.append(ticks[:count])
                ticks = ticks[count:]
            shared.append(group)
        return (*shared, ticks)

    def finish(self):
        if not self.kinds:
            return

        @pl.when(jnp.logical_not(self.middle))
        def _():
            for kind in self.kinds:
                for c in range(self.count[kind]):
                    self.outward(kind, c).wait_recv()
                    self.inward(kind, c).wait_send()

        copies = [
            pltpu.make_async_copy(self.boxes[kind][3], out, self.boxes[kind][8]) for kind, out in self.outs.items()
        ]
        for copy in copies:
            copy.start()

        @pl.when(self.middle)
        def _():
            for kind, p in self.pairs:
                self.across(kind, p).wait_send()
                self.between(kind, 2 * p + self.side, p).wait_send()
                self.outward(kind, 2 * p).wait_send()
                self.outward(kind, 2 * p + 1).wait_send()

        for kind in self.dense:
            self.near_copy(kind).wait_send()
            for m in range(1, self.dp // 2):
                self.far(kind, m).wait_send()
        for copy in copies:
            copy.wait()


def sum_weights_plainly(dp, down, up, dense):
    dense = lax.psum_scatter(dense.reshape(dp, -1, dense.shape[-1]), "dp", scatter_dimension=0, tiled=True)
    up = lax.all_to_all(up, "dp", split_axis=1, concat_axis=1, tiled=True)
    experts, _, quarters, r, hid = up.shape
    up = jnp.transpose(up.reshape(experts, dp, quarters * r, hid), (0, 2, 1, 3))
    return lax.psum(down, "seq"), lax.psum(up.reshape(experts, quarters * r, -1), "seq"), lax.psum(dense, "seq")


def experts_backward(grad, blocks, act, slope, up, down, level, plan, job, leaving=None):
    rows, width = grad.shape
    experts, _, hid = up.shape
    wide = experts * hid
    size = plan.dp
    group = Group(size)
    swap = Swap(plan)
    extra = [] if leaving is None else [leaving]

    def kernel(*refs):
        (grad_ref, blocks_ref, act_ref, slope_ref, up_ref, down_all), refs = refs[:6], refs[6:]
        if extra:
            leaving_ref, refs = refs[0], refs[1:]
        job_refs, refs = refs[: len(job.args)], refs[len(job.args) :]
        (out_ref, tail_ref, up_out, down_out), refs = refs[:4], refs[4:]
        if extra:
            left_ref, refs = refs[0], refs[1:]
        job_outs, refs = refs[: len(job.args)], refs[len(job.args) :]
        slots, blocks, facts, act, slope, weighed, scaled, pre, flat, load_sem, down_ref, down_sem = refs[:12]
        refs = refs[12:]
        bring = pltpu.make_async_copy(down_all.at[level], down_ref, down_sem)
        bring.start()
        scratch, refs = refs[:13], refs[13:]
        if extra:
            (left, left_sem), refs = refs[:2], refs[2:]
        job.bind(job_refs, job_outs, refs)
        in_steps, in_sums, before, between, rest = job.share_out(EXPERT_TICKS)

        def loads(at):
            two = lax.rem(at, 2)
            slot = 2 * group.pair_at(at // 2) + 1 - two
            place = pl.ds(pl.multiple_of(slot * rows, 16), rows)
            return (
                pltpu.make_async_copy(blocks_ref.at[slot, pl.ds(0, rows)], blocks.at[place], load_sem.at[two, 0]),
                pltpu.make_async_copy(act_ref.at[slot], act.at[two], load_sem.at[two, 1]),
                pltpu.make_async_copy(slope_ref.at[slot], slope.at[two], load_sem.at[two, 2]),
                pltpu.make_async_copy(blocks_ref.at[slot, pl.ds(rows, 16)], facts.at[two], load_sem.at[two, 3]),
            )

        for load in loads(0):
            load.start()
        greet(*group.peers(), *job.peers(), *(swap.peers() if extra else []))
        slots[0] = grad_ref[...]
        if extra:
            swap.start(leaving_ref, left, left_sem)
        for expert in range(experts):
            flat[:, expert * hid : (expert + 1) * hid] = up_ref[expert]
        bring.wait()
        lane = lax.broadcasted_iota(jnp.int32, (16, wide), 1) // hid
        pick = (lane == lax.broadcasted_iota(jnp.int32, (16, wide), 0)).astype(F32).astype(BF16)

        def compute(slot, at):
            two = lax.rem(at, 2)

            @pl.when(at + 1 < size)
            def _():
                for load in loads(at + 1):
                    load.start()

            for load in loads(at):
                load.wait()
            gates = jnp.transpose(join_rows(facts[two]))[:rows]
            place = pl.ds(pl.multiple_of(slot * rows, 16), rows)
            for expert in range(experts):
                cols = slice(expert * hid, (expert + 1) * hid)
                gate = gates[:, expert : expert + 1]
                pull = dot(slots[slot], down_ref[cols, :], NT)
                value = act[two, :, cols].astype(F32)
                weighed[:, cols] = (pull * value).astype(BF16)
                scaled[place, cols] = (value * gate).astype(BF16)
                pre[place, cols] = (pull * gate * slope[two, :, cols].astype(F32)).astype(BF16)
            if job.kinds:
                pl.when(at == 0)(lambda: job.begin(*job.kinds))
                for step, ticks in enumerate(in_steps):
                    for tick in ticks:
                        pl.when(at == step)(tick)
            by_expert = pad_lanes(dot(pick, weighed[...], NT)[:8], width)
            return dot(pre[place, :], flat[...], NT), by_expert

        group.run(slots, scratch, rows, 16, compute)

        def weight_sums(expert, carry):
            cols = pl.ds(pl.multiple_of(expert * hid, 128), hid)
            down_out[cols, :] = dot(scaled[:, cols], slots[...].reshape(size * rows, width), TN).astype(BF16)
            up_out[expert] = dot(blocks[...], pre[:, cols], TN).astype(BF16)
            for step, ticks in enumerate(in_sums):
                for tick in ticks:
                    pl.when(expert == step)(tick)
            return carry

        lax.fori_loop(0, experts, weight_sums, 0)
        for tick in before[0]:
            tick()
        group.collect(between)
        out_ref[...] = group.own[0]
        tail_ref[...] = group.own_tail[0]
        for tick in rest:
            tick()
        job.finish()
        if extra:
            swap.wait(leaving_ref, left, left_sem)
            left_ref[...] = left[...]

    left_shape = [] if leaving is None else [jax.ShapeDtypeStruct(leaving.shape, BF16)]
    left_scratch = [
        pltpu.VMEM((plan.images, plan.piece, width), BF16),
        pltpu.SemaphoreType.DMA((2, plan.images)),
    ]
    return pl.pallas_call(
        kernel,
        out_shape=(
            jax.ShapeDtypeStruct((rows, width), F32),
            jax.ShapeDtypeStruct((8, width), F32),
            jax.ShapeDtypeStruct((experts, width, hid), BF16),
            jax.ShapeDtypeStruct((wide, width), BF16),
            *left_shape,
            *job.out_shape,
        ),
        in_specs=[in_vmem(), in_any(), in_any(), in_any(), in_vmem(), in_any()]
        + [in_vmem()] * (len(extra) + len(job.args)),
        out_specs=(in_vmem(),) * (4 + len(extra)) + (in_any(),) * len(job.args),
        scratch_shapes=[
            pltpu.VMEM((size, rows, width), BF16),
            pltpu.VMEM((size * rows, width), BF16),
            pltpu.VMEM((2, 16, width), BF16),
            pltpu.VMEM((2, rows, wide), BF16),
            pltpu.VMEM((2, rows, wide), BF16),
            pltpu.VMEM((rows, wide), BF16),
            pltpu.VMEM((size * rows, wide), BF16),
            pltpu.VMEM((size * rows, wide), BF16),
            pltpu.VMEM((width, wide), BF16),
            pltpu.SemaphoreType.DMA((2, 4)),
            pltpu.VMEM((wide, width), BF16),
            pltpu.SemaphoreType.DMA,
        ]
        + group.scratch(rows, 16, width)
        + (left_scratch if extra else [])
        + job.scratch_shapes,
        compiler_params=pltpu.CompilerParams(
            collective_id=3 if job.kinds else 2, has_side_effects=True, vmem_limit_bytes=VMEM_LIMIT
        ),
        name="experts_backward_and_sums" if job.kinds else "experts_backward",
    )(grad, blocks, act, slope, up, down, *extra, *job.args)


def attention_forward(plan, level, expert_in, later=None, entry=None):
    first = entry is not None
    share, size, rows = plan.share, plan.dp, plan.rows
    swap = Swap(plan)
    levels, experts, strip, hidden = expert_in.shape
    spread = Spread(size)
    width = strip * size
    columns = 4 * width + 128
    keys_len = rows * share
    heads = width // HEAD
    hid = hidden // size

    given = entry or later

    def kernel(in_ref, *refs):
        taken, refs = refs[: len(given)], refs[len(given) :]
        (message, middle, queries, kv, log_total, mixed, gates_ref, up_ref), refs = refs[:8], refs[8:]
        if first:
            (grad, grad_low, state_ref, chosen_all, length_ref, dense_out), refs = refs[:6], refs[6:]
        (all_kv, values_t, up_all, whole, parts, send, recv, save, up_send, up_recv), refs = refs[:10], refs[10:]
        bring = pltpu.make_async_copy(in_ref.at[level], whole, save)
        bring.start()
        me = lax.axis_index("dp")
        part = lax.rem(me, share)
        greet(*[({"dp": me ^ r}, None) for r in range(1, size)], *(swap.peers() if first else []))

        def shift(r):
            return remote(
                parts.at[me ^ r], up_all.at[:, pl.ds(pl.multiple_of(me * strip, 16), strip)],
                up_send.at[r], up_recv.at[r], {"dp": me ^ r},
            )

        if first:
            tokens_ref, facts_ref, cot_ref, *strips = taken
            tok, fact, cot, dense_all, tok_sem, fact_sem, cot_sem, keep_sem, *sems = refs
            lay_strip(strips, level, dense_all, pl.ds(pl.multiple_of(me * strip, 16), strip))
            spread.bind(Strips(dense_all, strip), sems)
            spread.start()
            swap.start(facts_ref, fact, fact_sem)
            swap.start(tokens_ref, tok, tok_sem)
        bring.wait()
        for owner in range(size):
            parts[owner] = whole[:, :, owner * hid : (owner + 1) * hid]
        up_all[:, pl.ds(pl.multiple_of(me * strip, 16), strip)] = parts[me]
        if first:
            for pair in spread.order[1:]:
                spread.arrive(pair)
            for r in range(1, size):
                shift(r).start()
            swap.start(cot_ref, cot, cot_sem)
            swap.wait(facts_ref, fact, fact_sem)
            total = fact[0].astype(F32)
            for k in range(1, plan.images):
                total += fact[k].astype(F32)
            for at in range(levels):
                chosen_all[at] = total[8 * at : 8 * at + 8]
            length = total[8 * levels : 8 * levels + 1, :1] * 4.0 + total[8 * levels + 1 : 8 * levels + 2, :1]
            length_ref[...] = jnp.broadcast_to(length, length_ref.shape)
            swap.wait(tokens_ref, tok, tok_sem)
            for k in range(plan.images):
                state_ref[k * plan.piece : (k + 1) * plan.piece] = tok[k].astype(F32)
            for pair in spread.order:
                spread.handed(pair).wait_recv()
            keep_dense = pltpu.make_async_copy(dense_all, dense_out, keep_sem)
            keep_dense.start()
            dense_ref, chosen_ref = dense_all, chosen_all.at[level]
        else:
            state_ref, dense_ref, chosen_ref, length_ref = taken
            for r in range(1, size):
                shift(r).start()
        rows_of = weight_rows(dense_ref)
        unit, _ = normalize(state_ref[...])
        normed = (unit * rows_of[0:1] + rows_of[1:2]).astype(BF16)
        all_kv[part] = dot(normed, dense_ref[:, width : 3 * width]).astype(BF16)
        copies = [
            remote(all_kv.at[part], all_kv.at[part], send.at[k], recv.at[k], {"dp": me ^ k})
            for k in range(1, share)
        ]
        for copy in copies:
            copy.start()
        queries[...] = (dot(normed, dense_ref[:, :width]) * HEAD ** (-0.5)).astype(BF16)
        for copy in copies:
            copy.wait()
        saving = pltpu.make_async_copy(all_kv, kv, save)
        saving.start()
        for at in range(share):
            values_t[:, at * rows : (at + 1) * rows] = jnp.transpose(
                all_kv[at, :, width:].astype(F32)
            ).astype(BF16)
        key = lax.broadcasted_iota(jnp.int32, (keys_len, rows), 0)
        valid = key.astype(F32) < length_ref[0:1, 0:1]

        def pair_of_heads(pair, carry):
            lanes = pl.ds(pl.multiple_of(pair * 128, 128), 128)
            keys_pair = all_kv[:, :, lanes].reshape(keys_len, 128)
            queries_pair = queries[:, lanes]
            for parity in range(2):
                head = 2 * pair + parity
                scores = dot(keys_pair, one_head(queries_pair, parity), NT)
                scores = jnp.where(valid, scores, NEG)
                highest = jnp.max(scores, 0, keepdims=True)
                expo = jnp.exp(scores - highest)
                totals = row_sums(expo)
                log_total[head] = highest + jnp.log(totals)
                place = pl.ds(pl.multiple_of(head * HEAD, HEAD), HEAD)
                mixed[place, :] = (dot(values_t[place, :], expo.astype(BF16)) / totals).astype(BF16)
            return carry

        lax.fori_loop(0, heads // 2, pair_of_heads, 0)
        middle[...] = state_ref[...] + dot(mixed[...], dense_ref[:, 3 * width : 4 * width], TN)
        unit, _ = normalize(middle[...])
        normed = (unit * rows_of[2:3] + rows_of[3:4]).astype(BF16)
        message[:rows] = normed
        router = jnp.concatenate([rows_of[4:8], jnp.zeros((12, width), F32)], 0).astype(BF16)
        logits = dot(router, normed, NT)[:8]
        row = lax.broadcasted_iota(jnp.int32, logits.shape, 0)
        logits = jnp.where(row < experts, logits, NEG)
        expo = jnp.exp(logits - jnp.max(logits, 0, keepdims=True))
        gates = expo / row_sums(expo)
        gates_ref[...] = gates
        message[rows:] = split_rows(pad_lanes(gates * chosen_ref[:, :rows], width))
        saving.wait()
        for r in range(1, size):
            shift(r).wait_recv()
        keep = pltpu.make_async_copy(up_all, up_ref, save)
        keep.start()
        if first:
            swap.wait(cot_ref, cot, cot_sem)
            for k in range(plan.images):
                place = slice(k * plan.piece, (k + 1) * plan.piece)
                row = lax.broadcasted_iota(jnp.int32, (plan.piece, width), 0) + part * rows + k * plan.piece
                masked = jnp.where(row.astype(F32) < length_ref[0:1, 0:1], cot[k].astype(F32), 0.0)
                grad[place] = masked
                grad_low[place] = masked.astype(BF16)
            spread.drain()
            keep_dense.wait()
        for r in range(1, size):
            shift(r).wait_send()
        keep.wait()

    pieces = pltpu.VMEM((plan.images, plan.piece, width), BF16)
    swap_sem = pltpu.SemaphoreType.DMA((2, plan.images))
    entry_out, entry_specs, entry_scratch = (), (), []
    if first:
        entry_out = (
            jax.ShapeDtypeStruct((rows, width), F32),
            jax.ShapeDtypeStruct((rows, width), BF16),
            jax.ShapeDtypeStruct((rows, width), F32),
            jax.ShapeDtypeStruct((levels, 8, width), F32),
            jax.ShapeDtypeStruct((8, 128), F32),
            jax.ShapeDtypeStruct((width, columns), BF16),
        )
        entry_specs = (in_vmem(),) * 5 + (in_any(),)
        entry_scratch = [
            pieces,
            pltpu.VMEM(entry[1].shape, BF16),
            pieces,
            pltpu.VMEM((width, columns), BF16),
            swap_sem,
            swap_sem,
            swap_sem,
            pltpu.SemaphoreType.DMA,
        ] + spread.semaphores()
    return pl.pallas_call(
        kernel,
        out_shape=(
            jax.ShapeDtypeStruct((rows + 16, width), BF16),
            jax.ShapeDtypeStruct((rows, width), F32),
            jax.ShapeDtypeStruct((rows, width), BF16),
            jax.ShapeDtypeStruct((share, rows, 2 * width), BF16),
            jax.ShapeDtypeStruct((heads, 1, rows), F32),
            jax.ShapeDtypeStruct((width, rows), BF16),
            jax.ShapeDtypeStruct((8, rows), F32),
            jax.ShapeDtypeStruct((experts, width, hid), BF16),
            *entry_out,
        ),
        in_specs=[in_any()] + [in_vmem()] * len(given),
        out_specs=(in_vmem(),) * 3 + (in_any(),) + (in_vmem(),) * 3 + (in_any(),) + entry_specs,
        scratch_shapes=[
            pltpu.VMEM((share, rows, 2 * width), BF16),
            pltpu.VMEM((width, keys_len), BF16),
            pltpu.VMEM((experts, width, hid), BF16),
            pltpu.VMEM((experts, strip, hidden), BF16),
            pltpu.VMEM((size, experts, strip, hid), BF16),
            pltpu.SemaphoreType.DMA((share,)),
            pltpu.SemaphoreType.DMA((share,)),
            pltpu.SemaphoreType.DMA,
            pltpu.SemaphoreType.DMA((size,)),
            pltpu.SemaphoreType.DMA((size,)),
        ]
        + entry_scratch,
        compiler_params=pltpu.CompilerParams(
            collective_id=5 + first, has_side_effects=True, vmem_limit_bytes=VMEM_LIMIT
        ),
        name="attention_forward_first" if first else "attention_forward",
    )(expert_in, *given)


def attention_backward(
    grad, back, back_tail, state, middle, message, gates, chosen, queries, kv, log_total, mixed,
    dense, length, up_grad, plan, job, last,
):
    rows, width = state.shape
    share = plan.share
    keys_len = rows * share
    heads = width // HEAD
    columns = dense.shape[1]
    swap = Swap(plan)
    strip = width // plan.dp
    dense_shape = (plan.dp // 2, 2, strip, columns)
    moves = up_grad is not None
    shift = Shift(up_grad) if moves else None
    moved_out = moves and not last
    totals_shape = [
        jax.ShapeDtypeStruct((len(job.kept), strip, wide), F32)
        for wide in ((3 * width, width, columns - 4 * width) if job.kept else ())
    ]

    def kernel(*refs):
        (
            grad_ref, back_ref, tail_ref, state_ref, mid_ref, msg_ref, gates_ref, chosen_ref, queries, kv,
            log_total, mixed, weights, length_ref,
        ), refs = refs[:14], refs[14:]
        if moves:
            up_ref, refs = refs[0], refs[1:]
        taken = len(job.args)
        job_refs, refs = refs[:taken], refs[taken:]
        (new_ref, new_low_ref, dense_ref), refs = refs[:3], refs[3:]
        if moved_out:
            moved_ref, refs = refs[0], refs[1:]
        if totals_shape:
            totals, refs = refs[:3], refs[3:]
        job_outs, refs = refs[: len(job.out_shape)], refs[len(job.out_shape) :]
        (
            keys_t, normed_ref, grad_mid, grad_heads, grad_q, kv_grads, kv_got, grad_packed, send, recv,
        ), refs = refs[:10], refs[10:]
        if moves:
            moving = (up_ref, *refs[:3])
            refs = refs[3:]
        if last:
            (pieces, piece_sem), refs = refs[:2], refs[2:]
            if job.kinds:
                job_refs = (job_refs[0], moving[1], *job_refs[1:], dense_ref)
        summing = last and job.kinds
        job.bind(job_refs, job_outs, refs)
        in_heads, after_heads, after_sums, rest = job.share_out(HEAD_TICKS)
        me = lax.axis_index("dp")
        part = lax.rem(me, share)
        greet(
            *[({"dp": me ^ k}, None) for k in range(1, plan.dp if moves else share)],
            *job.peers(),
            *(swap.peers() if last else []),
        )
        if moves:
            shift.start(*moving)
        if job.kinds:
            job.begin("down")
        if summing:
            job.dense_begin(job.dense[0])
        rows_of = weight_rows(weights)
        gates = gates_ref[...]
        grad_gates = tail_ref[:, :rows] * chosen_ref[:, :rows]
        grad_logits = split_rows(gates * (grad_gates - row_sums(gates * grad_gates)))
        router = jnp.concatenate([rows_of[4:8], jnp.zeros((4, width), F32)], 0)
        twice = jnp.concatenate([router, router], 0).astype(BF16)
        grad_normed = back_ref[...] + dot(grad_logits, twice, TN)
        router_grad = dot(grad_logits, msg_ref[:rows])
        router_grad = router_grad[:8] + router_grad[8:]
        unit, inverse = normalize(mid_ref[...])
        gain_two = row_sums(grad_normed * unit)
        bias_two = row_sums(grad_normed)
        grad_mid[...] = grad_ref[...] + norm_back(grad_normed * rows_of[2:3], unit, inverse)
        low = grad_mid[...].astype(BF16)

        def put(columns_of, values):
            for at in range(plan.dp):
                dense_ref[at // 2, at % 2, :, columns_of] = values[at * strip : (at + 1) * strip].astype(BF16)

        put(slice(3 * width, 4 * width), dot(mixed[...], low))
        grad_heads[...] = dot(low, weights[:, 3 * width : 4 * width], NT).astype(BF16)
        for at in range(share):
            keys_t[:, at * rows : (at + 1) * rows] = jnp.transpose(kv[at, :, :width].astype(F32)).astype(BF16)
        key = lax.broadcasted_iota(jnp.int32, (keys_len, rows), 0)
        valid = key.astype(F32) < length_ref[0:1, 0:1]

        def pair_of_heads(pair, carry):
            lanes = pl.ds(pl.multiple_of(pair * 128, 128), 128)
            value_lanes = pl.ds(pl.multiple_of(width + pair * 128, 128), 128)
            keys_pair = kv[:, :, lanes].reshape(keys_len, 128)
            values_pair = kv[:, :, value_lanes].reshape(keys_len, 128)
            grad_k = jnp.zeros((keys_len, 128), F32)
            grad_v = jnp.zeros((keys_len, 128), F32)
            for parity in range(2):
                head = 2 * pair + parity
                query = one_head(queries[:, lanes], parity)
                pull = one_head(grad_heads[:, lanes], parity)
                scores = dot(keys_pair, query, NT)
                probs = jnp.where(valid, jnp.exp(scores - log_total[head]), 0.0)
                grad_probs = dot(values_pair, pull, NT)
                grad_scores = probs * (grad_probs - row_sums(probs * grad_probs))
                grad_scores = grad_scores.astype(BF16)
                grad_v += dot(probs.astype(BF16), pull)
                grad_k += dot(grad_scores, query)
                place = pl.ds(pl.multiple_of(head * HEAD, HEAD), HEAD)
                grad_q[place, :] = dot(keys_t[place, :], grad_scores) * HEAD ** (-0.5)
            kv_grads[:, :, lanes] = grad_k.astype(BF16).reshape(share, rows, 128)
            kv_grads[:, :, value_lanes] = grad_v.astype(BF16).reshape(share, rows, 128)
            for at, ticks in enumerate(in_heads):
                for tick in ticks:
                    pl.when(pair == at)(tick)
            if summing:
                pl.when(pair == heads // 2 - 2)(lambda: job.dense_near(job.dense[0]))
            return carry

        lax.fori_loop(0, heads // 2, pair_of_heads, 0)
        for tick in after_heads[0]:
            tick()
        copies = [
            remote(kv_grads.at[part ^ k], kv_got.at[k], send.at[k], recv.at[k], {"dp": me ^ k})
            for k in range(1, share)
        ]
        for copy in copies:
            copy.start()
        unit, inverse = normalize(state_ref[...])
        normed_ref[...] = (unit * rows_of[0:1] + rows_of[1:2]).astype(BF16)
        grad_packed[:, :width] = jnp.transpose(grad_q[...]).astype(BF16)
        for copy in copies:
            copy.wait()
        total = kv_grads[part].astype(F32)
        for k in range(1, share):
            total += kv_got[k].astype(F32)
        grad_packed[:, width:] = total.astype(BF16)
        grad_normed = dot(grad_packed[...], weights[:, : 3 * width], NT)
        for block in range(3):
            cols = slice(block * width, (block + 1) * width)
            put(cols, dot(normed_ref[...], grad_packed[:, cols], TN))
        gain_one = row_sums(grad_normed * unit)
        bias_one = row_sums(grad_normed)
        tail = jnp.concatenate([gain_one, bias_one, gain_two, bias_two, router_grad[:4]], 0)
        put(slice(4 * width, columns), pad_lanes(jnp.transpose(tail), columns - 4 * width))
        for tick in after_sums[0]:
            tick()
        if summing:
            job.dense_begin(job.dense[1])
            shift.arrive(*moving)
            job.begin("up")
        new = grad_mid[...] + norm_back(grad_normed * rows_of[0:1], unit, inverse)
        if last:
            for k in range(plan.images):
                new_low_ref[k] = new[k * plan.piece : (k + 1) * plan.piece].astype(BF16)
            swap.start(new_low_ref, pieces, piece_sem)
        else:
            new_low_ref[...] = new.astype(BF16)
            new_ref[...] = new
        if moved_out:
            shift.arrive(*moving)
            moved_ref[...] = moving[1][...]
        for at, tick in enumerate(rest, sum(map(sum, HEAD_TICKS))):
            if summing and at == DENSE_TICKS[0]:
                job.dense_near(job.dense[1])
            if summing and at == DENSE_TICKS[1]:
                job.dense_far(job.dense[0])
            if summing and at == DENSE_TICKS[2]:
                job.dense_far(job.dense[1])
            tick()
        job.finish()
        for at, kind in enumerate(job.kept):
            start = 0
            for total in totals:
                wide = total.shape[2]
                for chunk in range(4):
                    place = slice(chunk * strip // 4, (chunk + 1) * strip // 4)
                    total[at, place] = job.boxes[kind][3][chunk, :, start : start + wide].astype(F32)
                start += wide
        if moves:
            shift.drain(*moving)
        if last:
            swap.wait(new_low_ref, pieces, piece_sem)
            for k in range(plan.images):
                new_ref[k] = pieces[k].astype(F32)

    image_shape = (plan.images, plan.piece, width) if last else (rows, width)
    last_scratch = [
        pltpu.VMEM((plan.images, plan.piece, width), BF16),
        pltpu.SemaphoreType.DMA((2, plan.images)),
    ]
    return pl.pallas_call(
        kernel,
        out_shape=(
            jax.ShapeDtypeStruct(image_shape, F32),
            jax.ShapeDtypeStruct(image_shape, BF16),
            jax.ShapeDtypeStruct(dense_shape, BF16),
            *([jax.ShapeDtypeStruct(shift.shape, BF16)] if moved_out else []),
            *totals_shape,
            *job.out_shape,
        ),
        in_specs=[in_vmem()] * (14 + moves + len(job.args)),
        out_specs=(in_vmem(),) * (3 + moved_out + len(totals_shape)) + (in_any(),) * len(job.out_shape),
        scratch_shapes=[
            pltpu.VMEM((width, keys_len), BF16),
            pltpu.VMEM((rows, width), BF16),
            pltpu.VMEM((rows, width), F32),
            pltpu.VMEM((rows, width), BF16),
            pltpu.VMEM((width, rows), F32),
            pltpu.VMEM((share, rows, 2 * width), BF16),
            pltpu.VMEM((share, rows, 2 * width), BF16),
            pltpu.VMEM((rows, 3 * width), BF16),
            pltpu.SemaphoreType.DMA((share,)),
            pltpu.SemaphoreType.DMA((share,)),
        ]
        + (shift.scratch_shapes if moves else [])
        + (last_scratch if last else [])
        + job.scratch_shapes,
        compiler_params=pltpu.CompilerParams(
            collective_id=9 if last else 8, has_side_effects=True, vmem_limit_bytes=VMEM_LIMIT
        ),
        name="attention_backward_last" if last else "attention_backward",
    )(
        grad, back, back_tail, state, middle, message, gates, chosen, queries, kv, log_total, mixed,
        dense, length, *([up_grad] if moves else []), *job.args,
    )


def build(mesh):
    def shards(
        tokens,
        cotangent,
        routes,
        token_mask,
        ln1_gain,
        ln1_bias,
        qkv_weight,
        out_weight,
        ln2_gain,
        ln2_bias,
        router_weight,
        expert_in,
        expert_out,
    ):
        images, piece, width = tokens.shape
        levels, experts = expert_in.shape[:2]
        plan = Plan(mesh, images, token_mask.shape[1])
        rows = plan.rows
        wide = experts * expert_out.shape[2]
        lined = plan.seq == 4

        mine = lax.rem(lax.axis_index("seq"), images)
        chosen = jnp.sum((routes[..., None] == jnp.arange(experts, dtype=jnp.int32)).astype(F32), -2)
        chosen = jnp.transpose(chosen, (1, 0, 3, 2))
        at_slot = (jnp.arange(images) == mine).astype(F32)[:, None]
        chosen = (chosen[..., None, :] * at_slot).reshape(images, levels, experts, rows)
        chosen = jnp.pad(chosen, ((0, 0), (0, 0), (0, 8 - experts), (0, width - rows)))
        lengths = jnp.where(mine == 0, jnp.sum(token_mask, -1), 0)
        lengths = jnp.stack([lengths // 4, lengths % 4], -1).astype(F32)
        lengths = jnp.pad(lengths, ((0, 0), (0, 14)))[:, :, None]
        facts = jnp.concatenate(
            [chosen.reshape(images, 8 * levels, width), jnp.broadcast_to(lengths, (images, 16, width))], 1
        ).astype(BF16)

        strips = (qkv_weight, out_weight, router_weight, ln1_gain, ln1_bias, ln2_gain, ln2_bias)
        down_all = expert_out.reshape(levels, wide, width)

        saved = []
        for level in range(levels):
            if level:
                made = attention_forward(
                    plan, level, expert_in, later=(state, dense, chosen[level], length)
                )
            else:
                *made, grad, grad_low, state, chosen, length, dense = attention_forward(
                    plan, level, expert_in, entry=(tokens, facts, cotangent, *strips)
                )
            message, middle, queries, kv, log_total, mixed, gates, up = made
            new_state, new_low, blocks, act, slope, *next_dense = experts_forward(
                message, middle, up, down_all, level, plan.dp, strips if level + 1 < levels else ()
            )
            attended = (
                state, middle, message, gates, chosen[level], queries, kv, log_total, mixed,
                dense, length,
            )
            dense = next_dense[0] if next_dense else None
            saved.append((attended, (blocks, act, slope, up, down_all)))
            state = new_state
        leaving = new_low.reshape(images, piece, width)

        sums = [None] * levels
        job = LineSums()
        for level in reversed(range(levels)):
            attended, routed = saved[level]
            last = level == 0
            back, back_tail, up_grad, down_grad, *others = experts_backward(
                grad_low, *routed, level, plan, job, leaving
            )
            if leaving is not None:
                output, *others = others
                leaving = None
            if job.kinds:
                downs, ups = jnp.concatenate([first_downs, others[0]]), others[1]
            up_grad = up_grad.reshape(experts, plan.dp, 4, width // plan.dp // 4, -1)
            down_grad = down_grad.reshape(16, wide // 16, width)
            job = LineSums(plan.dp, (0, EARLY_CHUNKS), down=down_grad) if lined else LineSums()
            if lined and last:
                job = LineSums(
                    plan.dp,
                    None,
                    ("dense", "dense_more"),
                    down=down_grad,
                    up=jax.ShapeDtypeStruct(Shift(up_grad).shape, BF16),
                    dense_more=dense_grad,
                    dense=jax.ShapeDtypeStruct(dense_grad.shape, BF16),
                )
            grad, grad_low, dense_grad, *others = attention_backward(
                grad, back, back_tail, *attended, up_grad if lined else None, plan, job, last
            )
            if not lined:
                sums[level] = sum_weights_plainly(plan.dp, down_grad, up_grad, dense_grad)
            elif last:
                packed_grad, out_grad, tail_grad = others[:3]
                sums[level] = others[3:]
                sums[level + 1] = (downs, ups)
            else:
                first_downs = others[1]
                job = LineSums(plan.dp, (EARLY_CHUNKS, 16), down=down_grad, up=others[0])
        down_grad, up_grad = (
            jnp.stack([item.reshape(like.shape[1:]) for item in items]).astype(F32)
            for items, like in zip(zip(*(item[:2] for item in sums)), (expert_out, expert_in))
        )
        if not lined:
            dense_grad = jnp.stack([item[2].reshape(width // plan.dp, -1) for item in sums]).astype(F32)
            packed_grad, out_grad = dense_grad[..., : 3 * width], dense_grad[..., 3 * width : 4 * width]
            tail_grad = dense_grad[..., 4 * width :]
        return (
            output,
            grad,
            tail_grad[..., 0],
            tail_grad[..., 1],
            packed_grad,
            out_grad,
            tail_grad[..., 2],
            tail_grad[..., 3],
            tail_grad[..., 4 : 4 + experts],
            up_grad,
            down_grad,
        )

    return shards


def solution(mesh):
    return jax.shard_map(
        build(mesh),
        mesh=mesh,
        in_specs=(
            P("dp", "seq", None),
            P("dp", "seq", None),
            P(None, "dp", "seq", None),
            P("dp", None),
            P(None, "dp"),
            P(None, "dp"),
            P(None, "dp", None),
            P(None, "dp", None),
            P(None, "dp"),
            P(None, "dp"),
            P(None, "dp", None),
            P(None, None, "dp", None),
            P(None, None, "dp", None),
        ),
        out_specs=(
            P("dp", "seq", None),
            P("dp", "seq", None),
            P(None, "dp"),
            P(None, "dp"),
            P(None, "dp", None),
            P(None, "dp", None),
            P(None, "dp"),
            P(None, "dp"),
            P(None, "dp", None),
            P(None, None, "dp", None),
            P(None, None, "dp", None),
        ),
        check_vma=False,
    )
```

```python
import itertools

import jax
import jax.numpy as jnp
from jax import lax
from jax.experimental import pallas as pl
from jax.experimental.pallas import tpu as pltpu
from jax.sharding import PartitionSpec as P

HEAD = 64
EPS = 1e-06
NEG = -1e30
F32 = jnp.float32
BF16 = jnp.bfloat16
MESH = pl.DeviceIdType.MESH
VMEM_LIMIT = 60 * 1024 * 1024
EXPERT_TICKS = ((0, 2, 1, 1, 1, 1, 1, 1), (1, 0, 1, 0), (1,), (1, 1, 0))
HEAD_TICKS = ((0, 1, 1, 1), (1,), (1,))
DENSE_TICKS = (6, 7, 16)
EARLY_CHUNKS = 4
NT = ((1,), (1,))
TN = ((0,), (0,))


def normalize(values):
    center = values - jnp.mean(values, -1, keepdims=True)
    inverse = lax.rsqrt(jnp.mean(center * center, -1, keepdims=True) + EPS)
    return center * inverse, inverse


def norm_back(grad_unit, unit, inverse):
    return inverse * (
        grad_unit
        - jnp.mean(grad_unit, -1, keepdims=True)
        - unit * jnp.mean(grad_unit * unit, -1, keepdims=True)
    )


def in_vmem():
    return pl.BlockSpec(memory_space=pltpu.VMEM)


def in_any():
    return pl.BlockSpec(memory_space=pl.ANY)


def greet(*peers):
    barrier = pltpu.get_barrier_semaphore()
    count = 0
    for peer, condition in peers:

        def signal(peer=peer):
            pl.semaphore_signal(barrier, inc=1, device_id=peer, device_id_type=MESH)

        if condition is None:
            signal()
            count += 1
        else:
            pl.when(condition)(signal)
            count += condition.astype(jnp.int32)
    pl.semaphore_wait(barrier, count)


def remote(src, dst, send, recv, peer):
    return pltpu.make_async_remote_copy(
        src_ref=src, dst_ref=dst, send_sem=send, recv_sem=recv, device_id=peer, device_id_type=MESH
    )


def split_rows(rows8):
    high = rows8.astype(BF16).astype(F32)
    return jnp.concatenate([high, rows8 - high], 0).astype(BF16)


def join_rows(rows16):
    wide = rows16.astype(F32)
    return wide[:8] + wide[8:]


def gelu_parts(u):
    bell = jnp.exp2(u * u * -0.7213475204444817)
    t = pl.reciprocal(1.0 + 0.23164190 * jnp.abs(u), approx=True)
    poly = t * (
        0.127414796 + t * (-0.142248368 + t * (0.7107068705 + t * (-0.7265760135 + t * 0.5307027145)))
    )
    half = poly * bell
    cdf = jnp.where(u >= 0, 1.0 - half, half)
    return u * cdf, cdf + u * 0.3989422804014327 * bell


def dot(left, right, dims=((1,), (0,))):
    return lax.dot_general(left, right, (dims, ((), ())), preferred_element_type=F32)


def row_sums(values):
    return jnp.sum(values, 0, keepdims=True)


def pad_lanes(values, lanes):
    if values.shape[1] == lanes:
        return values
    return jnp.concatenate([values, jnp.zeros((values.shape[0], lanes - values.shape[1]), values.dtype)], 1)


def one_head(pair, parity):
    lane = lax.broadcasted_iota(jnp.int32, pair.shape, 1) // HEAD
    return jnp.where(lane == parity, pair.astype(F32), 0.0).astype(BF16)


def weight_rows(dense_ref):
    width = dense_ref.shape[0]
    return jnp.transpose(dense_ref[:, 4 * width :].astype(F32))


def lay_strip(refs, level, dense, place):
    packed, out, router, *vectors = refs
    strip, width = out.shape[1:]
    dense[place, : 3 * width] = packed[level]
    dense[place, 3 * width : 4 * width] = out[level]
    rows = [vector[...].astype(F32)[level : level + 1] for vector in vectors]
    rows = jnp.concatenate(rows + [jnp.zeros((4, strip), F32)], 0)
    columns = jnp.transpose(pad_lanes(rows, 128))[:strip, :4]
    tail = jnp.concatenate([columns, router[level].astype(F32)], 1)
    dense[place, 4 * width :] = pad_lanes(tail, 128).astype(BF16)


class Plan:
    def __init__(self, mesh, images, length):
        self.dp = mesh.shape["dp"]
        self.seq = mesh.shape["seq"]
        self.images = images
        self.piece = length // self.seq
        self.share = self.seq // images
        self.rows = images * self.piece


class Swap:
    def __init__(self, plan):
        self.plan = plan

    def where(self, k):
        me, mine = lax.axis_index("dp"), lax.axis_index("seq")
        share, images = self.plan.share, self.plan.images
        part = lax.rem(me, share)
        peer = {"dp": me - part + mine // images, "seq": part * images + k}
        stays = (part == mine // images) & (lax.rem(mine, images) == k)
        return peer, stays

    def peers(self):
        both = [self.where(k) for k in range(self.plan.images)]
        return [(peer, jnp.logical_not(stays)) for peer, stays in both]

    def start(self, src, dst, sems):
        slot = lax.rem(lax.axis_index("seq"), self.plan.images)
        for k in range(self.plan.images):
            peer, stays = self.where(k)

            @pl.when(jnp.logical_not(stays))
            def _():
                remote(src.at[k], dst.at[slot], sems.at[0, k], sems.at[1, slot], peer).start()

            @pl.when(stays)
            def _():
                pltpu.make_async_copy(src.at[k], dst.at[k], sems.at[1, k]).start()

    def wait(self, src, dst, sems):
        for k in range(self.plan.images):
            peer, stays = self.where(k)
            moved = remote(src.at[k], dst.at[k], sems.at[0, k], sems.at[1, k], peer)

            @pl.when(jnp.logical_not(stays))
            def _():
                moved.wait_recv()
                moved.wait_send()

            @pl.when(stays)
            def _():
                pltpu.make_async_copy(src.at[k], dst.at[k], sems.at[1, k]).wait()


class Slots:
    def __init__(self, ref):
        self.ref = ref
        self.rows = ref.shape[1]

    def at(self, slot, part, device):
        return self.ref.at[slot, part]


class Strips:
    def __init__(self, ref, rows):
        self.ref = ref
        self.rows = rows

    def at(self, slot, part, device):
        first = pl.multiple_of((device ^ slot) * self.rows + part.start, 16)
        return self.ref.at[pl.ds(first, part.size)]


class Spread:
    def __init__(self, size):
        self.size = size
        self.pairs = size // 2
        self.order = sorted(range(self.pairs), key=lambda pair: (bin(pair).count("1"), pair))
        self.bits = [1 << k for k in range(self.pairs.bit_length() - 1)]

    def ways(self, pair):
        return (pair & -pair, 1 << (pair.bit_length() - 1))

    def pair_at(self, turn):
        if isinstance(turn, int):
            return self.order[turn]
        pair = turn
        for at, value in enumerate(self.order):
            if at != value:
                pair = jnp.where(turn == at, value, pair)
        return pair

    def peers(self):
        me = lax.axis_index("dp")
        return [({"dp": me ^ r}, None) for r in (1, *range(2, self.size, 2))]

    def semaphores(self):
        return [
            pltpu.SemaphoreType.DMA((2, self.pairs)),
            pltpu.SemaphoreType.DMA((2, self.size)),
            pltpu.SemaphoreType.DMA((self.pairs,)),
        ]

    def bind(self, slots, semaphores):
        self.slots = slots
        self.send, self.recv, self.hand = semaphores
        self.me = lax.axis_index("dp")
        cut = slots.rows // 32 * 16
        self.whole = pl.ds(0, slots.rows)
        self.halves = (pl.ds(0, cut), pl.ds(cut, slots.rows - cut))

    def move(self, slot, to_slot, part, peer, send, recv):
        return remote(
            self.slots.at(slot, part, self.me), self.slots.at(to_slot, part, peer), send, recv, {"dp": peer}
        )

    def block(self, pair):
        slot = 2 * pair
        return self.move(0, slot, self.whole, self.me ^ slot, self.send.at[0, pair], self.recv.at[0, slot])

    def half_block(self, pair, half):
        way = self.ways(pair)[half]
        return self.move(
            2 * (pair ^ way), 2 * pair, self.halves[half], self.me ^ (2 * way),
            self.send.at[half, pair], self.recv.at[half, 2 * pair],
        )

    def handed(self, pair):
        slot = 2 * pair
        return self.move(
            slot, slot + 1, self.whole, self.me ^ 1, self.hand.at[pair], self.recv.at[0, slot + 1]
        )

    def start(self):
        self.handed(0).start()
        for bit in self.bits:
            self.block(bit).start()

    def arrive(self, pair):
        for known in range(1, self.pairs):

            @pl.when(jnp.asarray(pair) == known)
            def _():
                if known in self.bits:
                    self.block(known).wait_recv()
                else:
                    self.half_block(known, 0).wait_recv()
                    self.half_block(known, 1).wait_recv()
                for far in range(1, self.pairs):
                    for half, way in enumerate(self.ways(far)):
                        if far not in self.bits and far ^ way == known:
                            self.half_block(far, half).start()

        self.handed(pair).start()

    def drain(self):
        for pair in range(self.pairs):
            self.handed(pair).wait_send()
            if pair in self.bits:
                self.block(pair).wait_send()
            elif pair:
                self.half_block(pair, 0).wait_send()
                self.half_block(pair, 1).wait_send()


class Group(Spread):
    def scratch(self, rows, tail, width):
        full = rows + tail
        return self.semaphores() + [
            pltpu.VMEM((self.pairs, rows, width), F32),
            pltpu.VMEM((self.pairs, 8, width), F32),
            pltpu.VMEM((self.pairs, full, width), BF16),
            pltpu.VMEM((self.pairs, full, width), BF16),
            pltpu.VMEM((self.pairs, full, width), BF16),
            pltpu.VMEM((self.pairs, full, width), BF16),
            pltpu.SemaphoreType.DMA((self.pairs,)),
            pltpu.SemaphoreType.DMA((self.pairs,)),
            pltpu.SemaphoreType.DMA((self.pairs,)),
            pltpu.SemaphoreType.DMA((self.pairs,)),
        ]

    def given(self, pair):
        return remote(
            self.give.at[pair], self.take.at[pair], self.g_send.at[pair], self.g_recv.at[pair], {"dp": self.me ^ 1}
        )

    def paid(self, pair):
        return remote(
            self.pay.at[pair], self.due.at[pair], self.p_send.at[pair], self.p_recv.at[pair],
            {"dp": self.me ^ (2 * pair)},
        )

    def run(self, slots, scratch, rows, tail, compute):
        self.bind(Slots(slots), scratch[:3])
        (
            self.own, self.own_tail, self.give, self.take, self.pay, self.due,
            self.g_send, self.g_recv, self.p_send, self.p_recv,
        ) = scratch[3:]
        self.sizes = rows, tail

        def settle(pair):
            self.given(pair).wait_recv()
            self.own[pair] += self.take[pair, :rows].astype(F32)
            if tail:
                self.own_tail[pair] += join_rows(self.take[pair, rows:])

            @pl.when(jnp.asarray(pair) > 0)
            def _():
                self.pay[pair, :rows] = self.own[pair].astype(BF16)
                if tail:
                    self.pay[pair, rows:] = split_rows(self.own_tail[pair])
                self.paid(pair).start()

        self.start()

        def step(at, carry):
            turn = at // 2
            pair = self.pair_at(turn)
            odd = lax.rem(at, 2) == 0
            slot = 2 * pair + 1 - lax.rem(at, 2)

            @pl.when(odd & (turn == 1))
            def _():
                for bit in self.bits:
                    self.arrive(bit)

            @pl.when(odd & (turn > len(self.bits)))
            def _():
                self.arrive(pair)

            @pl.when(odd)
            def _():
                self.handed(pair).wait_recv()

            total, total_tail = compute(slot, at)

            @pl.when(odd)
            def _():
                self.give[pair, :rows] = total.astype(BF16)
                if tail:
                    self.give[pair, rows:] = split_rows(total_tail)
                self.given(pair).start()

            @pl.when(jnp.logical_not(odd))
            def _():
                self.own[pair] = total
                if tail:
                    self.own_tail[pair] = total_tail
                settle(pair)

            return carry

        lax.fori_loop(0, self.size, step, 0)

    def collect(self, between=()):
        rows, tail = self.sizes
        for pair, steps in zip(self.order[1:], itertools.chain(between, itertools.repeat(()))):
            self.paid(pair).wait_recv()
            for step in steps:
                step()
            self.own[0] += self.due[pair, :rows].astype(F32)
            if tail:
                self.own_tail[0] += join_rows(self.due[pair, rows:])
        for pair in range(self.pairs):
            self.given(pair).wait_send()
            if pair:
                self.paid(pair).wait_send()
        self.drain()


def experts_forward(message, middle, up, down, level, size, strips=()):
    rows, width = middle.shape
    experts, _, hid = up.shape
    wide = experts * hid
    group = Group(size)
    spread = Spread(size)
    extra = bool(strips)
    strip = width // size

    def kernel(msg_ref, mid_ref, up_ref, down_all, *refs):
        strip_refs, refs = refs[: len(strips)], refs[len(strips) :]
        (out_ref, low_ref, all_ref, act_ref, slope_ref), refs = refs[:5], refs[5:]
        if extra:
            dense_ref, refs = refs[0], refs[1:]
        (down_ref, down_sem, slots, act, slope, scaled, save_sem), refs = refs[:7], refs[7:]
        scratch, refs = refs[:13], refs[13:]
        bring = pltpu.make_async_copy(down_all.at[level], down_ref, down_sem)
        bring.start()
        if extra:
            dense_all, keep_sem, *sems = refs
            me = lax.axis_index("dp")
            spread.bind(Strips(dense_all, strip), sems)
            lay_strip(strip_refs, level + 1, dense_all, pl.ds(pl.multiple_of(me * strip, 16), strip))
        greet(*group.peers())
        slots[0] = msg_ref[...]
        bring.wait()

        def saves(slot):
            return (
                pltpu.make_async_copy(slots.at[slot], all_ref.at[slot], save_sem.at[slot, 0]),
                pltpu.make_async_copy(act.at[slot], act_ref.at[slot], save_sem.at[slot, 1]),
                pltpu.make_async_copy(slope.at[slot], slope_ref.at[slot], save_sem.at[slot, 2]),
            )

        def compute(slot, at):
            gates = jnp.transpose(join_rows(slots[slot, rows:]))[:rows]
            for expert in range(experts):
                cols = slice(expert * hid, (expert + 1) * hid)
                value, grade = gelu_parts(dot(slots[slot, :rows], up_ref[expert]))
                value = value.astype(BF16)
                act[slot, :, cols] = value
                slope[slot, :, cols] = grade.astype(BF16)
                scaled[:, cols] = (value.astype(F32) * gates[:, expert : expert + 1]).astype(BF16)
            for save in saves(slot):
                save.start()
            if extra:
                pl.when(at == 0)(spread.start)
                for turn, pair in enumerate(spread.order[1:], 1):
                    pl.when(at == (3 if pair in spread.bits else 5))(lambda pair=pair: spread.arrive(pair))
            return dot(scaled[...], down_ref[...]), None

        group.run(slots, scratch, rows, 0, compute)
        if extra:
            for pair in spread.order:
                spread.handed(pair).wait_recv()
            keep = pltpu.make_async_copy(dense_all, dense_ref, keep_sem)
            keep.start()
        group.collect()
        out = mid_ref[...] + group.own[0]
        out_ref[...] = out
        low_ref[...] = out.astype(BF16)
        for slot in range(size):
            for save in saves(slot):
                save.wait()
        if extra:
            spread.drain()
            keep.wait()

    return pl.pallas_call(
        kernel,
        out_shape=(
            jax.ShapeDtypeStruct((rows, width), F32),
            jax.ShapeDtypeStruct((rows, width), BF16),
            jax.ShapeDtypeStruct((size, rows + 16, width), BF16),
            jax.ShapeDtypeStruct((size, rows, wide), BF16),
            jax.ShapeDtypeStruct((size, rows, wide), BF16),
            *([jax.ShapeDtypeStruct((width, 4 * width + 128), BF16)] if extra else []),
        ),
        in_specs=[in_vmem()] * 3 + [in_any()] + [in_vmem()] * len(strips),
        out_specs=(in_vmem(), in_vmem(), in_any(), in_any(), in_any()) + (in_any(),) * extra,
        scratch_shapes=[
            pltpu.VMEM((wide, width), BF16),
            pltpu.SemaphoreType.DMA,
            pltpu.VMEM((size, rows + 16, width), BF16),
            pltpu.VMEM((size, rows, wide), BF16),
            pltpu.VMEM((size, rows, wide), BF16),
            pltpu.VMEM((rows, wide), BF16),
            pltpu.SemaphoreType.DMA((size, 3)),
        ]
        + group.scratch(rows, 0, width)
        + (
            [pltpu.VMEM((width, 4 * width + 128), BF16), pltpu.SemaphoreType.DMA]
            + spread.semaphores()
            if extra
            else []
        ),
        compiler_params=pltpu.CompilerParams(
            collective_id=10 if extra else 1, has_side_effects=True, vmem_limit_bytes=VMEM_LIMIT
        ),
        name="experts_forward",
    )(message, middle, up, down, *strips)


class Shift:
    def __init__(self, source):
        experts, self.dp, quarters, r, self.hid = source.shape
        self.experts = experts
        self.shape = (experts, quarters, r, self.dp * self.hid)
        self.scratch_shapes = [
            pltpu.VMEM(self.shape, BF16),
            pltpu.VMEM((self.dp, experts, quarters, r, self.hid), BF16),
            pltpu.SemaphoreType.DMA((2, self.dp)),
        ]

    def copy(self, src, dst, box, sems, r):
        me = lax.axis_index("dp")
        return remote(src.at[:, me ^ r], box.at[me], sems.at[0, r], sems.at[1, r], {"dp": me ^ r})

    def start(self, *refs):
        for r in range(1, self.dp):
            self.copy(*refs, r).start()

    def arrive(self, src, dst, box, sems):
        me = lax.axis_index("dp")
        box[me] = src[:, me]
        for r in range(1, self.dp):
            self.copy(src, dst, box, sems, r).wait_recv()
        for owner in range(self.dp):
            dst[:, :, :, owner * self.hid : (owner + 1) * self.hid] = box[owner]

    def drain(self, *refs):
        for r in range(1, self.dp):
            self.copy(*refs, r).wait_send()


class LineSums:
    def __init__(self, dp=0, down_chunks=None, kept=(), **arrays):
        self.dp = dp
        self.kept = kept
        self.first = down_chunks[0] if down_chunks else 0
        self.kinds = list(arrays)
        self.args = tuple(array for array in arrays.values() if not isinstance(array, jax.ShapeDtypeStruct))
        self.dense = [kind for kind in self.kinds if kind.startswith("dense")]
        self.chunk, self.count = {}, {}
        self.out_shape, self.scratch_shapes = (), []
        for kind, array in arrays.items():
            shape = array.shape
            special = []
            if kind == "up":
                self.chunk[kind], self.count[kind] = shape[2:], shape[0] * shape[1]
            elif kind == "down":
                self.chunk[kind] = shape[1:]
                self.count[kind] = down_chunks[1] - down_chunks[0] if down_chunks else shape[0]
            else:
                self.chunk[kind], self.count[kind] = (shape[2] // 4, shape[3]), 4
                whole = (dp // 2,) + shape[2:]
                special = [
                    pltpu.VMEM(whole, BF16),
                    pltpu.VMEM(whole, BF16),
                    pltpu.VMEM((4,) + self.chunk[kind], BF16),
                    pltpu.SemaphoreType.DMA((2,)),
                    pltpu.SemaphoreType.DMA((2, dp // 2)),
                ]
            count, chunk = self.count[kind], self.chunk[kind]
            if kind not in kept:
                self.out_shape += (jax.ShapeDtypeStruct((count,) + chunk, BF16),)
            self.scratch_shapes += [
                pltpu.VMEM((count,) + chunk, BF16),
                pltpu.VMEM((count // 2,) + chunk, BF16),
                pltpu.VMEM((count // 2,) + chunk, BF16),
                pltpu.VMEM((count,) + chunk, BF16),
                pltpu.SemaphoreType.DMA((2, count)),
                pltpu.SemaphoreType.DMA((2, count // 2)),
                pltpu.SemaphoreType.DMA((2, count)),
                pltpu.SemaphoreType.DMA((count // 2,)),
                pltpu.SemaphoreType.DMA,
            ] + special
        self.pairs = [(kind, p) for kind in self.kinds for p in range(self.count[kind] // 2)]

    def peers(self):
        if not self.kinds:
            return []
        mine = lax.axis_index("seq")
        middle = (mine == 1) | (mine == 2)
        return [
            ({"seq": jnp.where(middle, 3 - mine, 1 + mine // 2)}, None),
            ({"seq": jnp.where(middle, 3 * (mine - 1), mine)}, middle),
        ]

    def bind(self, refs, outs, scratch):
        self.refs = dict(zip(self.kinds, refs))
        self.outs = dict(zip((kind for kind in self.kinds if kind not in self.kept), outs))
        self.boxes = {}
        for kind in self.kinds:
            held = 14 if kind in self.dense else 9
            self.boxes[kind], scratch = scratch[:held], scratch[held:]
        self.me, self.mine = lax.axis_index("dp"), lax.axis_index("seq")
        self.middle = (self.mine == 1) | (self.mine == 2)
        self.inner = {"seq": jnp.where(self.middle, 3 - self.mine, 1 + self.mine // 2)}
        self.outer = {"seq": jnp.where(self.middle, 3 * (self.mine - 1), self.mine)}
        self.side = jnp.where(self.mine == 2, 1, 0)

    def source(self, kind, c):
        if kind == "up":
            return self.refs[kind].at[c // 4, lax.rem(c, 4)]
        return self.boxes[kind][11].at[c] if kind in self.dense else self.refs[kind].at[self.first + c]

    def inward(self, kind, c):
        box, sem = self.boxes[kind][0], self.boxes[kind][4]
        return remote(self.source(kind, c), box.at[c], sem.at[0, c], sem.at[1, c], self.inner)

    def across(self, kind, p):
        box, sem = self.boxes[kind], self.boxes[kind][5]
        return remote(box[2].at[p], box[1].at[p], sem.at[0, p], sem.at[1, p], self.inner)

    def outward(self, kind, c):
        box, sem = self.boxes[kind][3], self.boxes[kind][6]
        return remote(box.at[c], box.at[c], sem.at[0, c], sem.at[1, c], self.outer)

    def between(self, kind, c, p):
        box = self.boxes[kind]
        return remote(box[3].at[c], box[3].at[c], box[7].at[p], box[6].at[1, c], self.inner)

    def near_copy(self, kind):
        box = self.boxes[kind]
        away = self.refs[kind].at[:, 1 - lax.rem(self.me, 2)]
        return remote(away, box[9], box[12].at[0], box[12].at[1], {"dp": self.me ^ 1})

    def far(self, kind, m):
        box = self.boxes[kind]
        return remote(
            box[9].at[(self.me // 2) ^ m], box[10].at[m], box[13].at[0, m], box[13].at[1, m],
            {"dp": self.me ^ (2 * m)},
        )

    def begin(self, *kinds):
        @pl.when(jnp.logical_not(self.middle))
        def _():
            for kind in kinds:
                for c in range(self.count[kind]):
                    self.inward(kind, c).start()

    def dense_begin(self, kind):
        self.near_copy(kind).start()

    def dense_near(self, kind):
        self.near_copy(kind).wait_recv()
        box = self.boxes[kind]
        for at in range(self.dp // 2):
            box[9][at] = (
                self.refs[kind][at, lax.rem(self.me, 2)].astype(F32) + box[9][at].astype(F32)
            ).astype(BF16)
        for m in range(1, self.dp // 2):
            self.far(kind, m).start()

    def dense_far(self, kind):
        for m in range(1, self.dp // 2):
            self.far(kind, m).wait_recv()
        box = self.boxes[kind]
        rows = self.chunk[kind][0]
        for at in range(4):
            place = slice(at * rows, (at + 1) * rows)
            total = box[9][self.me // 2, place].astype(F32)
            for m in range(1, self.dp // 2):
                total += box[10][m, place].astype(F32)
            box[11][at] = total.astype(BF16)
        self.begin(kind)

    def relay(self, kind, p):
        c = 2 * p + 1 - self.side
        box = self.boxes[kind]
        self.inward(kind, c).wait_recv()
        box[2][p] = (self.source(kind, c)[...].astype(F32) + box[0][c].astype(F32)).astype(BF16)
        self.across(kind, p).start()

    def total(self, kind, p):
        c = 2 * p + self.side
        box = self.boxes[kind]
        self.inward(kind, c).wait_recv()
        self.across(kind, p).wait_recv()
        box[3][c] = (
            self.source(kind, c)[...].astype(F32) + box[0][c].astype(F32) + box[1][p].astype(F32)
        ).astype(BF16)
        self.between(kind, c, p).start()
        self.outward(kind, c).start()

    def forward(self, kind, p):
        c = 2 * p + 1 - self.side
        self.outward(kind, c).wait_recv()
        self.outward(kind, c).start()

    def ticks(self):
        count = len(self.pairs)
        if not count:
            return []

        def tick(at):
            @pl.when(self.middle)
            def _():
                for act, behind in ((self.relay, 0), (self.total, 2), (self.forward, 4)):
                    if 0 <= at - behind < count:
                        act(*self.pairs[at - behind])

        return [lambda at=at: tick(at) for at in range(count + 4)]

    def share_out(self, places):
        ticks, shared = self.ticks(), []
        for counts in places:
            group = []
            for count in counts:
                group.append(ticks[:count])
                ticks = ticks[count:]
            shared.append(group)
        return (*shared, ticks)

    def finish(self):
        if not self.kinds:
            return

        @pl.when(jnp.logical_not(self.middle))
        def _():
            for kind in self.kinds:
                for c in range(self.count[kind]):
                    self.outward(kind, c).wait_recv()
                    self.inward(kind, c).wait_send()

        copies = [
            pltpu.make_async_copy(self.boxes[kind][3], out, self.boxes[kind][8]) for kind, out in self.outs.items()
        ]
        for copy in copies:
            copy.start()

        @pl.when(self.middle)
        def _():
            for kind, p in self.pairs:
                self.across(kind, p).wait_send()
                self.between(kind, 2 * p + self.side, p).wait_send()
                self.outward(kind, 2 * p).wait_send()
                self.outward(kind, 2 * p + 1).wait_send()

        for kind in self.dense:
            self.near_copy(kind).wait_send()
            for m in range(1, self.dp // 2):
                self.far(kind, m).wait_send()
        for copy in copies:
            copy.wait()


def sum_weights_plainly(dp, down, up, dense):
    dense = lax.psum_scatter(dense.reshape(dp, -1, dense.shape[-1]), "dp", scatter_dimension=0, tiled=True)
    up = lax.all_to_all(up, "dp", split_axis=1, concat_axis=1, tiled=True)
    experts, _, quarters, r, hid = up.shape
    up = jnp.transpose(up.reshape(experts, dp, quarters * r, hid), (0, 2, 1, 3))
    return lax.psum(down, "seq"), lax.psum(up.reshape(experts, quarters * r, -1), "seq"), lax.psum(dense, "seq")


def experts_backward(grad, blocks, act, slope, up, down, level, plan, job, leaving=None):
    rows, width = grad.shape
    experts, _, hid = up.shape
    wide = experts * hid
    size = plan.dp
    group = Group(size)
    swap = Swap(plan)
    extra = [] if leaving is None else [leaving]

    def kernel(*refs):
        (grad_ref, blocks_ref, act_ref, slope_ref, up_ref, down_all), refs = refs[:6], refs[6:]
        if extra:
            leaving_ref, refs = refs[0], refs[1:]
        job_refs, refs = refs[: len(job.args)], refs[len(job.args) :]
        (out_ref, tail_ref, up_out, down_out), refs = refs[:4], refs[4:]
        if extra:
            left_ref, refs = refs[0], refs[1:]
        job_outs, refs = refs[: len(job.args)], refs[len(job.args) :]
        slots, blocks, facts, act, slope, weighed, scaled, pre, flat, load_sem, down_ref, down_sem = refs[:12]
        refs = refs[12:]
        bring = pltpu.make_async_copy(down_all.at[level], down_ref, down_sem)
        bring.start()
        scratch, refs = refs[:13], refs[13:]
        if extra:
            (left, left_sem), refs = refs[:2], refs[2:]
        job.bind(job_refs, job_outs, refs)
        in_steps, in_sums, before, between, rest = job.share_out(EXPERT_TICKS)

        def loads(at):
            two = lax.rem(at, 2)
            slot = 2 * group.pair_at(at // 2) + 1 - two
            place = pl.ds(pl.multiple_of(slot * rows, 16), rows)
            return (
                pltpu.make_async_copy(blocks_ref.at[slot, pl.ds(0, rows)], blocks.at[place], load_sem.at[two, 0]),
                pltpu.make_async_copy(act_ref.at[slot], act.at[two], load_sem.at[two, 1]),
                pltpu.make_async_copy(slope_ref.at[slot], slope.at[two], load_sem.at[two, 2]),
                pltpu.make_async_copy(blocks_ref.at[slot, pl.ds(rows, 16)], facts.at[two], load_sem.at[two, 3]),
            )

        for load in loads(0):
            load.start()
        greet(*group.peers(), *job.peers(), *(swap.peers() if extra else []))
        slots[0] = grad_ref[...]
        if extra:
            swap.start(leaving_ref, left, left_sem)
        for expert in range(experts):
            flat[:, expert * hid : (expert + 1) * hid] = up_ref[expert]
        bring.wait()
        lane = lax.broadcasted_iota(jnp.int32, (16, wide), 1) // hid
        pick = (lane == lax.broadcasted_iota(jnp.int32, (16, wide), 0)).astype(F32).astype(BF16)

        def compute(slot, at):
            two = lax.rem(at, 2)

            @pl.when(at + 1 < size)
            def _():
                for load in loads(at + 1):
                    load.start()

            for load in loads(at):
                load.wait()
            gates = jnp.transpose(join_rows(facts[two]))[:rows]
            place = pl.ds(pl.multiple_of(slot * rows, 16), rows)
            for expert in range(experts):
                cols = slice(expert * hid, (expert + 1) * hid)
                gate = gates[:, expert : expert + 1]
                pull = dot(slots[slot], down_ref[cols, :], NT)
                value = act[two, :, cols].astype(F32)
                weighed[:, cols] = (pull * value).astype(BF16)
                scaled[place, cols] = (value * gate).astype(BF16)
                pre[place, cols] = (pull * gate * slope[two, :, cols].astype(F32)).astype(BF16)
            if job.kinds:
                pl.when(at == 0)(lambda: job.begin(*job.kinds))
                for step, ticks in enumerate(in_steps):
                    for tick in ticks:
                        pl.when(at == step)(tick)
            by_expert = pad_lanes(dot(pick, weighed[...], NT)[:8], width)
            return dot(pre[place, :], flat[...], NT), by_expert

        group.run(slots, scratch, rows, 16, compute)

        def weight_sums(expert, carry):
            cols = pl.ds(pl.multiple_of(expert * hid, 128), hid)
            down_out[cols, :] = dot(scaled[:, cols], slots[...].reshape(size * rows, width), TN).astype(BF16)
            up_out[expert] = dot(blocks[...], pre[:, cols], TN).astype(BF16)
            for step, ticks in enumerate(in_sums):
                for tick in ticks:
                    pl.when(expert == step)(tick)
            return carry

        lax.fori_loop(0, experts, weight_sums, 0)
        for tick in before[0]:
            tick()
        group.collect(between)
        out_ref[...] = group.own[0]
        tail_ref[...] = group.own_tail[0]
        for tick in rest:
            tick()
        job.finish()
        if extra:
            swap.wait(leaving_ref, left, left_sem)
            left_ref[...] = left[...]

    left_shape = [] if leaving is None else [jax.ShapeDtypeStruct(leaving.shape, BF16)]
    left_scratch = [
        pltpu.VMEM((plan.images, plan.piece, width), BF16),
        pltpu.SemaphoreType.DMA((2, plan.images)),
    ]
    return pl.pallas_call(
        kernel,
        out_shape=(
            jax.ShapeDtypeStruct((rows, width), F32),
            jax.ShapeDtypeStruct((8, width), F32),
            jax.ShapeDtypeStruct((experts, width, hid), BF16),
            jax.ShapeDtypeStruct((wide, width), BF16),
            *left_shape,
            *job.out_shape,
        ),
        in_specs=[in_vmem(), in_any(), in_any(), in_any(), in_vmem(), in_any()]
        + [in_vmem()] * (len(extra) + len(job.args)),
        out_specs=(in_vmem(),) * (4 + len(extra)) + (in_any(),) * len(job.args),
        scratch_shapes=[
            pltpu.VMEM((size, rows, width), BF16),
            pltpu.VMEM((size * rows, width), BF16),
            pltpu.VMEM((2, 16, width), BF16),
            pltpu.VMEM((2, rows, wide), BF16),
            pltpu.VMEM((2, rows, wide), BF16),
            pltpu.VMEM((rows, wide), BF16),
            pltpu.VMEM((size * rows, wide), BF16),
            pltpu.VMEM((size * rows, wide), BF16),
            pltpu.VMEM((width, wide), BF16),
            pltpu.SemaphoreType.DMA((2, 4)),
            pltpu.VMEM((wide, width), BF16),
            pltpu.SemaphoreType.DMA,
        ]
        + group.scratch(rows, 16, width)
        + (left_scratch if extra else [])
        + job.scratch_shapes,
        compiler_params=pltpu.CompilerParams(
            collective_id=3 if job.kinds else 2, has_side_effects=True, vmem_limit_bytes=VMEM_LIMIT
        ),
        name="experts_backward_and_sums" if job.kinds else "experts_backward",
    )(grad, blocks, act, slope, up, down, *extra, *job.args)


def attention_forward(plan, level, expert_in, later=None, entry=None):
    first = entry is not None
    share, size, rows = plan.share, plan.dp, plan.rows
    swap = Swap(plan)
    levels, experts, strip, hidden = expert_in.shape
    spread = Spread(size)
    width = strip * size
    columns = 4 * width + 128
    keys_len = rows * share
    heads = width // HEAD
    hid = hidden // size

    given = entry or later

    def kernel(in_ref, *refs):
        taken, refs = refs[: len(given)], refs[len(given) :]
        (message, middle, queries, kv, log_total, mixed, gates_ref, up_ref), refs = refs[:8], refs[8:]
        if first:
            (grad, grad_low, state_ref, chosen_all, length_ref, dense_out), refs = refs[:6], refs[6:]
        (all_kv, values_t, up_all, whole, parts, send, recv, save, up_send, up_recv), refs = refs[:10], refs[10:]
        bring = pltpu.make_async_copy(in_ref.at[level], whole, save)
        bring.start()
        me = lax.axis_index("dp")
        part = lax.rem(me, share)
        greet(*[({"dp": me ^ r}, None) for r in range(1, size)], *(swap.peers() if first else []))

        def shift(r):
            return remote(
                parts.at[me ^ r], up_all.at[:, pl.ds(pl.multiple_of(me * strip, 16), strip)],
                up_send.at[r], up_recv.at[r], {"dp": me ^ r},
            )

        if first:
            tokens_ref, facts_ref, cot_ref, *strips = taken
            tok, fact, cot, dense_all, tok_sem, fact_sem, cot_sem, keep_sem, *sems = refs
            lay_strip(strips, level, dense_all, pl.ds(pl.multiple_of(me * strip, 16), strip))
            spread.bind(Strips(dense_all, strip), sems)
            spread.start()
            swap.start(facts_ref, fact, fact_sem)
            swap.start(tokens_ref, tok, tok_sem)
        bring.wait()
        for owner in range(size):
            parts[owner] = whole[:, :, owner * hid : (owner + 1) * hid]
        up_all[:, pl.ds(pl.multiple_of(me * strip, 16), strip)] = parts[me]
        if first:
            for pair in spread.order[1:]:
                spread.arrive(pair)
            for r in range(1, size):
                shift(r).start()
            swap.start(cot_ref, cot, cot_sem)
            swap.wait(facts_ref, fact, fact_sem)
            total = fact[0].astype(F32)
            for k in range(1, plan.images):
                total += fact[k].astype(F32)
            for at in range(levels):
                chosen_all[at] = total[8 * at : 8 * at + 8]
            length = total[8 * levels : 8 * levels + 1, :1] * 4.0 + total[8 * levels + 1 : 8 * levels + 2, :1]
            length_ref[...] = jnp.broadcast_to(length, length_ref.shape)
            swap.wait(tokens_ref, tok, tok_sem)
            for k in range(plan.images):
                state_ref[k * plan.piece : (k + 1) * plan.piece] = tok[k].astype(F32)
            for pair in spread.order:
                spread.handed(pair).wait_recv()
            keep_dense = pltpu.make_async_copy(dense_all, dense_out, keep_sem)
            keep_dense.start()
            dense_ref, chosen_ref = dense_all, chosen_all.at[level]
        else:
            state_ref, dense_ref, chosen_all, length_ref = taken
            chosen_ref = chosen_all.at[level]
            for r in range(1, size):
                shift(r).start()
        rows_of = weight_rows(dense_ref)
        unit, _ = normalize(state_ref[...])
        normed = (unit * rows_of[0:1] + rows_of[1:2]).astype(BF16)
        all_kv[part] = dot(normed, dense_ref[:, width : 3 * width]).astype(BF16)
        copies = [
            remote(all_kv.at[part], all_kv.at[part], send.at[k], recv.at[k], {"dp": me ^ k})
            for k in range(1, share)
        ]
        for copy in copies:
            copy.start()
        queries[...] = (dot(normed, dense_ref[:, :width]) * HEAD ** (-0.5)).astype(BF16)
        for copy in copies:
            copy.wait()
        saving = pltpu.make_async_copy(all_kv, kv, save)
        saving.start()
        for at in range(share):
            values_t[:, at * rows : (at + 1) * rows] = jnp.transpose(
                all_kv[at, :, width:].astype(F32)
            ).astype(BF16)
        key = lax.broadcasted_iota(jnp.int32, (keys_len, rows), 0)
        valid = key.astype(F32) < length_ref[0:1, 0:1]

        def pair_of_heads(pair, carry):
            lanes = pl.ds(pl.multiple_of(pair * 128, 128), 128)
            keys_pair = all_kv[:, :, lanes].reshape(keys_len, 128)
            queries_pair = queries[:, lanes]
            for parity in range(2):
                head = 2 * pair + parity
                scores = dot(keys_pair, one_head(queries_pair, parity), NT)
                scores = jnp.where(valid, scores, NEG)
                highest = jnp.max(scores, 0, keepdims=True)
                expo = jnp.exp(scores - highest)
                totals = row_sums(expo)
                log_total[head] = highest + jnp.log(totals)
                place = pl.ds(pl.multiple_of(head * HEAD, HEAD), HEAD)
                mixed[place, :] = (dot(values_t[place, :], expo.astype(BF16)) / totals).astype(BF16)
            return carry

        lax.fori_loop(0, heads // 2, pair_of_heads, 0)
        middle[...] = state_ref[...] + dot(mixed[...], dense_ref[:, 3 * width : 4 * width], TN)
        unit, _ = normalize(middle[...])
        normed = (unit * rows_of[2:3] + rows_of[3:4]).astype(BF16)
        message[:rows] = normed
        router = jnp.concatenate([rows_of[4:8], jnp.zeros((12, width), F32)], 0).astype(BF16)
        logits = dot(router, normed, NT)[:8]
        row = lax.broadcasted_iota(jnp.int32, logits.shape, 0)
        logits = jnp.where(row < experts, logits, NEG)
        expo = jnp.exp(logits - jnp.max(logits, 0, keepdims=True))
        gates = expo / row_sums(expo)
        gates_ref[...] = gates
        message[rows:] = split_rows(pad_lanes(gates * chosen_ref[:, :rows], width))
        saving.wait()
        for r in range(1, size):
            shift(r).wait_recv()
        keep = pltpu.make_async_copy(up_all, up_ref, save)
        keep.start()
        if first:
            swap.wait(cot_ref, cot, cot_sem)
            for k in range(plan.images):
                place = slice(k * plan.piece, (k + 1) * plan.piece)
                row = lax.broadcasted_iota(jnp.int32, (plan.piece, width), 0) + part * rows + k * plan.piece
                masked = jnp.where(row.astype(F32) < length_ref[0:1, 0:1], cot[k].astype(F32), 0.0)
                grad[place] = masked
                grad_low[place] = masked.astype(BF16)
            spread.drain()
            keep_dense.wait()
        for r in range(1, size):
            shift(r).wait_send()
        keep.wait()

    pieces = pltpu.VMEM((plan.images, plan.piece, width), BF16)
    swap_sem = pltpu.SemaphoreType.DMA((2, plan.images))
    entry_out, entry_specs, entry_scratch = (), (), []
    if first:
        entry_out = (
            jax.ShapeDtypeStruct((rows, width), F32),
            jax.ShapeDtypeStruct((rows, width), BF16),
            jax.ShapeDtypeStruct((rows, width), F32),
            jax.ShapeDtypeStruct((levels, 8, width), F32),
            jax.ShapeDtypeStruct((8, 128), F32),
            jax.ShapeDtypeStruct((width, columns), BF16),
        )
        entry_specs = (in_vmem(),) * 5 + (in_any(),)
        entry_scratch = [
            pieces,
            pltpu.VMEM(entry[1].shape, BF16),
            pieces,
            pltpu.VMEM((width, columns), BF16),
            swap_sem,
            swap_sem,
            swap_sem,
            pltpu.SemaphoreType.DMA,
        ] + spread.semaphores()
    return pl.pallas_call(
        kernel,
        out_shape=(
            jax.ShapeDtypeStruct((rows + 16, width), BF16),
            jax.ShapeDtypeStruct((rows, width), F32),
            jax.ShapeDtypeStruct((rows, width), BF16),
            jax.ShapeDtypeStruct((share, rows, 2 * width), BF16),
            jax.ShapeDtypeStruct((heads, 1, rows), F32),
            jax.ShapeDtypeStruct((width, rows), BF16),
            jax.ShapeDtypeStruct((8, rows), F32),
            jax.ShapeDtypeStruct((experts, width, hid), BF16),
            *entry_out,
        ),
        in_specs=[in_any()] + [in_vmem()] * len(given),
        out_specs=(in_vmem(),) * 3 + (in_any(),) + (in_vmem(),) * 3 + (in_any(),) + entry_specs,
        scratch_shapes=[
            pltpu.VMEM((share, rows, 2 * width), BF16),
            pltpu.VMEM((width, keys_len), BF16),
            pltpu.VMEM((experts, width, hid), BF16),
            pltpu.VMEM((experts, strip, hidden), BF16),
            pltpu.VMEM((size, experts, strip, hid), BF16),
            pltpu.SemaphoreType.DMA((share,)),
            pltpu.SemaphoreType.DMA((share,)),
            pltpu.SemaphoreType.DMA,
            pltpu.SemaphoreType.DMA((size,)),
            pltpu.SemaphoreType.DMA((size,)),
        ]
        + entry_scratch,
        compiler_params=pltpu.CompilerParams(
            collective_id=5 + first, has_side_effects=True, vmem_limit_bytes=VMEM_LIMIT
        ),
        name="attention_forward_first" if first else "attention_forward",
    )(expert_in, *given)


def attention_backward(
    grad, back, back_tail, state, middle, message, gates, chosen, queries, kv, log_total, mixed,
    dense, length, up_grad, level, plan, job,
):
    rows, width = state.shape
    last = level == 0
    share = plan.share
    keys_len = rows * share
    heads = width // HEAD
    columns = dense.shape[1]
    swap = Swap(plan)
    strip = width // plan.dp
    dense_shape = (plan.dp // 2, 2, strip, columns)
    moves = up_grad is not None
    shift = Shift(up_grad) if moves else None
    moved_out = moves and not last
    totals_shape = [
        jax.ShapeDtypeStruct((len(job.kept), strip, wide), F32)
        for wide in ((3 * width, width, columns - 4 * width) if job.kept else ())
    ]

    def kernel(*refs):
        (
            grad_ref, back_ref, tail_ref, state_ref, mid_ref, msg_ref, gates_ref, chosen_ref, queries, kv,
            log_total, mixed, weights, length_ref,
        ), refs = refs[:14], refs[14:]
        if moves:
            up_ref, refs = refs[0], refs[1:]
        taken = len(job.args)
        job_refs, refs = refs[:taken], refs[taken:]
        (new_ref, new_low_ref), refs = refs[:2], refs[2:]
        if not totals_shape:
            dense_ref, refs = refs[0], refs[1:]
        if moved_out:
            moved_ref, refs = refs[0], refs[1:]
        if totals_shape:
            totals, refs = refs[:3], refs[3:]
        job_outs, refs = refs[: len(job.out_shape)], refs[len(job.out_shape) :]
        (
            keys_t, normed_ref, grad_mid, grad_heads, grad_q, kv_grads, kv_got, grad_packed, send, recv,
        ), refs = refs[:10], refs[10:]
        if moves:
            moving = (up_ref, *refs[:3])
            refs = refs[3:]
        if last:
            (pieces, piece_sem), refs = refs[:2], refs[2:]
            if totals_shape:
                dense_ref, refs = refs[0], refs[1:]
                job_refs = (job_refs[0], moving[1], *job_refs[1:], dense_ref)
        summing = last and job.kinds
        job.bind(job_refs, job_outs, refs)
        in_heads, after_heads, after_sums, rest = job.share_out(HEAD_TICKS)
        me = lax.axis_index("dp")
        part = lax.rem(me, share)
        greet(
            *[({"dp": me ^ k}, None) for k in range(1, plan.dp if moves else share)],
            *job.peers(),
            *(swap.peers() if last else []),
        )
        if moves:
            shift.start(*moving)
        if job.kinds:
            job.begin("down")
        if summing:
            job.dense_begin(job.dense[0])
        rows_of = weight_rows(weights)
        gates = gates_ref[...]
        grad_gates = tail_ref[:, :rows] * chosen_ref[level, :, :rows]
        grad_logits = split_rows(gates * (grad_gates - row_sums(gates * grad_gates)))
        router = jnp.concatenate([rows_of[4:8], jnp.zeros((4, width), F32)], 0)
        twice = jnp.concatenate([router, router], 0).astype(BF16)
        grad_normed = back_ref[...] + dot(grad_logits, twice, TN)
        router_grad = dot(grad_logits, msg_ref[:rows])
        router_grad = router_grad[:8] + router_grad[8:]
        unit, inverse = normalize(mid_ref[...])
        gain_two = row_sums(grad_normed * unit)
        bias_two = row_sums(grad_normed)
        grad_mid[...] = grad_ref[...] + norm_back(grad_normed * rows_of[2:3], unit, inverse)
        low = grad_mid[...].astype(BF16)

        def put(columns_of, values):
            for at in range(plan.dp):
                dense_ref[at // 2, at % 2, :, columns_of] = values[at * strip : (at + 1) * strip].astype(BF16)

        put(slice(3 * width, 4 * width), dot(mixed[...], low))
        grad_heads[...] = dot(low, weights[:, 3 * width : 4 * width], NT).astype(BF16)
        for at in range(share):
            keys_t[:, at * rows : (at + 1) * rows] = jnp.transpose(kv[at, :, :width].astype(F32)).astype(BF16)
        key = lax.broadcasted_iota(jnp.int32, (keys_len, rows), 0)
        valid = key.astype(F32) < length_ref[0:1, 0:1]

        def pair_of_heads(pair, carry):
            lanes = pl.ds(pl.multiple_of(pair * 128, 128), 128)
            value_lanes = pl.ds(pl.multiple_of(width + pair * 128, 128), 128)
            keys_pair = kv[:, :, lanes].reshape(keys_len, 128)
            values_pair = kv[:, :, value_lanes].reshape(keys_len, 128)
            grad_k = jnp.zeros((keys_len, 128), F32)
            grad_v = jnp.zeros((keys_len, 128), F32)
            for parity in range(2):
                head = 2 * pair + parity
                query = one_head(queries[:, lanes], parity)
                pull = one_head(grad_heads[:, lanes], parity)
                scores = dot(keys_pair, query, NT)
                probs = jnp.where(valid, jnp.exp(scores - log_total[head]), 0.0)
                grad_probs = dot(values_pair, pull, NT)
                grad_scores = probs * (grad_probs - row_sums(probs * grad_probs))
                grad_scores = grad_scores.astype(BF16)
                grad_v += dot(probs.astype(BF16), pull)
                grad_k += dot(grad_scores, query)
                place = pl.ds(pl.multiple_of(head * HEAD, HEAD), HEAD)
                grad_q[place, :] = dot(keys_t[place, :], grad_scores) * HEAD ** (-0.5)
            kv_grads[:, :, lanes] = grad_k.astype(BF16).reshape(share, rows, 128)
            kv_grads[:, :, value_lanes] = grad_v.astype(BF16).reshape(share, rows, 128)
            for at, ticks in enumerate(in_heads):
                for tick in ticks:
                    pl.when(pair == at)(tick)
            if summing:
                pl.when(pair == heads // 2 - 2)(lambda: job.dense_near(job.dense[0]))
            return carry

        lax.fori_loop(0, heads // 2, pair_of_heads, 0)
        for tick in after_heads[0]:
            tick()
        copies = [
            remote(kv_grads.at[part ^ k], kv_got.at[k], send.at[k], recv.at[k], {"dp": me ^ k})
            for k in range(1, share)
        ]
        for copy in copies:
            copy.start()
        unit, inverse = normalize(state_ref[...])
        normed_ref[...] = (unit * rows_of[0:1] + rows_of[1:2]).astype(BF16)
        grad_packed[:, :width] = jnp.transpose(grad_q[...]).astype(BF16)
        for copy in copies:
            copy.wait()
        total = kv_grads[part].astype(F32)
        for k in range(1, share):
            total += kv_got[k].astype(F32)
        grad_packed[:, width:] = total.astype(BF16)
        grad_normed = dot(grad_packed[...], weights[:, : 3 * width], NT)
        for block in range(3):
            cols = slice(block * width, (block + 1) * width)
            put(cols, dot(normed_ref[...], grad_packed[:, cols], TN))
        gain_one = row_sums(grad_normed * unit)
        bias_one = row_sums(grad_normed)
        tail = jnp.concatenate([gain_one, bias_one, gain_two, bias_two, router_grad[:4]], 0)
        put(slice(4 * width, columns), pad_lanes(jnp.transpose(tail), columns - 4 * width))
        for tick in after_sums[0]:
            tick()
        if summing:
            job.dense_begin(job.dense[1])
            shift.arrive(*moving)
            job.begin("up")
        new = grad_mid[...] + norm_back(grad_normed * rows_of[0:1], unit, inverse)
        if last:
            for k in range(plan.images):
                new_low_ref[k] = new[k * plan.piece : (k + 1) * plan.piece].astype(BF16)
            if not summing:
                swap.start(new_low_ref, pieces, piece_sem)
        else:
            new_low_ref[...] = new.astype(BF16)
            new_ref[...] = new
        if moved_out:
            shift.arrive(*moving)
            moved_ref[...] = moving[1][...]
        for at, tick in enumerate(rest, sum(map(sum, HEAD_TICKS))):
            if summing and at == DENSE_TICKS[0]:
                job.dense_near(job.dense[1])
            if summing and at == DENSE_TICKS[1]:
                job.dense_far(job.dense[0])
            if summing and at == DENSE_TICKS[2]:
                job.dense_far(job.dense[1])
                swap.start(new_low_ref, pieces, piece_sem)
            tick()
        job.finish()
        for at, kind in enumerate(job.kept):
            start = 0
            for total in totals:
                wide = total.shape[2]
                for chunk in range(4):
                    place = slice(chunk * strip // 4, (chunk + 1) * strip // 4)
                    total[at, place] = job.boxes[kind][3][chunk, :, start : start + wide].astype(F32)
                start += wide
        if moves:
            shift.drain(*moving)
        if last:
            swap.wait(new_low_ref, pieces, piece_sem)
            for k in range(plan.images):
                new_ref[k] = pieces[k].astype(F32)

    image_shape = (plan.images, plan.piece, width) if last else (rows, width)
    last_scratch = [
        pltpu.VMEM((plan.images, plan.piece, width), BF16),
        pltpu.SemaphoreType.DMA((2, plan.images)),
    ]
    return pl.pallas_call(
        kernel,
        out_shape=(
            jax.ShapeDtypeStruct(image_shape, F32),
            jax.ShapeDtypeStruct(image_shape, BF16),
            *([] if totals_shape else [jax.ShapeDtypeStruct(dense_shape, BF16)]),
            *([jax.ShapeDtypeStruct(shift.shape, BF16)] if moved_out else []),
            *totals_shape,
            *job.out_shape,
        ),
        in_specs=[in_vmem()] * (14 + moves + len(job.args)),
        out_specs=(in_vmem(),) * (2 + (len(totals_shape) or 1) + moved_out) + (in_any(),) * len(job.out_shape),
        scratch_shapes=[
            pltpu.VMEM((width, keys_len), BF16),
            pltpu.VMEM((rows, width), BF16),
            pltpu.VMEM((rows, width), F32),
            pltpu.VMEM((rows, width), BF16),
            pltpu.VMEM((width, rows), F32),
            pltpu.VMEM((share, rows, 2 * width), BF16),
            pltpu.VMEM((share, rows, 2 * width), BF16),
            pltpu.VMEM((rows, 3 * width), BF16),
            pltpu.SemaphoreType.DMA((share,)),
            pltpu.SemaphoreType.DMA((share,)),
        ]
        + (shift.scratch_shapes if moves else [])
        + (last_scratch if last else [])
        + ([pltpu.VMEM(dense_shape, BF16)] if totals_shape else [])
        + job.scratch_shapes,
        compiler_params=pltpu.CompilerParams(
            collective_id=9 if last else 8, has_side_effects=True, vmem_limit_bytes=VMEM_LIMIT
        ),
        name="attention_backward_last" if last else "attention_backward",
    )(
        grad, back, back_tail, state, middle, message, gates, chosen, queries, kv, log_total, mixed,
        dense, length, *([up_grad] if moves else []), *job.args,
    )


def build(mesh):
    def shards(
        tokens,
        cotangent,
        routes,
        token_mask,
        ln1_gain,
        ln1_bias,
        qkv_weight,
        out_weight,
        ln2_gain,
        ln2_bias,
        router_weight,
        expert_in,
        expert_out,
    ):
        images, piece, width = tokens.shape
        levels, experts = expert_in.shape[:2]
        plan = Plan(mesh, images, token_mask.shape[1])
        rows = plan.rows
        wide = experts * expert_out.shape[2]
        lined = plan.seq == 4

        mine = lax.rem(lax.axis_index("seq"), images)
        chosen = jnp.sum((routes[..., None] == jnp.arange(experts, dtype=jnp.int32)).astype(F32), -2)
        chosen = jnp.transpose(chosen, (1, 0, 3, 2))
        at_slot = (jnp.arange(images) == mine).astype(F32)[:, None]
        chosen = (chosen[..., None, :] * at_slot).reshape(images, levels, experts, rows)
        chosen = jnp.pad(chosen, ((0, 0), (0, 0), (0, 8 - experts), (0, width - rows)))
        lengths = jnp.where(mine == 0, jnp.sum(token_mask, -1), 0)
        lengths = jnp.stack([lengths // 4, lengths % 4], -1).astype(F32)
        lengths = jnp.pad(lengths, ((0, 0), (0, 14)))[:, :, None]
        facts = jnp.concatenate(
            [chosen.reshape(images, 8 * levels, width), jnp.broadcast_to(lengths, (images, 16, width))], 1
        ).astype(BF16)

        strips = (qkv_weight, out_weight, router_weight, ln1_gain, ln1_bias, ln2_gain, ln2_bias)
        down_all = expert_out.reshape(levels, wide, width)

        saved = []
        for level in range(levels):
            if level:
                made = attention_forward(
                    plan, level, expert_in, later=(state, dense, chosen, length)
                )
            else:
                *made, grad, grad_low, state, chosen, length, dense = attention_forward(
                    plan, level, expert_in, entry=(tokens, facts, cotangent, *strips)
                )
            message, middle, queries, kv, log_total, mixed, gates, up = made
            new_state, new_low, blocks, act, slope, *next_dense = experts_forward(
                message, middle, up, down_all, level, plan.dp, strips if level + 1 < levels else ()
            )
            attended = (
                state, middle, message, gates, chosen, queries, kv, log_total, mixed,
                dense, length,
            )
            dense = next_dense[0] if next_dense else None
            saved.append((attended, (blocks, act, slope, up, down_all)))
            state = new_state
        leaving = new_low.reshape(images, piece, width)

        sums = [None] * levels
        job = LineSums()
        for level in reversed(range(levels)):
            attended, routed = saved[level]
            last = level == 0
            back, back_tail, up_grad, down_grad, *others = experts_backward(
                grad_low, *routed, level, plan, job, leaving
            )
            if leaving is not None:
                output, *others = others
                leaving = None
            if job.kinds:
                downs, ups = jnp.concatenate([first_downs, others[0]]), others[1]
            up_grad = up_grad.reshape(experts, plan.dp, 4, width // plan.dp // 4, -1)
            down_grad = down_grad.reshape(16, wide // 16, width)
            job = LineSums(plan.dp, (0, EARLY_CHUNKS), down=down_grad) if lined else LineSums()
            if lined and last:
                job = LineSums(
                    plan.dp,
                    None,
                    ("dense", "dense_more"),
                    down=down_grad,
                    up=jax.ShapeDtypeStruct(Shift(up_grad).shape, BF16),
                    dense_more=dense_grad,
                    dense=jax.ShapeDtypeStruct(dense_grad.shape, BF16),
                )
            grad, grad_low, *others = attention_backward(
                grad, back, back_tail, *attended, up_grad if lined else None, level, plan, job
            )
            if not (lined and last):
                dense_grad, *others = others
            if not lined:
                sums[level] = sum_weights_plainly(plan.dp, down_grad, up_grad, dense_grad)
            elif last:
                packed_grad, out_grad, tail_grad = others[:3]
                sums[level] = others[3:]
                sums[level + 1] = (downs, ups)
            else:
                first_downs = others[1]
                job = LineSums(plan.dp, (EARLY_CHUNKS, 16), down=down_grad, up=others[0])
        down_grad, up_grad = (
            jnp.stack([item.reshape(like.shape[1:]) for item in items]).astype(F32)
            for items, like in zip(zip(*(item[:2] for item in sums)), (expert_out, expert_in))
        )
        if not lined:
            dense_grad = jnp.stack([item[2].reshape(width // plan.dp, -1) for item in sums]).astype(F32)
            packed_grad, out_grad = dense_grad[..., : 3 * width], dense_grad[..., 3 * width : 4 * width]
            tail_grad = dense_grad[..., 4 * width :]
        return (
            output,
            grad,
            tail_grad[..., 0],
            tail_grad[..., 1],
            packed_grad,
            out_grad,
            tail_grad[..., 2],
            tail_grad[..., 3],
            tail_grad[..., 4 : 4 + experts],
            up_grad,
            down_grad,
        )

    return shards


def solution(mesh):
    return jax.shard_map(
        build(mesh),
        mesh=mesh,
        in_specs=(
            P("dp", "seq", None),
            P("dp", "seq", None),
            P(None, "dp", "seq", None),
            P("dp", None),
            P(None, "dp"),
            P(None, "dp"),
            P(None, "dp", None),
            P(None, "dp", None),
            P(None, "dp"),
            P(None, "dp"),
            P(None, "dp", None),
            P(None, None, "dp", None),
            P(None, None, "dp", None),
        ),
        out_specs=(
            P("dp", "seq", None),
            P("dp", "seq", None),
            P(None, "dp"),
            P(None, "dp"),
            P(None, "dp", None),
            P(None, "dp", None),
            P(None, "dp"),
            P(None, "dp"),
            P(None, "dp", None),
            P(None, None, "dp", None),
            P(None, None, "dp", None),
        ),
        check_vma=False,
    )
```

```python
import itertools

import jax
import jax.numpy as jnp
from jax import lax
from jax.experimental import pallas as pl
from jax.experimental.pallas import tpu as pltpu
from jax.sharding import PartitionSpec as P

HEAD = 64
EPS = 1e-06
NEG = -1e30
F32 = jnp.float32
BF16 = jnp.bfloat16
MESH = pl.DeviceIdType.MESH
VMEM_LIMIT = 60 * 1024 * 1024
EXPERT_TICKS = ((0, 2, 1, 1, 1, 1, 1, 1), (1, 1, 1, 1), (1,), (2, 2, 1))
HEAD_TICKS = ((0, 1, 1, 1), (1,), (1,))
DENSE_TICKS = (6, 7, 16)
EARLY_CHUNKS = 4
NT = ((1,), (1,))
TN = ((0,), (0,))


def normalize(values):
    center = values - jnp.mean(values, -1, keepdims=True)
    inverse = lax.rsqrt(jnp.mean(center * center, -1, keepdims=True) + EPS)
    return center * inverse, inverse


def norm_back(grad_unit, unit, inverse):
    return inverse * (
        grad_unit
        - jnp.mean(grad_unit, -1, keepdims=True)
        - unit * jnp.mean(grad_unit * unit, -1, keepdims=True)
    )


def in_vmem():
    return pl.BlockSpec(memory_space=pltpu.VMEM)


def in_any():
    return pl.BlockSpec(memory_space=pl.ANY)


def greet(*peers):
    barrier = pltpu.get_barrier_semaphore()
    count = 0
    for peer, condition in peers:

        def signal(peer=peer):
            pl.semaphore_signal(barrier, inc=1, device_id=peer, device_id_type=MESH)

        if condition is None:
            signal()
            count += 1
        else:
            pl.when(condition)(signal)
            count += condition.astype(jnp.int32)
    pl.semaphore_wait(barrier, count)


def remote(src, dst, send, recv, peer):
    return pltpu.make_async_remote_copy(
        src_ref=src, dst_ref=dst, send_sem=send, recv_sem=recv, device_id=peer, device_id_type=MESH
    )


def split_rows(rows8):
    high = rows8.astype(BF16).astype(F32)
    return jnp.concatenate([high, rows8 - high], 0).astype(BF16)


def join_rows(rows16):
    wide = rows16.astype(F32)
    return wide[:8] + wide[8:]


def gelu_parts(u):
    bell = jnp.exp2(u * u * -0.7213475204444817)
    under = 1.0 + 0.23164190 * jnp.abs(u)
    t = pl.reciprocal(under, approx=True)
    t = t * (2.0 - under * t)
    poly = t * (
        0.127414796 + t * (-0.142248368 + t * (0.7107068705 + t * (-0.7265760135 + t * 0.5307027145)))
    )
    half = poly * bell
    cdf = jnp.where(u >= 0, 1.0 - half, half)
    return u * cdf, cdf + u * 0.3989422804014327 * bell


def dot(left, right, dims=((1,), (0,))):
    return lax.dot_general(left, right, (dims, ((), ())), preferred_element_type=F32)


def row_sums(values):
    return jnp.sum(values, 0, keepdims=True)


def pad_lanes(values, lanes):
    if values.shape[1] == lanes:
        return values
    return jnp.concatenate([values, jnp.zeros((values.shape[0], lanes - values.shape[1]), values.dtype)], 1)


def one_head(pair, parity):
    lane = lax.broadcasted_iota(jnp.int32, pair.shape, 1) // HEAD
    return jnp.where(lane == parity, pair.astype(F32), 0.0).astype(BF16)


def weight_rows(dense_ref):
    width = dense_ref.shape[0]
    return jnp.transpose(dense_ref[:, 4 * width :].astype(F32))


def lay_strip(refs, level, dense, place):
    packed, out, router, *vectors = refs
    strip, width = out.shape[1:]
    dense[place, : 3 * width] = packed[level]
    dense[place, 3 * width : 4 * width] = out[level]
    rows = [vector[...].astype(F32)[level : level + 1] for vector in vectors]
    rows = jnp.concatenate(rows + [jnp.zeros((4, strip), F32)], 0)
    columns = jnp.transpose(pad_lanes(rows, 128))[:strip, :4]
    tail = jnp.concatenate([columns, router[level].astype(F32)], 1)
    dense[place, 4 * width :] = pad_lanes(tail, 128).astype(BF16)


class Plan:
    def __init__(self, mesh, images, length):
        self.dp = mesh.shape["dp"]
        self.seq = mesh.shape["seq"]
        self.images = images
        self.piece = length // self.seq
        self.share = self.seq // images
        self.rows = images * self.piece


class Swap:
    def __init__(self, plan):
        self.plan = plan

    def where(self, k):
        me, mine = lax.axis_index("dp"), lax.axis_index("seq")
        share, images = self.plan.share, self.plan.images
        part = lax.rem(me, share)
        peer = {"dp": me - part + mine // images, "seq": part * images + k}
        stays = (part == mine // images) & (lax.rem(mine, images) == k)
        return peer, stays

    def peers(self):
        both = [self.where(k) for k in range(self.plan.images)]
        return [(peer, jnp.logical_not(stays)) for peer, stays in both]

    def start(self, src, dst, sems):
        slot = lax.rem(lax.axis_index("seq"), self.plan.images)
        for k in range(self.plan.images):
            peer, stays = self.where(k)

            @pl.when(jnp.logical_not(stays))
            def _():
                remote(src.at[k], dst.at[slot], sems.at[0, k], sems.at[1, slot], peer).start()

            @pl.when(stays)
            def _():
                pltpu.make_async_copy(src.at[k], dst.at[k], sems.at[1, k]).start()

    def wait(self, src, dst, sems):
        for k in range(self.plan.images):
            peer, stays = self.where(k)
            moved = remote(src.at[k], dst.at[k], sems.at[0, k], sems.at[1, k], peer)

            @pl.when(jnp.logical_not(stays))
            def _():
                moved.wait_recv()
                moved.wait_send()

            @pl.when(stays)
            def _():
                pltpu.make_async_copy(src.at[k], dst.at[k], sems.at[1, k]).wait()


class Slots:
    def __init__(self, ref):
        self.ref = ref
        self.rows = ref.shape[1]

    def at(self, slot, part, device):
        return self.ref.at[slot, part]


class Strips:
    def __init__(self, ref, rows):
        self.ref = ref
        self.rows = rows

    def at(self, slot, part, device):
        first = pl.multiple_of((device ^ slot) * self.rows + part.start, 16)
        return self.ref.at[pl.ds(first, part.size)]


class Spread:
    def __init__(self, size):
        self.size = size
        self.pairs = size // 2
        self.order = sorted(range(self.pairs), key=lambda pair: (bin(pair).count("1"), pair))
        self.bits = [1 << k for k in range(self.pairs.bit_length() - 1)]

    def ways(self, pair):
        return (pair & -pair, 1 << (pair.bit_length() - 1))

    def pair_at(self, turn):
        if isinstance(turn, int):
            return self.order[turn]
        pair = turn
        for at, value in enumerate(self.order):
            if at != value:
                pair = jnp.where(turn == at, value, pair)
        return pair

    def peers(self):
        me = lax.axis_index("dp")
        return [({"dp": me ^ r}, None) for r in (1, *range(2, self.size, 2))]

    def semaphores(self):
        return [
            pltpu.SemaphoreType.DMA((2, self.pairs)),
            pltpu.SemaphoreType.DMA((2, self.size)),
            pltpu.SemaphoreType.DMA((self.pairs,)),
        ]

    def bind(self, slots, semaphores):
        self.slots = slots
        self.send, self.recv, self.hand = semaphores
        self.me = lax.axis_index("dp")
        cut = slots.rows // 32 * 16
        self.whole = pl.ds(0, slots.rows)
        self.halves = (pl.ds(0, cut), pl.ds(cut, slots.rows - cut))

    def move(self, slot, to_slot, part, peer, send, recv):
        return remote(
            self.slots.at(slot, part, self.me), self.slots.at(to_slot, part, peer), send, recv, {"dp": peer}
        )

    def block(self, pair):
        slot = 2 * pair
        return self.move(0, slot, self.whole, self.me ^ slot, self.send.at[0, pair], self.recv.at[0, slot])

    def half_block(self, pair, half):
        way = self.ways(pair)[half]
        return self.move(
            2 * (pair ^ way), 2 * pair, self.halves[half], self.me ^ (2 * way),
            self.send.at[half, pair], self.recv.at[half, 2 * pair],
        )

    def handed(self, pair):
        slot = 2 * pair
        return self.move(
            slot, slot + 1, self.whole, self.me ^ 1, self.hand.at[pair], self.recv.at[0, slot + 1]
        )

    def start(self):
        self.handed(0).start()
        for bit in self.bits:
            self.block(bit).start()

    def arrive(self, pair):
        for known in range(1, self.pairs):

            @pl.when(jnp.asarray(pair) == known)
            def _():
                if known in self.bits:
                    self.block(known).wait_recv()
                else:
                    self.half_block(known, 0).wait_recv()
                    self.half_block(known, 1).wait_recv()
                for far in range(1, self.pairs):
                    for half, way in enumerate(self.ways(far)):
                        if far not in self.bits and far ^ way == known:
                            self.half_block(far, half).start()

        self.handed(pair).start()

    def drain(self):
        for pair in range(self.pairs):
            self.handed(pair).wait_send()
            if pair in self.bits:
                self.block(pair).wait_send()
            elif pair:
                self.half_block(pair, 0).wait_send()
                self.half_block(pair, 1).wait_send()


class Group(Spread):
    def scratch(self, rows, tail, width):
        full = rows + tail
        return self.semaphores() + [
            pltpu.VMEM((self.pairs, rows, width), F32),
            pltpu.VMEM((self.pairs, 8, width), F32),
            pltpu.VMEM((self.pairs, full, width), BF16),
            pltpu.VMEM((self.pairs, full, width), BF16),
            pltpu.VMEM((self.pairs, full, width), BF16),
            pltpu.VMEM((self.pairs, full, width), BF16),
            pltpu.SemaphoreType.DMA((self.pairs,)),
            pltpu.SemaphoreType.DMA((self.pairs,)),
            pltpu.SemaphoreType.DMA((self.pairs,)),
            pltpu.SemaphoreType.DMA((self.pairs,)),
        ]

    def given(self, pair):
        return remote(
            self.give.at[pair], self.take.at[pair], self.g_send.at[pair], self.g_recv.at[pair], {"dp": self.me ^ 1}
        )

    def paid(self, pair):
        return remote(
            self.pay.at[pair], self.due.at[pair], self.p_send.at[pair], self.p_recv.at[pair],
            {"dp": self.me ^ (2 * pair)},
        )

    def run(self, slots, scratch, rows, tail, compute):
        self.bind(Slots(slots), scratch[:3])
        (
            self.own, self.own_tail, self.give, self.take, self.pay, self.due,
            self.g_send, self.g_recv, self.p_send, self.p_recv,
        ) = scratch[3:]
        self.sizes = rows, tail

        def settle(pair):
            self.given(pair).wait_recv()
            self.own[pair] += self.take[pair, :rows].astype(F32)
            if tail:
                self.own_tail[pair] += join_rows(self.take[pair, rows:])

            @pl.when(jnp.asarray(pair) > 0)
            def _():
                self.pay[pair, :rows] = self.own[pair].astype(BF16)
                if tail:
                    self.pay[pair, rows:] = split_rows(self.own_tail[pair])
                self.paid(pair).start()

        self.start()

        def step(at, carry):
            turn = at // 2
            pair = self.pair_at(turn)
            odd = lax.rem(at, 2) == 0
            slot = 2 * pair + 1 - lax.rem(at, 2)

            @pl.when(odd & (turn == 1))
            def _():
                for bit in self.bits:
                    self.arrive(bit)

            @pl.when(odd & (turn > len(self.bits)))
            def _():
                self.arrive(pair)

            @pl.when(odd)
            def _():
                self.handed(pair).wait_recv()

            total, total_tail = compute(slot, at)

            @pl.when(odd)
            def _():
                self.give[pair, :rows] = total.astype(BF16)
                if tail:
                    self.give[pair, rows:] = split_rows(total_tail)
                self.given(pair).start()

            @pl.when(jnp.logical_not(odd))
            def _():
                self.own[pair] = total
                if tail:
                    self.own_tail[pair] = total_tail
                settle(pair)

            return carry

        lax.fori_loop(0, self.size, step, 0)

    def collect(self, between=()):
        rows, tail = self.sizes
        for pair, steps in zip(self.order[1:], itertools.chain(between, itertools.repeat(()))):
            self.paid(pair).wait_recv()
            for step in steps:
                step()
            self.own[0] += self.due[pair, :rows].astype(F32)
            if tail:
                self.own_tail[0] += join_rows(self.due[pair, rows:])
        for pair in range(self.pairs):
            self.given(pair).wait_send()
            if pair:
                self.paid(pair).wait_send()
        self.drain()


def experts_forward(message, middle, up, down, level, size, strips=()):
    rows, width = middle.shape
    experts, _, hid = up.shape
    wide = experts * hid
    group = Group(size)
    spread = Spread(size)
    extra = bool(strips)
    strip = width // size

    def kernel(msg_ref, mid_ref, up_ref, down_all, *refs):
        strip_refs, refs = refs[: len(strips)], refs[len(strips) :]
        (out_ref, low_ref, all_ref, act_ref, slope_ref), refs = refs[:5], refs[5:]
        if extra:
            dense_ref, refs = refs[0], refs[1:]
        (down_ref, down_sem, slots, act, slope, scaled, save_sem), refs = refs[:7], refs[7:]
        scratch, refs = refs[:13], refs[13:]
        bring = pltpu.make_async_copy(down_all.at[level], down_ref, down_sem)
        bring.start()
        if extra:
            dense_all, keep_sem, *sems = refs
            me = lax.axis_index("dp")
            spread.bind(Strips(dense_all, strip), sems)
            lay_strip(strip_refs, level + 1, dense_all, pl.ds(pl.multiple_of(me * strip, 16), strip))
        greet(*group.peers())
        slots[0] = msg_ref[...]
        bring.wait()

        def saves(slot):
            return (
                pltpu.make_async_copy(slots.at[slot], all_ref.at[slot], save_sem.at[slot, 0]),
                pltpu.make_async_copy(act.at[slot], act_ref.at[slot], save_sem.at[slot, 1]),
                pltpu.make_async_copy(slope.at[slot], slope_ref.at[slot], save_sem.at[slot, 2]),
            )

        def compute(slot, at):
            gates = jnp.transpose(join_rows(slots[slot, rows:]))[:rows]
            for expert in range(experts):
                cols = slice(expert * hid, (expert + 1) * hid)
                value, grade = gelu_parts(dot(slots[slot, :rows], up_ref[expert]))
                value = value.astype(BF16)
                act[slot, :, cols] = value
                slope[slot, :, cols] = grade.astype(BF16)
                scaled[:, cols] = (value.astype(F32) * gates[:, expert : expert + 1]).astype(BF16)
            for save in saves(slot):
                save.start()
            if extra:
                pl.when(at == 0)(spread.start)
                for turn, pair in enumerate(spread.order[1:], 1):
                    pl.when(at == (3 if pair in spread.bits else 5))(lambda pair=pair: spread.arrive(pair))
            return dot(scaled[...], down_ref[...]), None

        group.run(slots, scratch, rows, 0, compute)
        if extra:
            for pair in spread.order:
                spread.handed(pair).wait_recv()
            keep = pltpu.make_async_copy(dense_all, dense_ref, keep_sem)
            keep.start()
        group.collect()
        out = mid_ref[...] + group.own[0]
        out_ref[...] = out
        low_ref[...] = out.astype(BF16)
        for slot in range(size):
            for save in saves(slot):
                save.wait()
        if extra:
            spread.drain()
            keep.wait()

    return pl.pallas_call(
        kernel,
        out_shape=(
            jax.ShapeDtypeStruct((rows, width), F32),
            jax.ShapeDtypeStruct((rows, width), BF16),
            jax.ShapeDtypeStruct((size, rows + 16, width), BF16),
            jax.ShapeDtypeStruct((size, rows, wide), BF16),
            jax.ShapeDtypeStruct((size, rows, wide), BF16),
            *([jax.ShapeDtypeStruct((width, 4 * width + 128), BF16)] if extra else []),
        ),
        in_specs=[in_vmem()] * 3 + [in_any()] + [in_vmem()] * len(strips),
        out_specs=(in_vmem(), in_vmem(), in_any(), in_any(), in_any()) + (in_any(),) * extra,
        scratch_shapes=[
            pltpu.VMEM((wide, width), BF16),
            pltpu.SemaphoreType.DMA,
            pltpu.VMEM((size, rows + 16, width), BF16),
            pltpu.VMEM((size, rows, wide), BF16),
            pltpu.VMEM((size, rows, wide), BF16),
            pltpu.VMEM((rows, wide), BF16),
            pltpu.SemaphoreType.DMA((size, 3)),
        ]
        + group.scratch(rows, 0, width)
        + (
            [pltpu.VMEM((width, 4 * width + 128), BF16), pltpu.SemaphoreType.DMA]
            + spread.semaphores()
            if extra
            else []
        ),
        compiler_params=pltpu.CompilerParams(
            collective_id=10 if extra else 1, has_side_effects=True, vmem_limit_bytes=VMEM_LIMIT
        ),
        name="experts_forward",
    )(message, middle, up, down, *strips)


class Shift:
    def __init__(self, source):
        experts, self.dp, quarters, r, self.hid = source.shape
        self.experts = experts
        self.shape = (experts, quarters, r, self.dp * self.hid)
        self.scratch_shapes = [
            pltpu.VMEM(self.shape, BF16),
            pltpu.VMEM((self.dp, experts, quarters, r, self.hid), BF16),
            pltpu.SemaphoreType.DMA((2, self.dp)),
        ]

    def copy(self, src, dst, box, sems, r):
        me = lax.axis_index("dp")
        return remote(src.at[:, me ^ r], box.at[me], sems.at[0, r], sems.at[1, r], {"dp": me ^ r})

    def start(self, *refs):
        for r in range(1, self.dp):
            self.copy(*refs, r).start()

    def arrive(self, src, dst, box, sems):
        me = lax.axis_index("dp")
        box[me] = src[:, me]
        for r in range(1, self.dp):
            self.copy(src, dst, box, sems, r).wait_recv()
        for owner in range(self.dp):
            dst[:, :, :, owner * self.hid : (owner + 1) * self.hid] = box[owner]

    def drain(self, *refs):
        for r in range(1, self.dp):
            self.copy(*refs, r).wait_send()


class LineSums:
    def __init__(self, dp=0, down_chunks=None, kept=(), **arrays):
        self.dp = dp
        self.kept = kept
        self.first = down_chunks[0] if down_chunks else 0
        self.kinds = list(arrays)
        self.args = tuple(array for array in arrays.values() if not isinstance(array, jax.ShapeDtypeStruct))
        self.dense = [kind for kind in self.kinds if kind.startswith("dense")]
        self.chunk, self.count = {}, {}
        self.out_shape, self.scratch_shapes = (), []
        for kind, array in arrays.items():
            shape = array.shape
            special = []
            if kind == "up":
                self.chunk[kind], self.count[kind] = shape[2:], shape[0] * shape[1]
            elif kind == "down":
                self.chunk[kind] = shape[1:]
                self.count[kind] = down_chunks[1] - down_chunks[0] if down_chunks else shape[0]
            else:
                self.chunk[kind], self.count[kind] = (shape[2] // 4, shape[3]), 4
                whole = (dp // 2,) + shape[2:]
                special = [
                    pltpu.VMEM(whole, BF16),
                    pltpu.VMEM(whole, BF16),
                    pltpu.VMEM((4,) + self.chunk[kind], BF16),
                    pltpu.SemaphoreType.DMA((2,)),
                    pltpu.SemaphoreType.DMA((2, dp // 2)),
                ]
            count, chunk = self.count[kind], self.chunk[kind]
            if kind not in kept:
                self.out_shape += (jax.ShapeDtypeStruct((count,) + chunk, BF16),)
            self.scratch_shapes += [
                pltpu.VMEM((count,) + chunk, BF16),
                pltpu.VMEM((count // 2,) + chunk, BF16),
                pltpu.VMEM((count // 2,) + chunk, BF16),
                pltpu.VMEM((count,) + chunk, BF16),
                pltpu.SemaphoreType.DMA((2, count)),
                pltpu.SemaphoreType.DMA((2, count // 2)),
                pltpu.SemaphoreType.DMA((2, count)),
                pltpu.SemaphoreType.DMA((count // 2,)),
                pltpu.SemaphoreType.DMA,
            ] + special
        self.pairs = [(kind, p) for kind in self.kinds for p in range(self.count[kind] // 2)]

    def peers(self):
        if not self.kinds:
            return []
        mine = lax.axis_index("seq")
        middle = (mine == 1) | (mine == 2)
        return [
            ({"seq": jnp.where(middle, 3 - mine, 1 + mine // 2)}, None),
            ({"seq": jnp.where(middle, 3 * (mine - 1), mine)}, middle),
        ]

    def bind(self, refs, outs, scratch):
        self.refs = dict(zip(self.kinds, refs))
        self.outs = dict(zip((kind for kind in self.kinds if kind not in self.kept), outs))
        self.boxes = {}
        for kind in self.kinds:
            held = 14 if kind in self.dense else 9
            self.boxes[kind], scratch = scratch[:held], scratch[held:]
        self.me, self.mine = lax.axis_index("dp"), lax.axis_index("seq")
        self.middle = (self.mine == 1) | (self.mine == 2)
        self.inner = {"seq": jnp.where(self.middle, 3 - self.mine, 1 + self.mine // 2)}
        self.outer = {"seq": jnp.where(self.middle, 3 * (self.mine - 1), self.mine)}
        self.side = jnp.where(self.mine == 2, 1, 0)

    def source(self, kind, c):
        if kind == "up":
            return self.refs[kind].at[c // 4, lax.rem(c, 4)]
        return self.boxes[kind][11].at[c] if kind in self.dense else self.refs[kind].at[self.first + c]

    def inward(self, kind, c):
        box, sem = self.boxes[kind][0], self.boxes[kind][4]
        return remote(self.source(kind, c), box.at[c], sem.at[0, c], sem.at[1, c], self.inner)

    def across(self, kind, p):
        box, sem = self.boxes[kind], self.boxes[kind][5]
        return remote(box[2].at[p], box[1].at[p], sem.at[0, p], sem.at[1, p], self.inner)

    def outward(self, kind, c):
        box, sem = self.boxes[kind][3], self.boxes[kind][6]
        return remote(box.at[c], box.at[c], sem.at[0, c], sem.at[1, c], self.outer)

    def between(self, kind, c, p):
        box = self.boxes[kind]
        return remote(box[3].at[c], box[3].at[c], box[7].at[p], box[6].at[1, c], self.inner)

    def near_copy(self, kind):
        box = self.boxes[kind]
        away = self.refs[kind].at[:, 1 - lax.rem(self.me, 2)]
        return remote(away, box[9], box[12].at[0], box[12].at[1], {"dp": self.me ^ 1})

    def far(self, kind, m):
        box = self.boxes[kind]
        return remote(
            box[9].at[(self.me // 2) ^ m], box[10].at[m], box[13].at[0, m], box[13].at[1, m],
            {"dp": self.me ^ (2 * m)},
        )

    def begin(self, *kinds):
        @pl.when(jnp.logical_not(self.middle))
        def _():
            for kind in kinds:
                for c in range(self.count[kind]):
                    self.inward(kind, c).start()

    def dense_begin(self, kind):
        self.near_copy(kind).start()

    def dense_near(self, kind):
        self.near_copy(kind).wait_recv()
        box = self.boxes[kind]
        for at in range(self.dp // 2):
            box[9][at] = (
                self.refs[kind][at, lax.rem(self.me, 2)].astype(F32) + box[9][at].astype(F32)
            ).astype(BF16)
        for m in range(1, self.dp // 2):
            self.far(kind, m).start()

    def dense_far(self, kind):
        for m in range(1, self.dp // 2):
            self.far(kind, m).wait_recv()
        box = self.boxes[kind]
        rows = self.chunk[kind][0]
        for at in range(4):
            place = slice(at * rows, (at + 1) * rows)
            total = box[9][self.me // 2, place].astype(F32)
            for m in range(1, self.dp // 2):
                total += box[10][m, place].astype(F32)
            box[11][at] = total.astype(BF16)
        self.begin(kind)

    def relay(self, kind, p):
        c = 2 * p + 1 - self.side
        box = self.boxes[kind]
        self.inward(kind, c).wait_recv()
        box[2][p] = (self.source(kind, c)[...].astype(F32) + box[0][c].astype(F32)).astype(BF16)
        self.across(kind, p).start()

    def total(self, kind, p):
        c = 2 * p + self.side
        box = self.boxes[kind]
        self.inward(kind, c).wait_recv()
        self.across(kind, p).wait_recv()
        box[3][c] = (
            self.source(kind, c)[...].astype(F32) + box[0][c].astype(F32) + box[1][p].astype(F32)
        ).astype(BF16)
        self.between(kind, c, p).start()
        self.outward(kind, c).start()

    def forward(self, kind, p):
        c = 2 * p + 1 - self.side
        self.outward(kind, c).wait_recv()
        self.outward(kind, c).start()

    def ticks(self):
        count = len(self.pairs)
        if not count:
            return []

        def tick(at):
            @pl.when(self.middle)
            def _():
                for act, behind in ((self.relay, 0), (self.total, 2), (self.forward, 4)):
                    if 0 <= at - behind < count:
                        act(*self.pairs[at - behind])

        return [lambda at=at: tick(at) for at in range(count + 4)]

    def share_out(self, places):
        ticks, shared = self.ticks(), []
        for counts in places:
            group = []
            for count in counts:
                group.append(ticks[:count])
                ticks = ticks[count:]
            shared.append(group)
        return (*shared, ticks)

    def finish(self):
        if not self.kinds:
            return

        @pl.when(jnp.logical_not(self.middle))
        def _():
            for kind in self.kinds:
                for c in range(self.count[kind]):
                    self.outward(kind, c).wait_recv()
                    self.inward(kind, c).wait_send()

        copies = [
            pltpu.make_async_copy(self.boxes[kind][3], out, self.boxes[kind][8]) for kind, out in self.outs.items()
        ]
        for copy in copies:
            copy.start()

        @pl.when(self.middle)
        def _():
            for kind, p in self.pairs:
                self.across(kind, p).wait_send()
                self.between(kind, 2 * p + self.side, p).wait_send()
                self.outward(kind, 2 * p).wait_send()
                self.outward(kind, 2 * p + 1).wait_send()

        for kind in self.dense:
            self.near_copy(kind).wait_send()
            for m in range(1, self.dp // 2):
                self.far(kind, m).wait_send()
        for copy in copies:
            copy.wait()


def sum_weights_plainly(dp, down, up, dense):
    dense = lax.psum_scatter(dense.reshape(dp, -1, dense.shape[-1]), "dp", scatter_dimension=0, tiled=True)
    up = lax.all_to_all(up, "dp", split_axis=1, concat_axis=1, tiled=True)
    experts, _, quarters, r, hid = up.shape
    up = jnp.transpose(up.reshape(experts, dp, quarters * r, hid), (0, 2, 1, 3))
    return lax.psum(down, "seq"), lax.psum(up.reshape(experts, quarters * r, -1), "seq"), lax.psum(dense, "seq")


def experts_backward(grad, blocks, act, slope, up, down, level, plan, job, leaving=None):
    rows, width = grad.shape
    experts, _, hid = up.shape
    wide = experts * hid
    size = plan.dp
    group = Group(size)
    swap = Swap(plan)
    extra = [] if leaving is None else [leaving]

    def kernel(*refs):
        (grad_ref, blocks_ref, act_ref, slope_ref, up_ref, down_all), refs = refs[:6], refs[6:]
        if extra:
            leaving_ref, refs = refs[0], refs[1:]
        job_refs, refs = refs[: len(job.args)], refs[len(job.args) :]
        (out_ref, tail_ref, up_out, down_out), refs = refs[:4], refs[4:]
        if extra:
            left_ref, refs = refs[0], refs[1:]
        job_outs, refs = refs[: len(job.args)], refs[len(job.args) :]
        slots, blocks, facts, act, slope, weighed, scaled, pre, flat, load_sem, down_ref, down_sem = refs[:12]
        refs = refs[12:]
        bring = pltpu.make_async_copy(down_all.at[level], down_ref, down_sem)
        bring.start()
        scratch, refs = refs[:13], refs[13:]
        if extra:
            (left, left_sem), refs = refs[:2], refs[2:]
        job.bind(job_refs, job_outs, refs)
        in_steps, in_sums, before, between, rest = job.share_out(EXPERT_TICKS)

        def loads(at):
            two = lax.rem(at, 2)
            slot = 2 * group.pair_at(at // 2) + 1 - two
            place = pl.ds(pl.multiple_of(slot * rows, 16), rows)
            return (
                pltpu.make_async_copy(blocks_ref.at[slot, pl.ds(0, rows)], blocks.at[place], load_sem.at[two, 0]),
                pltpu.make_async_copy(act_ref.at[slot], act.at[two], load_sem.at[two, 1]),
                pltpu.make_async_copy(slope_ref.at[slot], slope.at[two], load_sem.at[two, 2]),
                pltpu.make_async_copy(blocks_ref.at[slot, pl.ds(rows, 16)], facts.at[two], load_sem.at[two, 3]),
            )

        for load in loads(0):
            load.start()
        greet(*group.peers(), *job.peers(), *(swap.peers() if extra else []))
        slots[0] = grad_ref[...]
        if extra:
            swap.start(leaving_ref, left, left_sem)
        for expert in range(experts):
            flat[:, expert * hid : (expert + 1) * hid] = up_ref[expert]
        bring.wait()
        lane = lax.broadcasted_iota(jnp.int32, (16, wide), 1) // hid
        pick = (lane == lax.broadcasted_iota(jnp.int32, (16, wide), 0)).astype(F32).astype(BF16)

        def compute(slot, at):
            two = lax.rem(at, 2)

            @pl.when(at + 1 < size)
            def _():
                for load in loads(at + 1):
                    load.start()

            for load in loads(at):
                load.wait()
            gates = jnp.transpose(join_rows(facts[two]))[:rows]
            place = pl.ds(pl.multiple_of(slot * rows, 16), rows)
            for expert in range(experts):
                cols = slice(expert * hid, (expert + 1) * hid)
                gate = gates[:, expert : expert + 1]
                pull = dot(slots[slot], down_ref[cols, :], NT)
                value = act[two, :, cols].astype(F32)
                weighed[:, cols] = (pull * value).astype(BF16)
                scaled[place, cols] = (value * gate).astype(BF16)
                pre[place, cols] = (pull * gate * slope[two, :, cols].astype(F32)).astype(BF16)
            if job.kinds:
                pl.when(at == 0)(lambda: job.begin(*job.kinds))
                for step, ticks in enumerate(in_steps):
                    for tick in ticks:
                        pl.when(at == step)(tick)
            by_expert = pad_lanes(dot(pick, weighed[...], NT)[:8], width)
            return dot(pre[place, :], flat[...], NT), by_expert

        group.run(slots, scratch, rows, 16, compute)

        def weight_sums(expert, carry):
            cols = pl.ds(pl.multiple_of(expert * hid, 128), hid)
            down_out[cols, :] = dot(scaled[:, cols], slots[...].reshape(size * rows, width), TN).astype(BF16)
            up_out[expert] = dot(blocks[...], pre[:, cols], TN).astype(BF16)
            for step, ticks in enumerate(in_sums):
                for tick in ticks:
                    pl.when(expert == step)(tick)
            return carry

        lax.fori_loop(0, experts, weight_sums, 0)
        for tick in before[0]:
            tick()
        group.collect(between)
        out_ref[...] = group.own[0]
        tail_ref[...] = group.own_tail[0]
        for tick in rest:
            tick()
        job.finish()
        if extra:
            swap.wait(leaving_ref, left, left_sem)
            left_ref[...] = left[...]

    left_shape = [] if leaving is None else [jax.ShapeDtypeStruct(leaving.shape, BF16)]
    left_scratch = [
        pltpu.VMEM((plan.images, plan.piece, width), BF16),
        pltpu.SemaphoreType.DMA((2, plan.images)),
    ]
    return pl.pallas_call(
        kernel,
        out_shape=(
            jax.ShapeDtypeStruct((rows, width), F32),
            jax.ShapeDtypeStruct((8, width), F32),
            jax.ShapeDtypeStruct((experts, width, hid), BF16),
            jax.ShapeDtypeStruct((wide, width), BF16),
            *left_shape,
            *job.out_shape,
        ),
        in_specs=[in_vmem(), in_any(), in_any(), in_any(), in_vmem(), in_any()]
        + [in_vmem()] * (len(extra) + len(job.args)),
        out_specs=(in_vmem(),) * (4 + len(extra)) + (in_any(),) * len(job.args),
        scratch_shapes=[
            pltpu.VMEM((size, rows, width), BF16),
            pltpu.VMEM((size * rows, width), BF16),
            pltpu.VMEM((2, 16, width), BF16),
            pltpu.VMEM((2, rows, wide), BF16),
            pltpu.VMEM((2, rows, wide), BF16),
            pltpu.VMEM((rows, wide), BF16),
            pltpu.VMEM((size * rows, wide), BF16),
            pltpu.VMEM((size * rows, wide), BF16),
            pltpu.VMEM((width, wide), BF16),
            pltpu.SemaphoreType.DMA((2, 4)),
            pltpu.VMEM((wide, width), BF16),
            pltpu.SemaphoreType.DMA,
        ]
        + group.scratch(rows, 16, width)
        + (left_scratch if extra else [])
        + job.scratch_shapes,
        compiler_params=pltpu.CompilerParams(
            collective_id=3 if job.kinds else 2, has_side_effects=True, vmem_limit_bytes=VMEM_LIMIT
        ),
        name="experts_backward_and_sums" if job.kinds else "experts_backward",
    )(grad, blocks, act, slope, up, down, *extra, *job.args)


def attention_forward(plan, level, expert_in, later=None, entry=None):
    first = entry is not None
    share, size, rows = plan.share, plan.dp, plan.rows
    swap = Swap(plan)
    levels, experts, strip, hidden = expert_in.shape
    spread = Spread(size)
    width = strip * size
    columns = 4 * width + 128
    keys_len = rows * share
    heads = width // HEAD
    hid = hidden // size

    given = entry or later

    def kernel(in_ref, *refs):
        taken, refs = refs[: len(given)], refs[len(given) :]
        (message, middle, queries, kv, log_total, mixed, gates_ref, up_ref), refs = refs[:8], refs[8:]
        if first:
            (grad, grad_low, state_ref, chosen_all, length_ref, dense_out), refs = refs[:6], refs[6:]
        (all_kv, values_t, up_all, whole, parts, send, recv, save, up_send, up_recv), refs = refs[:10], refs[10:]
        bring = pltpu.make_async_copy(in_ref.at[level], whole, save)
        bring.start()
        me = lax.axis_index("dp")
        part = lax.rem(me, share)
        greet(*[({"dp": me ^ r}, None) for r in range(1, size)], *(swap.peers() if first else []))

        def shift(r):
            return remote(
                parts.at[me ^ r], up_all.at[:, pl.ds(pl.multiple_of(me * strip, 16), strip)],
                up_send.at[r], up_recv.at[r], {"dp": me ^ r},
            )

        if first:
            tokens_ref, facts_ref, cot_ref, *strips = taken
            tok, fact, cot, dense_all, tok_sem, fact_sem, cot_sem, keep_sem, *sems = refs
            lay_strip(strips, level, dense_all, pl.ds(pl.multiple_of(me * strip, 16), strip))
            spread.bind(Strips(dense_all, strip), sems)
            spread.start()
            swap.start(facts_ref, fact, fact_sem)
            swap.start(tokens_ref, tok, tok_sem)
        bring.wait()
        for owner in range(size):
            parts[owner] = whole[:, :, owner * hid : (owner + 1) * hid]
        up_all[:, pl.ds(pl.multiple_of(me * strip, 16), strip)] = parts[me]
        if first:
            for pair in spread.order[1:]:
                spread.arrive(pair)
            for r in range(1, size):
                shift(r).start()
            swap.start(cot_ref, cot, cot_sem)
            swap.wait(facts_ref, fact, fact_sem)
            total = fact[0].astype(F32)
            for k in range(1, plan.images):
                total += fact[k].astype(F32)
            for at in range(levels):
                chosen_all[at] = total[8 * at : 8 * at + 8]
            length = total[8 * levels : 8 * levels + 1, :1] * 4.0 + total[8 * levels + 1 : 8 * levels + 2, :1]
            length_ref[...] = jnp.broadcast_to(length, length_ref.shape)
            swap.wait(tokens_ref, tok, tok_sem)
            for k in range(plan.images):
                state_ref[k * plan.piece : (k + 1) * plan.piece] = tok[k].astype(F32)
            for pair in spread.order:
                spread.handed(pair).wait_recv()
            keep_dense = pltpu.make_async_copy(dense_all, dense_out, keep_sem)
            keep_dense.start()
            dense_ref, chosen_ref = dense_all, chosen_all.at[level]
        else:
            state_ref, dense_ref, chosen_all, length_ref = taken
            chosen_ref = chosen_all.at[level]
            for r in range(1, size):
                shift(r).start()
        rows_of = weight_rows(dense_ref)
        unit, _ = normalize(state_ref[...])
        normed = (unit * rows_of[0:1] + rows_of[1:2]).astype(BF16)
        all_kv[part] = dot(normed, dense_ref[:, width : 3 * width]).astype(BF16)
        copies = [
            remote(all_kv.at[part], all_kv.at[part], send.at[k], recv.at[k], {"dp": me ^ k})
            for k in range(1, share)
        ]
        for copy in copies:
            copy.start()
        queries[...] = (dot(normed, dense_ref[:, :width]) * HEAD ** (-0.5)).astype(BF16)
        for copy in copies:
            copy.wait()
        saving = pltpu.make_async_copy(all_kv, kv, save)
        saving.start()
        for at in range(share):
            values_t[:, at * rows : (at + 1) * rows] = jnp.transpose(
                all_kv[at, :, width:].astype(F32)
            ).astype(BF16)
        key = lax.broadcasted_iota(jnp.int32, (keys_len, rows), 0)
        valid = key.astype(F32) < length_ref[0:1, 0:1]

        def pair_of_heads(pair, carry):
            lanes = pl.ds(pl.multiple_of(pair * 128, 128), 128)
            keys_pair = all_kv[:, :, lanes].reshape(keys_len, 128)
            queries_pair = queries[:, lanes]
            for parity in range(2):
                head = 2 * pair + parity
                scores = dot(keys_pair, one_head(queries_pair, parity), NT)
                scores = jnp.where(valid, scores, NEG)
                highest = jnp.max(scores, 0, keepdims=True)
                expo = jnp.exp(scores - highest)
                totals = row_sums(expo)
                log_total[head] = highest + jnp.log(totals)
                place = pl.ds(pl.multiple_of(head * HEAD, HEAD), HEAD)
                mixed[place, :] = (dot(values_t[place, :], expo.astype(BF16)) / totals).astype(BF16)
            return carry

        lax.fori_loop(0, heads // 2, pair_of_heads, 0)
        middle[...] = state_ref[...] + dot(mixed[...], dense_ref[:, 3 * width : 4 * width], TN)
        unit, _ = normalize(middle[...])
        normed = (unit * rows_of[2:3] + rows_of[3:4]).astype(BF16)
        message[:rows] = normed
        router = jnp.concatenate([rows_of[4:8], jnp.zeros((12, width), F32)], 0).astype(BF16)
        logits = dot(router, normed, NT)[:8]
        row = lax.broadcasted_iota(jnp.int32, logits.shape, 0)
        logits = jnp.where(row < experts, logits, NEG)
        expo = jnp.exp(logits - jnp.max(logits, 0, keepdims=True))
        gates = expo / row_sums(expo)
        gates_ref[...] = gates
        message[rows:] = split_rows(pad_lanes(gates * chosen_ref[:, :rows], width))
        saving.wait()
        for r in range(1, size):
            shift(r).wait_recv()
        keep = pltpu.make_async_copy(up_all, up_ref, save)
        keep.start()
        if first:
            swap.wait(cot_ref, cot, cot_sem)
            for k in range(plan.images):
                place = slice(k * plan.piece, (k + 1) * plan.piece)
                row = lax.broadcasted_iota(jnp.int32, (plan.piece, width), 0) + part * rows + k * plan.piece
                masked = jnp.where(row.astype(F32) < length_ref[0:1, 0:1], cot[k].astype(F32), 0.0)
                grad[place] = masked
                grad_low[place] = masked.astype(BF16)
            spread.drain()
            keep_dense.wait()
        for r in range(1, size):
            shift(r).wait_send()
        keep.wait()

    pieces = pltpu.VMEM((plan.images, plan.piece, width), BF16)
    swap_sem = pltpu.SemaphoreType.DMA((2, plan.images))
    entry_out, entry_specs, entry_scratch = (), (), []
    if first:
        entry_out = (
            jax.ShapeDtypeStruct((rows, width), F32),
            jax.ShapeDtypeStruct((rows, width), BF16),
            jax.ShapeDtypeStruct((rows, width), F32),
            jax.ShapeDtypeStruct((levels, 8, width), F32),
            jax.ShapeDtypeStruct((8, 128), F32),
            jax.ShapeDtypeStruct((width, columns), BF16),
        )
        entry_specs = (in_vmem(),) * 5 + (in_any(),)
        entry_scratch = [
            pieces,
            pltpu.VMEM(entry[1].shape, BF16),
            pieces,
            pltpu.VMEM((width, columns), BF16),
            swap_sem,
            swap_sem,
            swap_sem,
            pltpu.SemaphoreType.DMA,
        ] + spread.semaphores()
    return pl.pallas_call(
        kernel,
        out_shape=(
            jax.ShapeDtypeStruct((rows + 16, width), BF16),
            jax.ShapeDtypeStruct((rows, width), F32),
            jax.ShapeDtypeStruct((rows, width), BF16),
            jax.ShapeDtypeStruct((share, rows, 2 * width), BF16),
            jax.ShapeDtypeStruct((heads, 1, rows), F32),
            jax.ShapeDtypeStruct((width, rows), BF16),
            jax.ShapeDtypeStruct((8, rows), F32),
            jax.ShapeDtypeStruct((experts, width, hid), BF16),
            *entry_out,
        ),
        in_specs=[in_any()] + [in_vmem()] * len(given),
        out_specs=(in_vmem(),) * 3 + (in_any(),) + (in_vmem(),) * 3 + (in_any(),) + entry_specs,
        scratch_shapes=[
            pltpu.VMEM((share, rows, 2 * width), BF16),
            pltpu.VMEM((width, keys_len), BF16),
            pltpu.VMEM((experts, width, hid), BF16),
            pltpu.VMEM((experts, strip, hidden), BF16),
            pltpu.VMEM((size, experts, strip, hid), BF16),
            pltpu.SemaphoreType.DMA((share,)),
            pltpu.SemaphoreType.DMA((share,)),
            pltpu.SemaphoreType.DMA,
            pltpu.SemaphoreType.DMA((size,)),
            pltpu.SemaphoreType.DMA((size,)),
        ]
        + entry_scratch,
        compiler_params=pltpu.CompilerParams(
            collective_id=5 + first, has_side_effects=True, vmem_limit_bytes=VMEM_LIMIT
        ),
        name="attention_forward_first" if first else "attention_forward",
    )(expert_in, *given)


def attention_backward(
    grad, back, back_tail, state, middle, message, gates, chosen, queries, kv, log_total, mixed,
    dense, length, up_grad, level, plan, job,
):
    rows, width = state.shape
    last = level == 0
    share = plan.share
    keys_len = rows * share
    heads = width // HEAD
    columns = dense.shape[1]
    swap = Swap(plan)
    strip = width // plan.dp
    dense_shape = (plan.dp // 2, 2, strip, columns)
    moves = up_grad is not None
    shift = Shift(up_grad) if moves else None
    moved_out = moves and not last
    totals_shape = [
        jax.ShapeDtypeStruct((len(job.kept), strip, wide), F32)
        for wide in ((3 * width, width, columns - 4 * width) if job.kept else ())
    ]

    def kernel(*refs):
        (
            grad_ref, back_ref, tail_ref, state_ref, mid_ref, msg_ref, gates_ref, chosen_ref, queries, kv,
            log_total, mixed, weights, length_ref,
        ), refs = refs[:14], refs[14:]
        if moves:
            up_ref, refs = refs[0], refs[1:]
        taken = len(job.args)
        job_refs, refs = refs[:taken], refs[taken:]
        (new_ref, new_low_ref), refs = refs[:2], refs[2:]
        if not totals_shape:
            dense_ref, refs = refs[0], refs[1:]
        if moved_out:
            moved_ref, refs = refs[0], refs[1:]
        if totals_shape:
            totals, refs = refs[:3], refs[3:]
        job_outs, refs = refs[: len(job.out_shape)], refs[len(job.out_shape) :]
        (
            keys_t, normed_ref, grad_mid, grad_heads, grad_q, kv_grads, kv_got, grad_packed, send, recv,
        ), refs = refs[:10], refs[10:]
        if moves:
            moving = (up_ref, *refs[:3])
            refs = refs[3:]
        if last:
            (pieces, piece_sem), refs = refs[:2], refs[2:]
            if totals_shape:
                dense_ref, refs = refs[0], refs[1:]
                job_refs = (job_refs[0], moving[1], *job_refs[1:], dense_ref)
        summing = last and job.kinds
        job.bind(job_refs, job_outs, refs)
        in_heads, after_heads, after_sums, rest = job.share_out(HEAD_TICKS)
        me = lax.axis_index("dp")
        part = lax.rem(me, share)
        greet(
            *[({"dp": me ^ k}, None) for k in range(1, plan.dp if moves else share)],
            *job.peers(),
            *(swap.peers() if last else []),
        )
        if moves:
            shift.start(*moving)
        if job.kinds:
            job.begin("down")
        if summing:
            job.dense_begin(job.dense[0])
        rows_of = weight_rows(weights)
        gates = gates_ref[...]
        grad_gates = tail_ref[:, :rows] * chosen_ref[level, :, :rows]
        grad_logits = split_rows(gates * (grad_gates - row_sums(gates * grad_gates)))
        router = jnp.concatenate([rows_of[4:8], jnp.zeros((4, width), F32)], 0)
        twice = jnp.concatenate([router, router], 0).astype(BF16)
        grad_normed = back_ref[...] + dot(grad_logits, twice, TN)
        router_grad = dot(grad_logits, msg_ref[:rows])
        router_grad = router_grad[:8] + router_grad[8:]
        unit, inverse = normalize(mid_ref[...])
        gain_two = row_sums(grad_normed * unit)
        bias_two = row_sums(grad_normed)
        grad_mid[...] = grad_ref[...] + norm_back(grad_normed * rows_of[2:3], unit, inverse)
        low = grad_mid[...].astype(BF16)

        def put(columns_of, values):
            for at in range(plan.dp):
                dense_ref[at // 2, at % 2, :, columns_of] = values[at * strip : (at + 1) * strip].astype(BF16)

        put(slice(3 * width, 4 * width), dot(mixed[...], low))
        grad_heads[...] = dot(low, weights[:, 3 * width : 4 * width], NT).astype(BF16)
        for at in range(share):
            keys_t[:, at * rows : (at + 1) * rows] = jnp.transpose(kv[at, :, :width].astype(F32)).astype(BF16)
        key = lax.broadcasted_iota(jnp.int32, (keys_len, rows), 0)
        valid = key.astype(F32) < length_ref[0:1, 0:1]

        def pair_of_heads(pair, carry):
            lanes = pl.ds(pl.multiple_of(pair * 128, 128), 128)
            value_lanes = pl.ds(pl.multiple_of(width + pair * 128, 128), 128)
            keys_pair = kv[:, :, lanes].reshape(keys_len, 128)
            values_pair = kv[:, :, value_lanes].reshape(keys_len, 128)
            grad_k = jnp.zeros((keys_len, 128), F32)
            grad_v = jnp.zeros((keys_len, 128), F32)
            for parity in range(2):
                head = 2 * pair + parity
                query = one_head(queries[:, lanes], parity)
                pull = one_head(grad_heads[:, lanes], parity)
                scores = dot(keys_pair, query, NT)
                probs = jnp.where(valid, jnp.exp(scores - log_total[head]), 0.0)
                grad_probs = dot(values_pair, pull, NT)
                grad_scores = probs * (grad_probs - row_sums(probs * grad_probs))
                grad_scores = grad_scores.astype(BF16)
                grad_v += dot(probs.astype(BF16), pull)
                grad_k += dot(grad_scores, query)
                place = pl.ds(pl.multiple_of(head * HEAD, HEAD), HEAD)
                grad_q[place, :] = dot(keys_t[place, :], grad_scores) * HEAD ** (-0.5)
            kv_grads[:, :, lanes] = grad_k.astype(BF16).reshape(share, rows, 128)
            kv_grads[:, :, value_lanes] = grad_v.astype(BF16).reshape(share, rows, 128)
            for at, ticks in enumerate(in_heads):
                for tick in ticks:
                    pl.when(pair == at)(tick)
            if summing:
                pl.when(pair == heads // 2 - 2)(lambda: job.dense_near(job.dense[0]))
            return carry

        lax.fori_loop(0, heads // 2, pair_of_heads, 0)
        for tick in after_heads[0]:
            tick()
        copies = [
            remote(kv_grads.at[part ^ k], kv_got.at[k], send.at[k], recv.at[k], {"dp": me ^ k})
            for k in range(1, share)
        ]
        for copy in copies:
            copy.start()
        unit, inverse = normalize(state_ref[...])
        normed_ref[...] = (unit * rows_of[0:1] + rows_of[1:2]).astype(BF16)
        grad_packed[:, :width] = jnp.transpose(grad_q[...]).astype(BF16)
        for copy in copies:
            copy.wait()
        total = kv_grads[part].astype(F32)
        for k in range(1, share):
            total += kv_got[k].astype(F32)
        grad_packed[:, width:] = total.astype(BF16)
        grad_normed = dot(grad_packed[...], weights[:, : 3 * width], NT)
        for block in range(3):
            cols = slice(block * width, (block + 1) * width)
            put(cols, dot(normed_ref[...], grad_packed[:, cols], TN))
        gain_one = row_sums(grad_normed * unit)
        bias_one = row_sums(grad_normed)
        tail = jnp.concatenate([gain_one, bias_one, gain_two, bias_two, router_grad[:4]], 0)
        put(slice(4 * width, columns), pad_lanes(jnp.transpose(tail), columns - 4 * width))
        for tick in after_sums[0]:
            tick()
        if summing:
            job.dense_begin(job.dense[1])
            shift.arrive(*moving)
            job.begin("up")
        new = grad_mid[...] + norm_back(grad_normed * rows_of[0:1], unit, inverse)
        if last:
            for k in range(plan.images):
                new_low_ref[k] = new[k * plan.piece : (k + 1) * plan.piece].astype(BF16)
            if not summing:
                swap.start(new_low_ref, pieces, piece_sem)
        else:
            new_low_ref[...] = new.astype(BF16)
            new_ref[...] = new
        if moved_out:
            shift.arrive(*moving)
            moved_ref[...] = moving[1][...]
        for at, tick in enumerate(rest, sum(map(sum, HEAD_TICKS))):
            if summing and at == DENSE_TICKS[0]:
                job.dense_near(job.dense[1])
            if summing and at == DENSE_TICKS[1]:
                job.dense_far(job.dense[0])
            if summing and at == DENSE_TICKS[2]:
                job.dense_far(job.dense[1])
                swap.start(new_low_ref, pieces, piece_sem)
            tick()
        job.finish()
        for at, kind in enumerate(job.kept):
            start = 0
            for total in totals:
                wide = total.shape[2]
                for chunk in range(4):
                    place = slice(chunk * strip // 4, (chunk + 1) * strip // 4)
                    total[at, place] = job.boxes[kind][3][chunk, :, start : start + wide].astype(F32)
                start += wide
        if moves:
            shift.drain(*moving)
        if last:
            swap.wait(new_low_ref, pieces, piece_sem)
            for k in range(plan.images):
                new_ref[k] = pieces[k].astype(F32)

    image_shape = (plan.images, plan.piece, width) if last else (rows, width)
    last_scratch = [
        pltpu.VMEM((plan.images, plan.piece, width), BF16),
        pltpu.SemaphoreType.DMA((2, plan.images)),
    ]
    return pl.pallas_call(
        kernel,
        out_shape=(
            jax.ShapeDtypeStruct(image_shape, F32),
            jax.ShapeDtypeStruct(image_shape, BF16),
            *([] if totals_shape else [jax.ShapeDtypeStruct(dense_shape, BF16)]),
            *([jax.ShapeDtypeStruct(shift.shape, BF16)] if moved_out else []),
            *totals_shape,
            *job.out_shape,
        ),
        in_specs=[in_vmem()] * (14 + moves + len(job.args)),
        out_specs=(in_vmem(),) * (2 + (len(totals_shape) or 1) + moved_out) + (in_any(),) * len(job.out_shape),
        scratch_shapes=[
            pltpu.VMEM((width, keys_len), BF16),
            pltpu.VMEM((rows, width), BF16),
            pltpu.VMEM((rows, width), F32),
            pltpu.VMEM((rows, width), BF16),
            pltpu.VMEM((width, rows), F32),
            pltpu.VMEM((share, rows, 2 * width), BF16),
            pltpu.VMEM((share, rows, 2 * width), BF16),
            pltpu.VMEM((rows, 3 * width), BF16),
            pltpu.SemaphoreType.DMA((share,)),
            pltpu.SemaphoreType.DMA((share,)),
        ]
        + (shift.scratch_shapes if moves else [])
        + (last_scratch if last else [])
        + ([pltpu.VMEM(dense_shape, BF16)] if totals_shape else [])
        + job.scratch_shapes,
        compiler_params=pltpu.CompilerParams(
            collective_id=9 if last else 8, has_side_effects=True, vmem_limit_bytes=VMEM_LIMIT
        ),
        name="attention_backward_last" if last else "attention_backward",
    )(
        grad, back, back_tail, state, middle, message, gates, chosen, queries, kv, log_total, mixed,
        dense, length, *([up_grad] if moves else []), *job.args,
    )


def build(mesh):
    def shards(
        tokens,
        cotangent,
        routes,
        token_mask,
        ln1_gain,
        ln1_bias,
        qkv_weight,
        out_weight,
        ln2_gain,
        ln2_bias,
        router_weight,
        expert_in,
        expert_out,
    ):
        images, piece, width = tokens.shape
        levels, experts = expert_in.shape[:2]
        plan = Plan(mesh, images, token_mask.shape[1])
        rows = plan.rows
        wide = experts * expert_out.shape[2]
        lined = plan.seq == 4

        mine = lax.rem(lax.axis_index("seq"), images)
        chosen = jnp.sum((routes[..., None] == jnp.arange(experts, dtype=jnp.int32)).astype(F32), -2)
        chosen = jnp.transpose(chosen, (1, 0, 3, 2))
        at_slot = (jnp.arange(images) == mine).astype(F32)[:, None]
        chosen = (chosen[..., None, :] * at_slot).reshape(images, levels, experts, rows)
        chosen = jnp.pad(chosen, ((0, 0), (0, 0), (0, 8 - experts), (0, width - rows)))
        lengths = jnp.where(mine == 0, jnp.sum(token_mask, -1), 0)
        lengths = jnp.stack([lengths // 4, lengths % 4], -1).astype(F32)
        lengths = jnp.pad(lengths, ((0, 0), (0, 14)))[:, :, None]
        facts = jnp.concatenate(
            [chosen.reshape(images, 8 * levels, width), jnp.broadcast_to(lengths, (images, 16, width))], 1
        ).astype(BF16)

        strips = (qkv_weight, out_weight, router_weight, ln1_gain, ln1_bias, ln2_gain, ln2_bias)
        down_all = expert_out.reshape(levels, wide, width)

        saved = []
        for level in range(levels):
            if level:
                made = attention_forward(
                    plan, level, expert_in, later=(state, dense, chosen, length)
                )
            else:
                *made, grad, grad_low, state, chosen, length, dense = attention_forward(
                    plan, level, expert_in, entry=(tokens, facts, cotangent, *strips)
                )
            message, middle, queries, kv, log_total, mixed, gates, up = made
            new_state, new_low, blocks, act, slope, *next_dense = experts_forward(
                message, middle, up, down_all, level, plan.dp, strips if level + 1 < levels else ()
            )
            attended = (
                state, middle, message, gates, chosen, queries, kv, log_total, mixed,
                dense, length,
            )
            dense = next_dense[0] if next_dense else None
            saved.append((attended, (blocks, act, slope, up, down_all)))
            state = new_state
        leaving = new_low.reshape(images, piece, width)

        sums = [None] * levels
        job = LineSums()
        for level in reversed(range(levels)):
            attended, routed = saved[level]
            last = level == 0
            back, back_tail, up_grad, down_grad, *others = experts_backward(
                grad_low, *routed, level, plan, job, leaving
            )
            if leaving is not None:
                output, *others = others
                leaving = None
            if job.kinds:
                downs, ups = jnp.concatenate([first_downs, others[0]]), others[1]
            up_grad = up_grad.reshape(experts, plan.dp, 4, width // plan.dp // 4, -1)
            down_grad = down_grad.reshape(16, wide // 16, width)
            job = LineSums(plan.dp, (0, EARLY_CHUNKS), down=down_grad) if lined else LineSums()
            if lined and last:
                job = LineSums(
                    plan.dp,
                    None,
                    ("dense", "dense_more"),
                    down=down_grad,
                    up=jax.ShapeDtypeStruct(Shift(up_grad).shape, BF16),
                    dense_more=dense_grad,
                    dense=jax.ShapeDtypeStruct(dense_grad.shape, BF16),
                )
            grad, grad_low, *others = attention_backward(
                grad, back, back_tail, *attended, up_grad if lined else None, level, plan, job
            )
            if not (lined and last):
                dense_grad, *others = others
            if not lined:
                sums[level] = sum_weights_plainly(plan.dp, down_grad, up_grad, dense_grad)
            elif last:
                packed_grad, out_grad, tail_grad = others[:3]
                sums[level] = others[3:]
                sums[level + 1] = (downs, ups)
            else:
                first_downs = others[1]
                job = LineSums(plan.dp, (EARLY_CHUNKS, 16), down=down_grad, up=others[0])
        down_grad, up_grad = (
            jnp.stack([item.reshape(like.shape[1:]) for item in items]).astype(F32)
            for items, like in zip(zip(*(item[:2] for item in sums)), (expert_out, expert_in))
        )
        if not lined:
            dense_grad = jnp.stack([item[2].reshape(width // plan.dp, -1) for item in sums]).astype(F32)
            packed_grad, out_grad = dense_grad[..., : 3 * width], dense_grad[..., 3 * width : 4 * width]
            tail_grad = dense_grad[..., 4 * width :]
        return (
            output,
            grad,
            tail_grad[..., 0],
            tail_grad[..., 1],
            packed_grad,
            out_grad,
            tail_grad[..., 2],
            tail_grad[..., 3],
            tail_grad[..., 4 : 4 + experts],
            up_grad,
            down_grad,
        )

    return shards


def solution(mesh):
    return jax.shard_map(
        build(mesh),
        mesh=mesh,
        in_specs=(
            P("dp", "seq", None),
            P("dp", "seq", None),
            P(None, "dp", "seq", None),
            P("dp", None),
            P(None, "dp"),
            P(None, "dp"),
            P(None, "dp", None),
            P(None, "dp", None),
            P(None, "dp"),
            P(None, "dp"),
            P(None, "dp", None),
            P(None, None, "dp", None),
            P(None, None, "dp", None),
        ),
        out_specs=(
            P("dp", "seq", None),
            P("dp", "seq", None),
            P(None, "dp"),
            P(None, "dp"),
            P(None, "dp", None),
            P(None, "dp", None),
            P(None, "dp"),
            P(None, "dp"),
            P(None, "dp", None),
            P(None, None, "dp", None),
            P(None, None, "dp", None),
        ),
        check_vma=False,
    )
```
